32 devices in a mesh: row: 4 (over x, core), col: 2 (over y), seq: 4 (over z).
Axes of the slice: x: 2, y: 2, z: 4, core: 2. Of those that a mesh axis runs over, the one named last changes fastest.
Arguments:
- left_piece: bfloat16 [512, 32, 256], P('seq', None, 'row'), may hold values from -6 to 6
- right_piece: bfloat16 [512, 32, 256], P('seq', 'row', 'col'), may hold values from -6 to 6
- proj_weight: bfloat16 [1024, 128], replicated, may hold values from -4 to 4
- proj_bias: float32 [128], replicated, may hold values from -3 to 3
- pair_rep: bfloat16 [256, 256, 128], P(('row', 'seq'), 'col'), may hold values from -6 to 6
- norm_gain: float32 [128], replicated, may hold values from 0.5 to 1.5
- up_weight: bfloat16 [128, 512], replicated, may hold values from -0.5 to 0.5
- up_bias: float32 [512], replicated, may hold values from -3 to 3
- down_weight: bfloat16 [512, 128], replicated, may hold values from -0.25 to 0.25
- down_bias: float32 [128], replicated, may hold values from -3 to 3
Outputs:
- refined: bfloat16 [256, 256, 128], P(('row', 'seq'), 'col')
The draws below stay inside these ranges and needn't reach their ends.
All inputs are finite; a program needn't handle non-finite values.
Results may differ from the reference program's by a relative error of at most 0.0085.
Values may be sent and summed in bfloat16 or wider, within the bound.
No kernel may reach another device: no remote copies, remote signals or barrier semaphores. Data moves between devices by JAX's collectives and lax.ppermute only.
A program may use at most 64 MiB of HBM per device.

```python
import jax
import jax.numpy as jnp
from jax import lax

C = 32
H = 128
F = 512
GROUPS = 4
S = 512
N = 256


def shard_levels(own_key, shape, pieces, least, largest):
    factor_of, own = 1.0, jax.random.fold_in(own_key, 6)
    for position, blocks in pieces:
        heights = jnp.exp(jax.random.uniform(jax.random.fold_in(own, position), (blocks,), jnp.float32, least / len(pieces), largest / len(pieces)))
        factor_of = factor_of * jnp.repeat(heights, shape[position] // blocks).reshape([-1 if axis == position else 1 for axis in range(len(shape))])
    return factor_of


def centred(stream_key, extent, width, limit, cuts=(), held_as=jnp.bfloat16):
    entries = jax.random.normal(stream_key, extent, jnp.float32) * width
    if len(cuts) > 0:
        entries = shard_levels(stream_key, extent, cuts, -0.22, 0.18) * entries
    return jnp.clip(entries, min=-limit, max=limit).astype(held_as)


def setup_inputs(seed: int = 0) -> dict:
    key_of = jax.random.split(jax.random.key(seed), 11)
    return {
        "left_piece": centred(key_of[0], (S, C, N), 1.0, 6.0, ((0, 4), (2, 4))),
        "right_piece": centred(key_of[1], (S, C, N), 1.0, 6.0, ((0, 4), (1, 4), (2, 2))),
        "proj_weight": centred(key_of[2], (C * C, H), (C * C / S) ** -0.5, 4.0),
        "proj_bias": centred(key_of[3], (H,), 0.5, 3.0, (), jnp.float32),
        "pair_rep": centred(key_of[4], (N, N, H), 1.0, 6.0, ((0, 16), (1, 2))),
        "norm_gain": jnp.clip(jax.random.uniform(key_of[5], (H,), jnp.float32, 0.5, 1.5), 0.5, 1.5),
        "up_weight": centred(key_of[6], (H, F), H ** -0.5, 0.5),
        "up_bias": centred(key_of[7], (F,), 0.5, 3.0, (), jnp.float32),
        "down_weight": centred(key_of[8], (F, H), F ** -0.5, 0.25),
        "down_bias": centred(key_of[9], (H,), 0.5, 3.0, (), jnp.float32),
    }


epsilon = 1e-05

def project_block(row_slab, right_all, proj_weight):
    seq_count, channels, row_count = row_slab.shape
    columns = right_all.shape[2]
    left_mat = row_slab.reshape(seq_count, channels * row_count)
    right_mat = right_all.reshape(seq_count, channels * columns)
    outer_prod = lax.dot_general(left_mat, right_mat, (((0,), (0,)), ((), ())), preferred_element_type=jnp.float32).astype(jnp.bfloat16)
    outer_prod = outer_prod.reshape(channels, row_count, channels, columns).transpose(1, 3, 0, 2)
    outer_prod = outer_prod.reshape(row_count * columns, channels * channels)
    result = jnp.dot(outer_prod, proj_weight, preferred_element_type=jnp.float32)
    return result.reshape(row_count, columns, proj_weight.shape[1])

def transition(middle, norm_gain, up_weight, up_bias, down_weight, down_bias):
    row_count, columns, channels = middle.shape
    values = middle.astype(jnp.float32).reshape(row_count * columns, channels)
    center = lax.optimization_barrier(jnp.mean(values, axis=1, keepdims=True))
    spread = lax.optimization_barrier(jnp.mean(jnp.square(values - center), axis=1, keepdims=True))
    normed = ((values - center) * lax.rsqrt(spread + epsilon) * norm_gain).astype(jnp.bfloat16)
    hidden = jnp.maximum(jnp.dot(normed, up_weight, preferred_element_type=jnp.float32) + up_bias, 0.0).astype(jnp.bfloat16)
    result = values + jnp.dot(hidden, down_weight, preferred_element_type=jnp.float32) + down_bias
    return result.astype(jnp.bfloat16).reshape(row_count, columns, channels)

def reference(left_piece, right_piece, proj_weight, proj_bias, pair_rep, norm_gain, up_weight, up_bias, down_weight, down_bias):
    group_len = S // GROUPS
    row_block = 16
    offsets = (jnp.arange(N // row_block) * row_block).astype(jnp.int32)

    def update_rows(offset):
        summed = jnp.zeros((row_block, N, H), jnp.float32)
        for group_id in range(GROUPS):
            left_group = left_piece[group_id * group_len:(group_id + 1) * group_len]
            right_group = right_piece[group_id * group_len:(group_id + 1) * group_len]
            row_slab = lax.dynamic_slice_in_dim(left_group, offset, row_block, 2)
            summed = summed + project_block(row_slab, right_group, proj_weight)
        return (summed / S + proj_bias).astype(jnp.bfloat16)
    update = lax.map(update_rows, offsets).reshape(N, N, H)
    mirrored_all = jnp.transpose(update, (1, 0, 2))

    def finish_rows(offset):
        own_part = lax.dynamic_slice_in_dim(update, offset, row_block, 0).astype(jnp.float32)
        mirrored = lax.dynamic_slice_in_dim(mirrored_all, offset, row_block, 0).astype(jnp.float32)
        residual = lax.dynamic_slice_in_dim(pair_rep, offset, row_block, 0).astype(jnp.float32)
        middle = (residual + 0.5 * (own_part + mirrored)).astype(jnp.bfloat16)
        return transition(middle, norm_gain, up_weight, up_bias, down_weight, down_bias)
    return lax.map(finish_rows, offsets).reshape(N, N, H)
```

```python
import functools

import jax
import jax.numpy as jnp
from jax import lax
from jax.experimental import pallas as pl
from jax.experimental.pallas import tpu as pltpu
from jax.sharding import PartitionSpec as P

epsilon = 1e-05
axes = ("row", "col", "seq")


def update_kernel(groups, xs, seq_total, *refs):
    place_ref = refs[0]
    left_refs = refs[1:3]
    right_refs = refs[3 : 3 + groups * xs]
    weight_ref, bias_ref = refs[3 + groups * xs : 5 + groups * xs]
    own_ref, other_ref = refs[5 + groups * xs : 7 + groups * xs]
    mirror_refs = refs[7 + groups * xs : 7 + groups * xs + groups]
    outer_ref, update_ref = refs[7 + groups * xs + groups :]
    own_rows, channels, group_len = left_refs[0].shape[1:]
    per = right_refs[0].shape[0]
    lanes = right_refs[0].shape[2]
    half = lanes // 2
    pair_channels = weight_ref.shape[0] // 2
    block = 8
    lane_low = lax.broadcasted_iota(jnp.int32, (pair_channels, lanes), 1) < half
    bias = bias_ref[...]

    def right_tile(item):
        dx, rest = divmod(item, per)
        return jnp.concatenate(
            [right_refs[dz * xs + dx][rest] for dz in range(groups)], axis=0
        )

    for side in range(2):
        left_ref = left_refs[side]

        @pl.loop(0, own_rows // block)
        def _(step):
            start = step * block
            left = jnp.concatenate(
                [
                    left_ref[dz, pl.ds(start, block)].reshape(block * channels, group_len)
                    for dz in range(groups)
                ],
                axis=1,
            )
            for pair in range(xs * per // 2):
                right = jnp.concatenate(
                    [right_tile(2 * pair), right_tile(2 * pair + 1)], axis=1
                )
                outer = jnp.dot(left, right, preferred_element_type=jnp.float32)
                outer = outer.astype(jnp.bfloat16)
                for part in range(2):
                    item = 2 * pair + part
                    outer_ref[:, item * channels : (item + 1) * channels, :] = outer[
                        :, part * lanes : (part + 1) * lanes
                    ].reshape(block, channels, lanes)
            for two in range(block // 2):
                both = jnp.concatenate([outer_ref[2 * two], outer_ref[2 * two + 1]], axis=1)
                proj = jnp.dot(weight_ref[...], both, preferred_element_type=jnp.float32)
                a0 = proj[:pair_channels, :lanes]
                a1 = proj[:pair_channels, lanes:]
                b0 = proj[pair_channels:, :lanes]
                b1 = proj[pair_channels:, lanes:]
                cell = jnp.where(lane_low, a0, b1) + pltpu.roll(
                    jnp.where(lane_low, a1, b0), half, 1
                )
                cell = cell.T / seq_total + bias
                update_ref[pl.ds(side * own_rows + start + 2 * two, 2)] = cell.astype(
                    jnp.bfloat16
                ).reshape(2, half, pair_channels)

    own_ref[...] = update_ref[:own_rows]
    other_ref[...] = update_ref[own_rows:]
    run = half // groups
    for dz in range(groups):
        begin = pl.multiple_of((place_ref[1] ^ dz) * run, run)
        mirror_refs[dz][...] = update_ref[:, pl.ds(begin, run), :]


def finish_kernel(groups, *refs):
    place_ref, pair_ref, own_ref, other_ref = refs[:4]
    mirror_refs = refs[4 : 4 + groups]
    gain_ref, up_ref, up_bias_ref, down_ref, down_bias_ref = refs[4 + groups : 9 + groups]
    out_ref, middle_ref = refs[9 + groups :]
    own_rows, columns, pair_channels = pair_ref.shape
    half = columns // 2
    run = half // groups
    for side in range(2):
        direct_ref = (own_ref, other_ref)[side]
        for dz in range(groups):
            local = pl.multiple_of((place_ref[1] ^ dz) * run, run)
            begin = pl.multiple_of((place_ref[0] ^ side) * half + local, run)
            mirrored = mirror_refs[dz][side * own_rows : (side + 1) * own_rows]
            mirrored = jnp.swapaxes(mirrored.astype(jnp.float32), 0, 1)
            direct = direct_ref[:, pl.ds(local, run), :].astype(jnp.float32)
            residual = pair_ref[:, pl.ds(begin, run), :].astype(jnp.float32)
            middle_ref[:, pl.ds(begin, run), :] = (
                residual + 0.5 * (direct + mirrored)
            ).astype(jnp.bfloat16)

    block = 4

    @pl.loop(0, own_rows // block)
    def _(step):
        values = middle_ref[pl.ds(step * block, block)].astype(jnp.float32)
        values = values.reshape(block * columns, pair_channels)
        center = jnp.mean(values, axis=1, keepdims=True)
        moved = values - center
        spread = jnp.mean(jnp.square(moved), axis=1, keepdims=True)
        normed = (moved * lax.rsqrt(spread + epsilon) * gain_ref[...]).astype(jnp.bfloat16)
        hidden = jnp.maximum(
            jnp.dot(normed, up_ref[...], preferred_element_type=jnp.float32)
            + up_bias_ref[...],
            0.0,
        ).astype(jnp.bfloat16)
        result = (
            values
            + jnp.dot(hidden, down_ref[...], preferred_element_type=jnp.float32)
            + down_bias_ref[...]
        )
        out_ref[pl.ds(step * block, block)] = result.astype(jnp.bfloat16).reshape(
            block, columns, pair_channels
        )


def on_device(
    left_piece,
    right_piece,
    proj_weight,
    proj_bias,
    pair_rep,
    norm_gain,
    up_weight,
    up_bias,
    down_weight,
    down_bias,
):
    rows = lax.axis_size("row")
    cols = lax.axis_size("col")
    groups = lax.axis_size("seq")
    xs = rows // 2
    row, col, seq = (lax.axis_index(name) for name in axes)
    core = row % 2
    own_rows, columns, pair_channels = pair_rep.shape
    group_len, channels, _ = left_piece.shape
    part_channels = right_piece.shape[1]
    half = columns // 2
    e1 = part_channels // 2
    seq_total = group_len * groups

    def swap(value, name, size, flip):
        return lax.ppermute(value, name, [(i, i ^ flip) for i in range(size)])

    right = right_piece.reshape(group_len, e1, 2, 2, half).transpose(3, 1, 0, 2, 4)
    right = right.reshape(2, e1, group_len, 2 * half)
    kept = lax.dynamic_index_in_dim(right, core, 0, False)
    sent = lax.dynamic_index_in_dim(right, 1 - core, 0, False)
    base = jnp.concatenate([kept, swap(sent, "row", rows, 1)], axis=0)

    left = left_piece.transpose(2, 1, 0).reshape(groups, own_rows, channels, group_len)

    rights = []
    bases = [base] + [swap(base, "seq", groups, dz) for dz in range(1, groups)]
    for item in bases:
        rights.append(item)
        for dx in range(1, xs):
            rights.append(swap(item, "row", rows, 2 * dx))
    lefts = []
    for dz in range(groups):
        piece = lax.dynamic_index_in_dim(left, seq ^ dz, 0, False)
        lefts.append(swap(piece, "seq", groups, dz) if dz > 0 else piece)
    left_own = jnp.stack(lefts)
    left_other = swap(left_own, "row", rows, 1)

    weight = proj_weight.reshape(channels, rows, e1, 2, pair_channels)
    weight = weight.transpose(1, 3, 4, 2, 0)
    weight = jnp.stack(
        [lax.dynamic_index_in_dim(weight, row ^ m, 0, False) for m in range(rows)], axis=2
    )
    weight = weight.reshape(2 * pair_channels, channels * channels // 2)

    place = jnp.stack([core, seq]).astype(jnp.int32)
    vmem = pl.BlockSpec(memory_space=pltpu.VMEM)
    smem = pl.BlockSpec(memory_space=pltpu.SMEM)
    bf16 = jnp.bfloat16
    run = half // groups
    count = 5 + groups * xs
    outs = pl.pallas_call(
        functools.partial(update_kernel, groups, xs, seq_total),
        out_shape=[jax.ShapeDtypeStruct((own_rows, half, pair_channels), bf16)] * 2
        + [jax.ShapeDtypeStruct((2 * own_rows, run, pair_channels), bf16)] * groups,
        in_specs=[smem] + [vmem] * (count - 1),
        out_specs=[vmem] * (2 + groups),
        scratch_shapes=[
            pltpu.VMEM((8, channels * channels // 2, 2 * half), bf16),
            pltpu.VMEM((2 * own_rows, half, pair_channels), bf16),
        ],
        compiler_params=pltpu.CompilerParams(vmem_limit_bytes=40 * 1024 * 1024),
        name="update",
    )(place, left_own, left_other, *rights, weight, proj_bias.reshape(1, pair_channels))
    update_own, update_other = outs[:2]
    update_other = swap(update_other, "row", rows, 1)

    mirrors = []
    for dz in range(groups):
        pairs = []
        for r in range(rows):
            for c in range(cols):
                for q in range(groups):
                    source = (r * cols + c) * groups + q
                    target = ((2 * c + r % 2) * cols + r // 2) * groups + (q ^ dz)
                    pairs.append((source, target))
        mirrors.append(lax.ppermute(outs[2 + dz], axes, pairs))

    return pl.pallas_call(
        functools.partial(finish_kernel, groups),
        out_shape=jax.ShapeDtypeStruct(pair_rep.shape, bf16),
        in_specs=[smem] + [vmem] * (8 + groups),
        out_specs=vmem,
        scratch_shapes=[pltpu.VMEM(pair_rep.shape, bf16)],
        compiler_params=pltpu.CompilerParams(vmem_limit_bytes=40 * 1024 * 1024),
        name="finish",
    )(
        place,
        pair_rep,
        update_own,
        update_other,
        *mirrors,
        norm_gain.reshape(1, -1),
        up_weight,
        up_bias.reshape(1, -1),
        down_weight,
        down_bias.reshape(1, -1),
    )


def solution(mesh):
    in_specs = (
        P("seq", None, "row"),
        P("seq", "row", "col"),
        P(),
        P(),
        P(("row", "seq"), "col", None),
        P(),
        P(),
        P(),
        P(),
        P(),
    )
    out_specs = P(("row", "seq"), "col", None)
    return jax.shard_map(
        on_device, mesh=mesh, in_specs=in_specs, out_specs=out_specs, check_vma=False
    )
```

```python
import functools

import jax
import jax.numpy as jnp
from jax import lax
from jax.experimental import pallas as pl
from jax.experimental.pallas import tpu as pltpu
from jax.sharding import PartitionSpec as P

epsilon = 1e-05
axes = ("row", "col", "seq")


def update_kernel(groups, own_rows, seq_total, last, *refs):
    left_refs = refs[:2]
    position = 2
    if last:
        place_ref, bias_ref, partial_ref = refs[2:5]
        position = 5
    weight_ref = refs[position]
    outs = groups + 2 if last else 1
    scratch = 2 if last else 1
    right_refs = refs[position + 1 : len(refs) - outs - scratch]
    out_refs = refs[len(refs) - outs - scratch : len(refs) - scratch]
    outer_ref = refs[len(refs) - scratch]
    channels, group_len = left_refs[0].shape[2:]
    per, _, lanes = right_refs[0].shape
    sources = len(right_refs) // groups
    half = lanes // 2
    pair_channels = weight_ref.shape[0] // 2
    block = 8
    lane_low = lax.broadcasted_iota(jnp.int32, (pair_channels, lanes), 1) < half

    def right_tile(item):
        dx, rest = divmod(item, per)
        return jnp.concatenate(
            [right_refs[dz * sources + dx][rest] for dz in range(groups)], axis=0
        )

    for side in range(2):
        left_ref = left_refs[side]

        @pl.loop(0, own_rows // block)
        def _(step):
            start = step * block
            left = jnp.concatenate(
                [
                    left_ref[dz, pl.ds(start, block)].reshape(block * channels, group_len)
                    for dz in range(groups)
                ],
                axis=1,
            )
            for pair in range(sources * per // 2):
                right = jnp.concatenate(
                    [right_tile(2 * pair), right_tile(2 * pair + 1)], axis=1
                )
                outer = jnp.dot(left, right, preferred_element_type=jnp.float32)
                outer = outer.astype(jnp.bfloat16)
                for part in range(2):
                    item = 2 * pair + part
                    outer_ref[:, item * channels : (item + 1) * channels, :] = outer[
                        :, part * lanes : (part + 1) * lanes
                    ].reshape(block, channels, lanes)
            for two in range(block // 2):
                both = jnp.concatenate([outer_ref[2 * two], outer_ref[2 * two + 1]], axis=1)
                proj = jnp.dot(weight_ref[...], both, preferred_element_type=jnp.float32)
                a0 = proj[:pair_channels, :lanes]
                a1 = proj[:pair_channels, lanes:]
                b0 = proj[pair_channels:, :lanes]
                b1 = proj[pair_channels:, lanes:]
                cell = jnp.where(lane_low, a0, b1) + pltpu.roll(
                    jnp.where(lane_low, a1, b0), half, 1
                )
                index = (side * own_rows + start) // 2 + two
                if last:
                    cell = (cell + partial_ref[index]).T / seq_total + bias_ref[...]
                    refs[-1][pl.ds(2 * index, 2)] = cell.astype(jnp.bfloat16).reshape(
                        2, half, pair_channels
                    )
                else:
                    out_refs[0][index] = cell

    if last:
        update_ref = refs[-1]
        out_refs[0][...] = update_ref[:own_rows]
        out_refs[1][...] = update_ref[own_rows:]
        run = half // groups
        for dz in range(groups):
            begin = pl.multiple_of((place_ref[1] ^ dz) * run, run)
            out_refs[2 + dz][...] = update_ref[:, pl.ds(begin, run), :]


def finish_kernel(groups, *refs):
    place_ref, pair_ref, own_ref, other_ref = refs[:4]
    mirror_refs = refs[4 : 4 + groups]
    gain_ref, up_ref, up_bias_ref, down_ref, down_bias_ref = refs[4 + groups : 9 + groups]
    out_ref, middle_ref = refs[9 + groups :]
    own_rows, columns, pair_channels = pair_ref.shape
    half = columns // 2
    run = half // groups
    for side in range(2):
        direct_ref = (own_ref, other_ref)[side]
        for dz in range(groups):
            local = pl.multiple_of((place_ref[1] ^ dz) * run, run)
            begin = pl.multiple_of((place_ref[0] ^ side) * half + local, run)
            mirrored = mirror_refs[dz][side * own_rows : (side + 1) * own_rows]
            mirrored = jnp.swapaxes(mirrored.astype(jnp.float32), 0, 1)
            direct = direct_ref[:, pl.ds(local, run), :].astype(jnp.float32)
            residual = pair_ref[:, pl.ds(begin, run), :].astype(jnp.float32)
            middle_ref[:, pl.ds(begin, run), :] = (
                residual + 0.5 * (direct + mirrored)
            ).astype(jnp.bfloat16)

    block = 4

    @pl.loop(0, own_rows // block)
    def _(step):
        values = middle_ref[pl.ds(step * block, block)].astype(jnp.float32)
        values = values.reshape(block * columns, pair_channels)
        ones = jnp.full((pair_channels, pair_channels), 1.0 / pair_channels, jnp.bfloat16)
        center = jnp.dot(
            values.astype(jnp.bfloat16), ones, preferred_element_type=jnp.float32
        )
        moved = values - center
        square = jnp.square(moved)
        high = square.astype(jnp.bfloat16)
        low = (square - high.astype(jnp.float32)).astype(jnp.bfloat16)
        spread = jnp.dot(high, ones, preferred_element_type=jnp.float32) + jnp.dot(
            low, ones, preferred_element_type=jnp.float32
        )
        normed = (moved * lax.rsqrt(spread + epsilon) * gain_ref[...]).astype(jnp.bfloat16)
        hidden = jnp.maximum(
            jnp.dot(normed, up_ref[...], preferred_element_type=jnp.float32)
            + up_bias_ref[...],
            0.0,
        ).astype(jnp.bfloat16)
        result = (
            values
            + jnp.dot(hidden, down_ref[...], preferred_element_type=jnp.float32)
            + down_bias_ref[...]
        )
        out_ref[pl.ds(step * block, block)] = result.astype(jnp.bfloat16).reshape(
            block, columns, pair_channels
        )


def on_device(
    left_piece,
    right_piece,
    proj_weight,
    proj_bias,
    pair_rep,
    norm_gain,
    up_weight,
    up_bias,
    down_weight,
    down_bias,
):
    rows = lax.axis_size("row")
    cols = lax.axis_size("col")
    groups = lax.axis_size("seq")
    xs = rows // 2
    row, col, seq = (lax.axis_index(name) for name in axes)
    core = row % 2
    own_rows, columns, pair_channels = pair_rep.shape
    group_len, channels, _ = left_piece.shape
    part_channels = right_piece.shape[1]
    half = columns // 2
    e1 = part_channels // 2
    seq_total = group_len * groups

    def swap(value, name, size, flip):
        return lax.ppermute(value, name, [(i, i ^ flip) for i in range(size)])

    share = own_rows // cols
    left = left_piece.transpose(2, 1, 0).reshape(groups, cols, share, channels, group_len)
    left = lax.dynamic_index_in_dim(left, col, 1, False)
    lefts = []
    for dz in range(groups):
        piece = lax.dynamic_index_in_dim(left, seq ^ dz, 0, False)
        lefts.append(swap(piece, "seq", groups, dz) if dz > 0 else piece)
    left = jnp.stack(lefts)
    shares = [left] + [swap(left, "col", cols, dy) for dy in range(1, cols)]
    stacked = jnp.stack(shares)
    stacked = jnp.stack(
        [lax.dynamic_index_in_dim(stacked, col ^ dy, 0, False) for dy in range(cols)], axis=1
    )
    left_own = stacked.reshape(groups, own_rows, channels, group_len)
    left_other = swap(left_own, "row", rows, 1)

    right = right_piece.reshape(group_len, e1, 2, 2, half).transpose(3, 1, 0, 2, 4)
    right = right.reshape(2, e1, group_len, 2 * half)
    kept = lax.dynamic_index_in_dim(right, core, 0, False)
    sent = lax.dynamic_index_in_dim(right, 1 - core, 0, False)
    base = jnp.concatenate([kept, swap(sent, "row", rows, 1)], axis=0)

    def cross(value):
        return [value] + [swap(value, "row", rows, 2 * dx) for dx in range(1, xs)]

    if groups == 4:
        middle = jnp.logical_or(seq == 1, seq == 2)
        near = swap(base, "seq", groups, 1)
        inner = lax.ppermute(base, "seq", [(1, 2), (2, 1)])
        first = cross(base)
        near_held, _ = lax.optimization_barrier((near, first[-1]))
        across = lax.ppermute(near, "seq", [(1, 2), (2, 1)])
        outward = lax.ppermute(inner, "seq", [(1, 0), (2, 3)])
        second = cross(near_held)
        farther = lax.ppermute(across, "seq", [(1, 0), (2, 3)])
        block_a = jnp.where(middle, inner, outward)
        block_b = jnp.where(middle, across, farther)
        block_a, _ = lax.optimization_barrier((block_a, second[-1]))
        third = cross(block_a)
        block_b, _ = lax.optimization_barrier((block_b, third[-1]))
        fourth = cross(block_b)
        rights = first + second + third + fourth
        swapped = jnp.concatenate([left_own[:2], left_own[3:], left_own[2:3]])
        left_own = jnp.where(middle, swapped, left_own)
        swapped = jnp.concatenate([left_other[:2], left_other[3:], left_other[2:3]])
        left_other = jnp.where(middle, swapped, left_other)
    else:
        rights = cross(base)
        for dz in range(1, groups):
            rights += cross(swap(base, "seq", groups, dz))

    weight = proj_weight.reshape(channels, rows, e1, 2, pair_channels)
    weight = weight.transpose(1, 3, 4, 2, 0)
    weight = jnp.stack(
        [lax.dynamic_index_in_dim(weight, row ^ m, 0, False) for m in range(rows)], axis=2
    )
    weight = weight.reshape(2 * pair_channels, channels * channels // 2)
    split = channels * channels // 2 // xs

    place = jnp.stack([core, seq]).astype(jnp.int32)
    vmem = pl.BlockSpec(memory_space=pltpu.VMEM)
    smem = pl.BlockSpec(memory_space=pltpu.SMEM)
    bf16 = jnp.bfloat16
    run = half // groups
    params = pltpu.CompilerParams(vmem_limit_bytes=40 * 1024 * 1024)
    partial = pl.pallas_call(
        functools.partial(update_kernel, groups, own_rows, seq_total, False),
        out_shape=jax.ShapeDtypeStruct((own_rows, pair_channels, 2 * half), jnp.float32),
        in_specs=[vmem] * (3 + groups),
        out_specs=vmem,
        scratch_shapes=[pltpu.VMEM((8, split, 2 * half), bf16)],
        compiler_params=params,
        name="update_first",
    )(left_own, left_other, weight[:, :split], *rights[::xs])
    others = [rights[i] for i in range(groups * xs) if i % xs > 0]
    outs = pl.pallas_call(
        functools.partial(update_kernel, groups, own_rows, seq_total, True),
        out_shape=[jax.ShapeDtypeStruct((own_rows, half, pair_channels), bf16)] * 2
        + [jax.ShapeDtypeStruct((2 * own_rows, run, pair_channels), bf16)] * groups,
        in_specs=[vmem] * 2 + [smem] + [vmem] * (3 + len(others)),
        out_specs=[vmem] * (2 + groups),
        scratch_shapes=[
            pltpu.VMEM((8, (xs - 1) * split, 2 * half), bf16),
            pltpu.VMEM((2 * own_rows, half, pair_channels), bf16),
        ],
        compiler_params=params,
        name="update_last",
    )(
        left_own,
        left_other,
        place,
        proj_bias.reshape(1, pair_channels),
        partial,
        weight[:, split:],
        *others,
    )
    update_own, update_other = outs[:2]
    update_other = swap(update_other, "row", rows, 1)

    mirrors = []
    for dz in range(groups):
        pairs = []
        for r in range(rows):
            for c in range(cols):
                for q in range(groups):
                    source = (r * cols + c) * groups + q
                    target = ((2 * c + r % 2) * cols + r // 2) * groups + (q ^ dz)
                    pairs.append((source, target))
        mirrors.append(lax.ppermute(outs[2 + dz], axes, pairs))

    return pl.pallas_call(
        functools.partial(finish_kernel, groups),
        out_shape=jax.ShapeDtypeStruct(pair_rep.shape, bf16),
        in_specs=[smem] + [vmem] * (8 + groups),
        out_specs=vmem,
        scratch_shapes=[pltpu.VMEM(pair_rep.shape, bf16)],
        compiler_params=pltpu.CompilerParams(vmem_limit_bytes=40 * 1024 * 1024),
        name="finish",
    )(
        place,
        pair_rep,
        update_own,
        update_other,
        *mirrors,
        norm_gain.reshape(1, -1),
        up_weight,
        up_bias.reshape(1, -1),
        down_weight,
        down_bias.reshape(1, -1),
    )


def solution(mesh):
    in_specs = (
        P("seq", None, "row"),
        P("seq", "row", "col"),
        P(),
        P(),
        P(("row", "seq"), "col", None),
        P(),
        P(),
        P(),
        P(),
        P(),
    )
    out_specs = P(("row", "seq"), "col", None)
    return jax.shard_map(
        on_device, mesh=mesh, in_specs=in_specs, out_specs=out_specs, check_vma=False
    )
```

```python
import functools

import jax
import jax.numpy as jnp
from jax import lax
from jax.experimental import pallas as pl
from jax.experimental.pallas import tpu as pltpu
from jax.sharding import PartitionSpec as P

epsilon = 1e-05
axes = ("row", "col", "seq")


def update_kernel(groups, shares, low, last, scale, *refs):
    refs = list(refs)
    place_ref = refs.pop(0)
    left_refs = [refs.pop(0) for _ in range(groups * shares)]
    bias_ref, partial_ref = (refs.pop(0), refs.pop(0)) if last else (None, None)
    weight_ref = refs.pop(0)
    update_ref = refs.pop() if last else None
    outer_ref = refs.pop()
    lhs_ref = refs.pop()
    outs = 2 + 2 * low if last else 1
    right_refs, out_refs = refs[:-outs], refs[-outs:]
    share, channels, group_len = left_refs[0].shape
    per, _, lanes = right_refs[0].shape
    sources = len(right_refs) // groups
    half = lanes // 2
    pair_channels = weight_ref.shape[0] // 2
    block = 8
    row_count = share * shares
    lane_low = lax.broadcasted_iota(jnp.int32, (pair_channels, lanes), 1) < half
    for dy in range(shares):
        begin = pl.multiple_of((place_ref[2] ^ dy) * share * channels, share * channels)
        for dz in range(groups):
            lhs_ref[pl.ds(begin, share * channels), dz * group_len : (dz + 1) * group_len] = (
                left_refs[dz * shares + dy][...].reshape(share * channels, group_len)
            )

    def right_tile(item):
        source, rest = divmod(item, per)
        return jnp.concatenate(
            [right_refs[dz * sources + source][rest] for dz in range(groups)], axis=0
        )

    @pl.loop(0, row_count // block)
    def _(step):
        start = step * block
        left = lhs_ref[pl.ds(start * channels, block * channels)]
        for pair in range(sources * per // 2):
            right = jnp.concatenate([right_tile(2 * pair), right_tile(2 * pair + 1)], axis=1)
            outer = jnp.dot(left, right, preferred_element_type=jnp.float32)
            outer = outer.astype(jnp.bfloat16)
            for part in range(2):
                item = 2 * pair + part
                outer_ref[:, item * channels : (item + 1) * channels, :] = outer[
                    :, part * lanes : (part + 1) * lanes
                ].reshape(block, channels, lanes)
        for two in range(block // 2):
            both = jnp.concatenate([outer_ref[2 * two], outer_ref[2 * two + 1]], axis=1)
            proj = jnp.dot(weight_ref[...], both, preferred_element_type=jnp.float32)
            a0 = proj[:pair_channels, :lanes]
            a1 = proj[:pair_channels, lanes:]
            b0 = proj[pair_channels:, :lanes]
            b1 = proj[pair_channels:, lanes:]
            cell = jnp.where(lane_low, a0, b1) + pltpu.roll(
                jnp.where(lane_low, a1, b0), half, 1
            )
            index = start // 2 + two
            if last:
                cell = (cell + partial_ref[index]) * scale + bias_ref[...]
                update_ref[pl.ds(2 * index, 2)] = (
                    cell.astype(jnp.bfloat16).T.reshape(2, half, pair_channels)
                )
            else:
                out_refs[0][index] = cell

    if last:
        core, z_low, z_high = place_ref[0], place_ref[1], place_ref[3]
        run = row_count // 2
        out_refs[0][...] = update_ref[pl.ds(z_high * run, run)]
        out_refs[1][...] = update_ref[pl.ds((1 - z_high) * run, run)]
        for flip in range(2):
            for dz in range(low):
                begin = (core ^ flip) * (half // 2) + (z_low ^ dz) * run
                out_refs[2 + flip * low + dz][...] = update_ref[
                    :, pl.ds(pl.multiple_of(begin, run), run), :
                ]


def finish_kernel(low, *refs):
    place_ref, pair_ref, own_ref, other_ref = refs[:4]
    mirror_refs = refs[4 : 4 + 2 * low]
    gain_ref, up_ref, up_bias_ref, down_ref, down_bias_ref, out_ref = refs[4 + 2 * low :]
    run, columns, pair_channels = pair_ref.shape
    half = columns // 2
    core, z_low, z_high = place_ref[0], place_ref[1], place_ref[3]
    cells = run * run
    to = lax.broadcasted_iota(jnp.int32, (cells, cells), 0)
    of = lax.broadcasted_iota(jnp.int32, (cells, cells), 1)
    swap_cells = jnp.where(
        jnp.logical_and(to // run == of % run, to % run == of // run), 1.0, 0.0
    ).astype(jnp.bfloat16)
    ones = jnp.full((2 * pair_channels, pair_channels), 1.0 / pair_channels, jnp.bfloat16)
    for dz in range(low):
        for flip in range(2):
            for part in range(2):
                local = (core ^ flip) * (half // 2) + (z_low ^ dz) * run
                local = pl.multiple_of(local, run)
                begin = (core ^ flip) * half + (part * low + (z_low ^ dz)) * run
                begin = pl.multiple_of(begin, run)
                piece = mirror_refs[flip * low + dz][part * run : (part + 1) * run]
                mirrored = jnp.dot(
                    swap_cells,
                    piece.reshape(cells, pair_channels),
                    preferred_element_type=jnp.float32,
                )
                direct = jnp.where(
                    z_high == part,
                    own_ref[:, pl.ds(local, run), :],
                    other_ref[:, pl.ds(local, run), :],
                ).reshape(cells, pair_channels)
                residual = pair_ref[:, pl.ds(begin, run), :].reshape(cells, pair_channels)
                middle = (
                    residual.astype(jnp.float32) + 0.5 * (direct.astype(jnp.float32) + mirrored)
                ).astype(jnp.bfloat16)
                values = middle.astype(jnp.float32)
                center = jnp.dot(
                    middle, ones[:pair_channels], preferred_element_type=jnp.float32
                )
                moved = values - center
                square = jnp.square(moved)
                high = square.astype(jnp.bfloat16)
                rest = (square - high.astype(jnp.float32)).astype(jnp.bfloat16)
                spread = jnp.dot(
                    jnp.concatenate([high, rest], axis=1),
                    ones,
                    preferred_element_type=jnp.float32,
                )
                normed = moved * lax.rsqrt(spread + epsilon) * gain_ref[...]
                hidden = jnp.dot(
                    normed.astype(jnp.bfloat16), up_ref[...], preferred_element_type=jnp.float32
                )
                hidden = jnp.maximum(hidden + up_bias_ref[...], 0.0).astype(jnp.bfloat16)
                result = (
                    values
                    + jnp.dot(hidden, down_ref[...], preferred_element_type=jnp.float32)
                    + down_bias_ref[...]
                )
                out_ref[:, pl.ds(begin, run), :] = result.astype(jnp.bfloat16).reshape(
                    run, run, pair_channels
                )


def on_device(
    left_piece,
    right_piece,
    proj_weight,
    proj_bias,
    pair_rep,
    norm_gain,
    up_weight,
    up_bias,
    down_weight,
    down_bias,
):
    rows = lax.axis_size("row")
    cols = lax.axis_size("col")
    groups = lax.axis_size("seq")
    xs = rows // 2
    low = groups // 2
    row, col, seq = (lax.axis_index(name) for name in axes)
    core, z_low, z_high = row % 2, seq % low, seq // low
    run, columns, pair_channels = pair_rep.shape
    group_len, channels, _ = left_piece.shape
    e1 = right_piece.shape[1] // 2
    half = columns // 2
    bf16 = jnp.bfloat16

    def pick(value, index, axis=0):
        return lax.dynamic_index_in_dim(value, index, axis, False)

    def swap(value, name, size, flip):
        return lax.ppermute(value, name, [(i, i ^ flip) for i in range(size)])

    right = right_piece.reshape(group_len, e1, 2, 2, 2, half // 2).transpose(4, 1, 0, 2, 3, 5)
    right = right.reshape(2, e1, group_len, 2 * half)
    mine = pick(right, z_high)
    theirs = pick(right, 1 - z_high)
    blocks = [mine]
    for dz in range(1, groups):
        blocks.append(swap(theirs if dz >= low else mine, "seq", groups, dz))
    firsts, others = [], []
    chain = None
    for block in blocks:
        firsts += [block, swap(block, "row", rows, 1)]
        for dx in range(1, xs):
            if chain is not None:
                block, _ = lax.optimization_barrier((block, chain))
            chain = swap(block, "row", rows, 2 * dx)
            others += [chain, swap(chain, "row", rows, 1)]

    share = 2 * run // cols
    left_piece, _ = lax.optimization_barrier((left_piece, mine))
    left = left_piece.transpose(2, 1, 0).reshape(2, low, run, channels, group_len)
    left = left.transpose(1, 0, 2, 3, 4).reshape(low, cols, share, channels, group_len)
    left = pick(left, col, 1)
    lefts = []
    for dz in range(groups):
        piece = pick(left, z_low ^ (dz % low))
        piece = swap(piece, "seq", groups, dz) if dz > 0 else piece
        lefts += [piece] + [swap(piece, "col", cols, dy) for dy in range(1, cols)]

    weight = proj_weight.reshape(channels, rows, e1, 2, pair_channels)
    weight = weight.transpose(1, 3, 4, 2, 0)
    weight = jnp.stack([pick(weight, row ^ m) for m in range(rows)], axis=2)
    weight = weight.reshape(2 * pair_channels, channels * channels // 2)
    split = channels * channels // 2 // xs

    place = jnp.stack([core, z_low, col, z_high]).astype(jnp.int32)
    vmem = pl.BlockSpec(memory_space=pltpu.VMEM)
    smem = pl.BlockSpec(memory_space=pltpu.SMEM)
    params = pltpu.CompilerParams(vmem_limit_bytes=40 * 1024 * 1024)
    scale = 1.0 / (group_len * groups)
    lhs = pltpu.VMEM((2 * run * channels, groups * group_len), bf16)
    partial = pl.pallas_call(
        functools.partial(update_kernel, groups, cols, low, False, scale),
        out_shape=jax.ShapeDtypeStruct((run, pair_channels, 2 * half), jnp.float32),
        in_specs=[smem] + [vmem] * (len(lefts) + 1 + len(firsts)),
        out_specs=vmem,
        scratch_shapes=[lhs, pltpu.VMEM((8, split, 2 * half), bf16)],
        compiler_params=params,
        name="update_first",
    )(place, *lefts, weight[:, :split], *firsts)
    bias = jnp.broadcast_to(proj_bias[:, None], (pair_channels, 2 * half))
    outs = pl.pallas_call(
        functools.partial(update_kernel, groups, cols, low, True, scale),
        out_shape=[jax.ShapeDtypeStruct((run, half, pair_channels), bf16)] * 2
        + [jax.ShapeDtypeStruct((2 * run, run, pair_channels), bf16)] * (2 * low),
        in_specs=[smem] + [vmem] * (len(lefts) + 3 + len(others)),
        out_specs=[vmem] * (2 + 2 * low),
        scratch_shapes=[
            lhs,
            pltpu.VMEM((8, (xs - 1) * split, 2 * half), bf16),
            pltpu.VMEM((2 * run, half, pair_channels), bf16),
        ],
        compiler_params=params,
        name="update_last",
    )(place, *lefts, bias, partial, weight[:, split:], *others)

    mirrors = []
    for flip in range(2):
        for dz in range(low):
            pairs = []
            for r in range(rows):
                for c in range(cols):
                    for q in range(groups):
                        source = (r * cols + c) * groups + q
                        target = 2 * c + (r % 2 ^ flip)
                        target = (target * cols + r // 2) * groups + (q ^ dz)
                        pairs.append((source, target))
            mirrors.append(lax.ppermute(outs[2 + flip * low + dz], axes, pairs))
    update_other = swap(outs[1], "seq", groups, low)

    return pl.pallas_call(
        functools.partial(finish_kernel, low),
        out_shape=jax.ShapeDtypeStruct(pair_rep.shape, bf16),
        in_specs=[smem] + [vmem] * (8 + 2 * low),
        out_specs=vmem,
        compiler_params=params,
        name="finish",
    )(
        place,
        pair_rep,
        outs[0],
        update_other,
        *mirrors,
        norm_gain.reshape(1, -1),
        up_weight,
        up_bias.reshape(1, -1),
        down_weight,
        down_bias.reshape(1, -1),
    )


def solution(mesh):
    in_specs = (
        P("seq", None, "row"),
        P("seq", "row", "col"),
        P(),
        P(),
        P(("row", "seq"), "col", None),
        P(),
        P(),
        P(),
        P(),
        P(),
    )
    out_specs = P(("row", "seq"), "col", None)
    return jax.shard_map(
        on_device, mesh=mesh, in_specs=in_specs, out_specs=out_specs, check_vma=False
    )
```

```python
import functools

import jax
import jax.numpy as jnp
from jax import lax
from jax.experimental import pallas as pl
from jax.experimental.pallas import tpu as pltpu
from jax.sharding import PartitionSpec as P

epsilon = 1e-05
axes = ("row", "col", "seq")


def update_kernel(places, shares, low, last, scale, *refs):
    left_places, right_places, share_rows, source_rows, group_len, operands = places
    refs = list(refs)
    place_ref = refs.pop(0)
    data_refs = [refs.pop(0) for _ in range(operands)]
    bias_ref, partial_ref = (refs.pop(0), refs.pop(0)) if last else (None, None)
    weight_ref = refs.pop(0)
    update_ref = refs.pop() if last else None
    outer_ref = refs.pop()
    lhs_ref = refs.pop()
    out_refs = refs
    groups = len(left_places)
    row_count, _, lanes = outer_ref.shape
    channels = share_rows * shares // row_count
    per = source_rows // group_len
    sources = len(right_places[0])
    half = lanes // 2
    pair_channels = weight_ref.shape[0] // 2
    lane_low = lax.broadcasted_iota(jnp.int32, (pair_channels, lanes), 1) < half
    for dy in range(shares):
        begin = pl.multiple_of((place_ref[2] ^ dy) * share_rows, share_rows)
        for dz in range(groups):
            operand, first = left_places[dz][dy]
            lhs_ref[pl.ds(begin, share_rows), dz * group_len : (dz + 1) * group_len] = data_refs[
                operand
            ][first : first + share_rows]

    def right_tile(item):
        source, rest = divmod(item, per)
        tiles = []
        for dz in range(groups):
            operand, first = right_places[dz][source]
            first += rest * group_len
            tiles.append(data_refs[operand][first : first + group_len])
        return jnp.concatenate(tiles, axis=0)

    for pair in range(sources * per // 2):
        right = jnp.concatenate([right_tile(2 * pair), right_tile(2 * pair + 1)], axis=1)
        outer = jnp.dot(lhs_ref[...], right, preferred_element_type=jnp.float32)
        outer = outer.astype(jnp.bfloat16)
        for part in range(2):
            item = 2 * pair + part
            outer_ref[:, item * channels : (item + 1) * channels, :] = outer[
                :, part * lanes : (part + 1) * lanes
            ].reshape(row_count, channels, lanes)

    @pl.loop(0, row_count // 8)
    def _(step):
        for two in range(4):
            index = step * 4 + two
            both = jnp.concatenate([outer_ref[2 * index], outer_ref[2 * index + 1]], axis=1)
            proj = jnp.dot(weight_ref[...], both, preferred_element_type=jnp.float32)
            a0 = proj[:pair_channels, :lanes]
            a1 = proj[:pair_channels, lanes:]
            b0 = proj[pair_channels:, :lanes]
            b1 = proj[pair_channels:, lanes:]
            cell = jnp.where(lane_low, a0, b1) + pltpu.roll(
                jnp.where(lane_low, a1, b0), half, 1
            )
            if last:
                cell = (cell + partial_ref[index]) * scale + bias_ref[...]
                update_ref[pl.ds(2 * index, 2)] = (
                    cell.astype(jnp.bfloat16).T.reshape(2, half, pair_channels)
                )
            else:
                out_refs[0][index] = cell

    if last:
        core, z_low, z_high = place_ref[0], place_ref[1], place_ref[3]
        run = row_count // 2
        out_refs[0][...] = update_ref[pl.ds(z_high * run, run)]
        out_refs[1][...] = update_ref[pl.ds((1 - z_high) * run, run)]
        for dz in range(low):
            for flip in range(2):
                begin = (core ^ flip) * (half // 2) + (z_low ^ dz) * run
                out_refs[2 + 2 * dz + flip][...] = update_ref[
                    :, pl.ds(pl.multiple_of(begin, run), run), :
                ]


def finish_kernel(low, dz, *refs):
    place_ref, pair_ref, own_ref, other_ref, mirror_low, mirror_high = refs[:6]
    gain_ref, up_ref, up_bias_ref, down_ref, down_bias_ref = refs[6:11]
    out_ref, middle_ref, done_ref, sems = refs[-4:]
    mirror_refs = (mirror_low, mirror_high)
    run, columns, pair_channels = pair_ref.shape
    half = columns // 2
    core, z_low, z_high = place_ref[0], place_ref[1], place_ref[3]
    cells = run * run
    to = lax.broadcasted_iota(jnp.int32, (cells, cells), 0)
    of = lax.broadcasted_iota(jnp.int32, (cells, cells), 1)
    swap_cells = jnp.where(
        jnp.logical_and(to // run == of % run, to % run == of // run), 1.0, 0.0
    ).astype(jnp.bfloat16)
    begins = []
    for flip in range(2):
        for part in range(2):
            index = 2 * flip + part
            local = (core ^ flip) * (half // 2) + (z_low ^ dz) * run
            local = pl.multiple_of(local, run)
            begin = (core ^ flip) * half + (part * low + (z_low ^ dz)) * run
            begin = pl.multiple_of(begin, run)
            begins.append(begin)
            piece = mirror_refs[flip][part * run : (part + 1) * run]
            mirrored = jnp.dot(
                swap_cells,
                piece.reshape(cells, pair_channels),
                preferred_element_type=jnp.float32,
            )
            direct = jnp.where(
                z_high == part,
                own_ref[:, pl.ds(local, run), :],
                other_ref[:, pl.ds(local, run), :],
            ).reshape(cells, pair_channels)
            residual = pair_ref[:, pl.ds(begin, run), :].reshape(cells, pair_channels)
            middle_ref[index * cells : (index + 1) * cells] = (
                residual.astype(jnp.float32) + 0.5 * (direct.astype(jnp.float32) + mirrored)
            ).astype(jnp.bfloat16)

    values = middle_ref[...].astype(jnp.float32)
    center = jnp.mean(values, axis=1, keepdims=True)
    moved = values - center
    spread = jnp.mean(jnp.square(moved), axis=1, keepdims=True)
    normed = moved * lax.rsqrt(spread + epsilon) * gain_ref[...]
    hidden = jnp.dot(
        normed.astype(jnp.bfloat16), up_ref[...], preferred_element_type=jnp.float32
    )
    hidden = jnp.maximum(hidden + up_bias_ref[...], 0.0).astype(jnp.bfloat16)
    result = jnp.dot(hidden, down_ref[...], preferred_element_type=jnp.float32)
    result = (values + result + down_bias_ref[...]).astype(jnp.bfloat16)
    done_ref[...] = result.reshape(4, run, run, pair_channels)
    copies = [
        pltpu.make_async_copy(
            done_ref.at[index], out_ref.at[:, pl.ds(begins[index], run), :], sems.at[index]
        )
        for index in range(4)
    ]
    for copy in copies:
        copy.start()
    for copy in copies:
        copy.wait()


def on_device(
    left_piece,
    right_piece,
    proj_weight,
    proj_bias,
    pair_rep,
    norm_gain,
    up_weight,
    up_bias,
    down_weight,
    down_bias,
):
    rows = lax.axis_size("row")
    cols = lax.axis_size("col")
    groups = lax.axis_size("seq")
    xs = rows // 2
    low = groups // 2
    row, col, seq = (lax.axis_index(name) for name in axes)
    core, z_low, z_high = row % 2, seq % low, seq // low
    run, columns, pair_channels = pair_rep.shape
    group_len, channels, _ = left_piece.shape
    e1 = right_piece.shape[1] // 2
    half = columns // 2
    bf16 = jnp.bfloat16

    def pick(value, index, axis=0):
        return lax.dynamic_index_in_dim(value, index, axis, False)

    def swap(value, name, size, flip):
        return lax.ppermute(value, name, [(i, i ^ flip) for i in range(size)])

    right = right_piece.reshape(group_len, e1, 2, 2, 2, half // 2).transpose(4, 1, 0, 2, 3, 5)
    source_rows = e1 * group_len
    right = right.reshape(2, source_rows, 2 * half)
    share_rows = 2 * run // cols * channels
    left = left_piece.transpose(2, 1, 0).reshape(2, low, run, channels, group_len)
    left = left.transpose(1, 0, 2, 3, 4).reshape(low, cols, share_rows, group_len)
    left = pick(left, col, 1)

    def packed(dz):
        return jnp.concatenate(
            [pick(right, z_high ^ (dz // low)), pick(left, z_low ^ (dz % low))], axis=0
        )

    order = [0, 1] + list(range(groups - 1, 1, -1))
    held = {dz: packed(dz) if dz == 0 else swap(packed(dz), "seq", groups, dz) for dz in order}
    bundles = [order[:2]] + [[dz] for dz in order[2:]]
    data, left_places, right_places, other_places = [], {}, {}, {}
    for dz in range(groups):
        left_places[dz] = [(len(data), source_rows)]
        right_places[dz] = [(len(data), 0)]
        other_places[dz] = []
        data.append(held[dz])
    others = []
    for bundle in bundles:
        rights = jnp.concatenate([held[dz][:source_rows] for dz in bundle], axis=0)
        lefts = jnp.concatenate([held[dz][source_rows:] for dz in bundle], axis=0)
        for position, dz in enumerate(bundle):
            right_places[dz].append((len(data), position * source_rows))
        data.append(swap(rights, "row", rows, 1))
        for dy in range(1, cols):
            for position, dz in enumerate(bundle):
                left_places[dz].append((len(data), position * share_rows))
            data.append(swap(lefts, "col", cols, dy))
        for dx in range(1, xs):
            crossed = swap(rights, "row", rows, 2 * dx)
            for value in (crossed, swap(crossed, "row", rows, 1)):
                for position, dz in enumerate(bundle):
                    other_places[dz].append((len(others), position * source_rows))
                others.append(value)

    weight = proj_weight.reshape(channels, rows, e1, 2, pair_channels)
    weight = weight.transpose(1, 3, 4, 2, 0)
    weight = jnp.stack([pick(weight, row ^ m) for m in range(rows)], axis=2)
    weight = weight.reshape(2 * pair_channels, channels * channels // 2)
    split = channels * channels // 2 // xs

    place = jnp.stack([core, z_low, col, z_high]).astype(jnp.int32)
    vmem = pl.BlockSpec(memory_space=pltpu.VMEM)
    smem = pl.BlockSpec(memory_space=pltpu.SMEM)
    params = pltpu.CompilerParams(vmem_limit_bytes=40 * 1024 * 1024)
    scale = 1.0 / (group_len * groups)
    lhs = pltpu.VMEM((2 * run * channels, groups * group_len), bf16)

    def tabled(table):
        return [table[dz] for dz in range(groups)]

    sizes = (share_rows, source_rows, group_len)
    places = (tabled(left_places), tabled(right_places)) + sizes + (len(data),)
    partial = pl.pallas_call(
        functools.partial(update_kernel, places, cols, low, False, scale),
        out_shape=jax.ShapeDtypeStruct((run, pair_channels, 2 * half), jnp.float32),
        in_specs=[smem] + [vmem] * (len(data) + 1),
        out_specs=vmem,
        scratch_shapes=[lhs, pltpu.VMEM((2 * run, split, 2 * half), bf16)],
        compiler_params=params,
        name="update_first",
    )(place, *data, weight[:, :split])
    shifted = [[(o + len(data), f) for o, f in other_places[dz]] for dz in range(groups)]
    places = (tabled(left_places), shifted) + sizes + (len(data) + len(others),)
    bias = jnp.broadcast_to(proj_bias[:, None], (pair_channels, 2 * half))
    outs = pl.pallas_call(
        functools.partial(update_kernel, places, cols, low, True, scale),
        out_shape=[jax.ShapeDtypeStruct((run, half, pair_channels), bf16)] * 2
        + [jax.ShapeDtypeStruct((2 * run, run, pair_channels), bf16)] * (2 * low),
        in_specs=[smem] + [vmem] * (len(data) + len(others) + 3),
        out_specs=[vmem] * (2 + 2 * low),
        scratch_shapes=[
            lhs,
            pltpu.VMEM((2 * run, (xs - 1) * split, 2 * half), bf16),
            pltpu.VMEM((2 * run, half, pair_channels), bf16),
        ],
        compiler_params=params,
        name="update_last",
    )(place, *data, *others, bias, partial, weight[:, split:])

    update_other = swap(outs[1], "seq", groups, low)
    mirrors = []
    for dz in range(low):
        for flip in range(2):
            pairs = []
            for r in range(rows):
                for c in range(cols):
                    for q in range(groups):
                        source = (r * cols + c) * groups + q
                        target = 2 * c + (r % 2 ^ flip)
                        target = (target * cols + r // 2) * groups + (q ^ dz)
                        pairs.append((source, target))
            mirrors.append(lax.ppermute(outs[2 + 2 * dz + flip], axes, pairs))

    anywhere = pl.BlockSpec(memory_space=pl.ANY)
    result = None
    for dz in range(low):
        operands = [
            place,
            pair_rep,
            outs[0],
            update_other,
            mirrors[2 * dz],
            mirrors[2 * dz + 1],
            norm_gain.reshape(1, -1),
            up_weight,
            up_bias.reshape(1, -1),
            down_weight,
            down_bias.reshape(1, -1),
        ]
        extra = [] if result is None else [result]
        result = pl.pallas_call(
            functools.partial(finish_kernel, low, dz),
            out_shape=jax.ShapeDtypeStruct(pair_rep.shape, bf16),
            in_specs=[smem] + [vmem] * 10 + [anywhere] * len(extra),
            out_specs=anywhere,
            scratch_shapes=[
                pltpu.VMEM((4 * run * run, pair_channels), bf16),
                pltpu.VMEM((4, run, run, pair_channels), bf16),
                pltpu.SemaphoreType.DMA((4,)),
            ],
            input_output_aliases={11: 0} if extra else {},
            compiler_params=params,
            name="finish",
        )(*operands, *extra)
    return result


def solution(mesh):
    in_specs = (
        P("seq", None, "row"),
        P("seq", "row", "col"),
        P(),
        P(),
        P(("row", "seq"), "col", None),
        P(),
        P(),
        P(),
        P(),
        P(),
    )
    out_specs = P(("row", "seq"), "col", None)
    return jax.shard_map(
        on_device, mesh=mesh, in_specs=in_specs, out_specs=out_specs, check_vma=False
    )
```

```python
import functools

import jax
import jax.numpy as jnp
from jax import lax
from jax.experimental import pallas as pl
from jax.experimental.pallas import tpu as pltpu
from jax.sharding import PartitionSpec as P

epsilon = 1e-05
axes = ("row", "col", "seq")


def update_kernel(places, shares, low, last, scale, *refs):
    left_places, right_places, share_rows, source_rows, group_len, operands = places
    refs = list(refs)
    place_ref = refs.pop(0)
    data_refs = [refs.pop(0) for _ in range(operands)]
    bias_ref, partial_ref = (refs.pop(0), refs.pop(0)) if last else (None, None)
    weight_ref = refs.pop(0)
    update_ref = refs.pop() if last else None
    outer_ref = refs.pop()
    lhs_ref = refs.pop()
    out_refs = refs
    groups = len(left_places)
    row_count, _, lanes = outer_ref.shape
    channels = share_rows * shares // row_count
    per = source_rows // group_len
    sources = len(right_places[0])
    half = lanes // 2
    pair_channels = weight_ref.shape[0] // 2
    lane_low = lax.broadcasted_iota(jnp.int32, (pair_channels, lanes), 1) < half
    for dy in range(shares):
        begin = pl.multiple_of((place_ref[2] ^ dy) * share_rows, share_rows)
        for dz in range(groups):
            operand, first = left_places[dz][dy]
            lhs_ref[pl.ds(begin, share_rows), dz * group_len : (dz + 1) * group_len] = data_refs[
                operand
            ][first : first + share_rows]

    def right_tile(item):
        source, rest = divmod(item, per)
        tiles = []
        for dz in range(groups):
            operand, first = right_places[dz][source]
            first += rest * group_len
            tiles.append(data_refs[operand][first : first + group_len])
        return jnp.concatenate(tiles, axis=0)

    for pair in range(sources * per // 2):
        right = jnp.concatenate([right_tile(2 * pair), right_tile(2 * pair + 1)], axis=1)
        outer = jnp.dot(lhs_ref[...], right, preferred_element_type=jnp.float32)
        outer = outer.astype(jnp.bfloat16)
        for part in range(2):
            item = 2 * pair + part
            outer_ref[:, item * channels : (item + 1) * channels, :] = outer[
                :, part * lanes : (part + 1) * lanes
            ].reshape(row_count, channels, lanes)

    @pl.loop(0, row_count // 8)
    def _(step):
        for two in range(4):
            index = step * 4 + two
            both = jnp.concatenate([outer_ref[2 * index], outer_ref[2 * index + 1]], axis=1)
            proj = jnp.dot(weight_ref[...], both, preferred_element_type=jnp.float32)
            a0 = proj[:pair_channels, :lanes]
            a1 = proj[:pair_channels, lanes:]
            b0 = proj[pair_channels:, :lanes]
            b1 = proj[pair_channels:, lanes:]
            cell = jnp.where(lane_low, a0, b1) + pltpu.roll(
                jnp.where(lane_low, a1, b0), half, 1
            )
            if last:
                cell = (cell + partial_ref[index]) * scale + bias_ref[...]
                update_ref[pl.ds(2 * index, 2)] = (
                    cell.astype(jnp.bfloat16).T.reshape(2, half, pair_channels)
                )
            else:
                out_refs[0][index] = cell

    if last:
        core, z_low, z_high = place_ref[0], place_ref[1], place_ref[3]
        run = row_count // 2
        out_refs[0][...] = update_ref[pl.ds(z_high * run, run)]
        out_refs[1][...] = update_ref[pl.ds((1 - z_high) * run, run)]
        for dz in range(low):
            for flip in range(2):
                begin = (core ^ flip) * (half // 2) + (z_low ^ dz) * run
                out_refs[2 + 2 * dz + flip][...] = update_ref[
                    :, pl.ds(pl.multiple_of(begin, run), run), :
                ]


def finish_kernel(low, dz, *refs):
    place_ref, pair_ref, own_ref, other_ref, mirror_low, mirror_high = refs[:6]
    up_ref, down_ref, vector_ref, swap_ref = refs[6:10]
    out_ref, middle_ref, done_ref, sems = refs[-4:]
    mirror_refs = (mirror_low, mirror_high)
    run, columns, pair_channels = pair_ref.shape
    half = columns // 2
    core, z_low, z_high = place_ref[0], place_ref[1], place_ref[3]
    cells = run * run
    gain = vector_ref[:, :pair_channels]
    down_bias = vector_ref[:, pair_channels : 2 * pair_channels]
    up_bias = vector_ref[:, 2 * pair_channels :]
    begins = []
    for flip in range(2):
        for part in range(2):
            index = 2 * flip + part
            local = (core ^ flip) * (half // 2) + (z_low ^ dz) * run
            local = pl.multiple_of(local, run)
            begin = (core ^ flip) * half + (part * low + (z_low ^ dz)) * run
            begin = pl.multiple_of(begin, run)
            begins.append(begin)
            piece = mirror_refs[flip][part * run : (part + 1) * run]
            mirrored = jnp.dot(
                swap_ref[...],
                piece.reshape(cells, pair_channels),
                preferred_element_type=jnp.float32,
            )
            direct = jnp.where(
                z_high == part,
                own_ref[:, pl.ds(local, run), :],
                other_ref[:, pl.ds(local, run), :],
            ).reshape(cells, pair_channels)
            residual = pair_ref[:, pl.ds(begin, run), :].reshape(cells, pair_channels)
            middle_ref[index * cells : (index + 1) * cells] = (
                residual.astype(jnp.float32) + 0.5 * (direct.astype(jnp.float32) + mirrored)
            ).astype(jnp.bfloat16)

    values = middle_ref[...].astype(jnp.float32)
    center = jnp.mean(values, axis=1, keepdims=True)
    moved = values - center
    spread = jnp.mean(jnp.square(moved), axis=1, keepdims=True)
    normed = moved * lax.rsqrt(spread + epsilon) * gain
    hidden = jnp.dot(
        normed.astype(jnp.bfloat16), up_ref[...], preferred_element_type=jnp.float32
    )
    hidden = jnp.maximum(hidden + up_bias, 0.0).astype(jnp.bfloat16)
    result = jnp.dot(hidden, down_ref[...], preferred_element_type=jnp.float32)
    result = (values + result + down_bias).astype(jnp.bfloat16)
    done_ref[...] = result.reshape(4, run, run, pair_channels)
    copies = [
        pltpu.make_async_copy(
            done_ref.at[index], out_ref.at[:, pl.ds(begins[index], run), :], sems.at[index]
        )
        for index in range(4)
    ]
    for copy in copies:
        copy.start()
    for copy in copies:
        copy.wait()


def on_device(
    left_piece,
    right_piece,
    proj_weight,
    proj_bias,
    pair_rep,
    norm_gain,
    up_weight,
    up_bias,
    down_weight,
    down_bias,
):
    rows = lax.axis_size("row")
    cols = lax.axis_size("col")
    groups = lax.axis_size("seq")
    xs = rows // 2
    low = groups // 2
    row, col, seq = (lax.axis_index(name) for name in axes)
    core, z_low, z_high = row % 2, seq % low, seq // low
    run, columns, pair_channels = pair_rep.shape
    group_len, channels, _ = left_piece.shape
    e1 = right_piece.shape[1] // 2
    half = columns // 2
    bf16 = jnp.bfloat16

    def pick(value, index, axis=0):
        return lax.dynamic_index_in_dim(value, index, axis, False)

    def swap(value, name, size, flip):
        return lax.ppermute(value, name, [(i, i ^ flip) for i in range(size)])

    right = right_piece.reshape(group_len, e1, 2, 2, 2, half // 2).transpose(4, 1, 0, 2, 3, 5)
    source_rows = e1 * group_len
    right = right.reshape(2, source_rows, 2 * half)
    share_rows = 2 * run // cols * channels
    left = left_piece.transpose(2, 1, 0).reshape(2, low, run, channels, group_len)
    left = left.transpose(1, 0, 2, 3, 4).reshape(low, cols, share_rows, group_len)
    left = pick(left, col, 1)

    blocks = [
        (pick(right, z_high ^ (dz // low)), pick(left, z_low ^ (dz % low))) for dz in range(groups)
    ]
    packs = [jnp.concatenate(pair, axis=0) for pair in blocks[:2] + blocks[3:]]
    packs = lax.optimization_barrier(packs + list(blocks[2]))
    own, packs, (final_right, final_left) = packs[0], packs[1:-2], packs[-2:]
    partners = [1] + list(range(3, groups))
    held = {dz: swap(pack, "seq", groups, dz) for dz, pack in zip(partners, packs)}
    final_left = swap(final_left, "seq", groups, 2)
    final_right = swap(final_right, "seq", groups, 2)
    held[0], _ = lax.optimization_barrier((own, held[1]))
    data, others = [], []
    left_places = {dz: [] for dz in range(groups)}
    right_places = {dz: [] for dz in range(groups)}
    other_places = {dz: [] for dz in range(groups)}

    def place_in(store, table, value, bundle, size):
        for position, dz in enumerate(bundle):
            table[dz].append((len(store), position * size))
        store.append(value)

    for dz in [0] + partners:
        left_places[dz].append((len(data), source_rows))
        right_places[dz].append((len(data), 0))
        data.append(held[dz])
    place_in(data, left_places, final_left, [2], share_rows)
    place_in(data, right_places, final_right, [2], source_rows)

    bundles = [[0, 1]] + [[dz] for dz in partners[1:]] + [[2]]
    rights, crosses = [], {dx: [] for dx in range(1, xs)}
    chain = None
    for bundle in bundles:
        if bundle == [2]:
            value, lefts = final_right, final_left
        elif len(bundle) > 1:
            value = jnp.concatenate([held[dz][:source_rows] for dz in bundle], axis=0)
            lefts = jnp.concatenate([held[dz][source_rows:] for dz in bundle], axis=0)
        else:
            value, lefts = held[bundle[0]][:source_rows], held[bundle[0]][source_rows:]
        rights.append(value)
        for dy in range(1, cols):
            place_in(data, left_places, swap(lefts, "col", cols, dy), bundle, share_rows)
        for dx in range(1, xs):
            if chain is not None:
                value, _ = lax.optimization_barrier((value, chain))
            chain = swap(value, "row", rows, 2 * dx)
            crosses[dx].append(chain)

    early = [dz for bundle in bundles[:-1] for dz in bundle]
    place_in(
        data, right_places, swap(jnp.concatenate(rights[:-1], axis=0), "row", rows, 1), early,
        source_rows,
    )
    place_in(data, right_places, swap(rights[-1], "row", rows, 1), [2], source_rows)
    for dx in range(1, xs):
        for value, bundle in zip(crosses[dx], bundles):
            place_in(others, other_places, value, bundle, source_rows)
        value = swap(jnp.concatenate(crosses[dx][:-1], axis=0), "row", rows, 1)
        place_in(others, other_places, value, early, source_rows)
        place_in(others, other_places, swap(crosses[dx][-1], "row", rows, 1), [2], source_rows)

    weight = proj_weight.reshape(channels, rows, e1, 2, pair_channels)
    weight = weight.transpose(1, 3, 4, 2, 0)
    weight = jnp.stack([pick(weight, row ^ m) for m in range(rows)], axis=2)
    weight = weight.reshape(2 * pair_channels, channels * channels // 2)
    split = channels * channels // 2 // xs

    place = jnp.stack([core, z_low, col, z_high]).astype(jnp.int32)
    vmem = pl.BlockSpec(memory_space=pltpu.VMEM)
    smem = pl.BlockSpec(memory_space=pltpu.SMEM)
    params = pltpu.CompilerParams(vmem_limit_bytes=40 * 1024 * 1024)
    scale = 1.0 / (group_len * groups)
    lhs = pltpu.VMEM((2 * run * channels, groups * group_len), bf16)

    def tabled(table):
        return [table[dz] for dz in range(groups)]

    sizes = (share_rows, source_rows, group_len)
    places = (tabled(left_places), tabled(right_places)) + sizes + (len(data),)
    partial = pl.pallas_call(
        functools.partial(update_kernel, places, cols, low, False, scale),
        out_shape=jax.ShapeDtypeStruct((run, pair_channels, 2 * half), jnp.float32),
        in_specs=[smem] + [vmem] * (len(data) + 1),
        out_specs=vmem,
        scratch_shapes=[lhs, pltpu.VMEM((2 * run, split, 2 * half), bf16)],
        compiler_params=params,
        name="update_first",
    )(place, *data, weight[:, :split])
    shifted = [[(o + len(data), f) for o, f in other_places[dz]] for dz in range(groups)]
    places = (tabled(left_places), shifted) + sizes + (len(data) + len(others),)
    bias = jnp.broadcast_to(proj_bias[:, None], (pair_channels, 2 * half))
    outs = pl.pallas_call(
        functools.partial(update_kernel, places, cols, low, True, scale),
        out_shape=[jax.ShapeDtypeStruct((run, half, pair_channels), bf16)] * 2
        + [jax.ShapeDtypeStruct((2 * run, run, pair_channels), bf16)] * (2 * low),
        in_specs=[smem] + [vmem] * (len(data) + len(others) + 3),
        out_specs=[vmem] * (2 + 2 * low),
        scratch_shapes=[
            lhs,
            pltpu.VMEM((2 * run, (xs - 1) * split, 2 * half), bf16),
            pltpu.VMEM((2 * run, half, pair_channels), bf16),
        ],
        compiler_params=params,
        name="update_last",
    )(place, *data, *others, bias, partial, weight[:, split:])

    update_other = swap(outs[1], "seq", groups, low)
    mirrors = []
    for dz in range(low):
        for flip in range(2):
            pairs = []
            for r in range(rows):
                for c in range(cols):
                    for q in range(groups):
                        source = (r * cols + c) * groups + q
                        target = 2 * c + (r % 2 ^ flip)
                        target = (target * cols + r // 2) * groups + (q ^ dz)
                        pairs.append((source, target))
            mirrors.append(lax.ppermute(outs[2 + 2 * dz + flip], axes, pairs))

    vectors = jnp.concatenate([norm_gain, down_bias, up_bias]).reshape(1, -1)
    cell = jnp.arange(run * run)
    mirror_cell = cell % run * run + cell // run
    swap_cells = (mirror_cell[:, None] == cell[None, :]).astype(bf16)
    anywhere = pl.BlockSpec(memory_space=pl.ANY)
    result = None
    for dz in range(low):
        operands = [
            place,
            pair_rep,
            outs[0],
            update_other,
            mirrors[2 * dz],
            mirrors[2 * dz + 1],
            up_weight,
            down_weight,
            vectors,
            swap_cells,
        ]
        extra = [] if result is None else [result]
        result = pl.pallas_call(
            functools.partial(finish_kernel, low, dz),
            out_shape=jax.ShapeDtypeStruct(pair_rep.shape, bf16),
            in_specs=[smem] + [vmem] * 9 + [anywhere] * len(extra),
            out_specs=anywhere,
            scratch_shapes=[
                pltpu.VMEM((4 * run * run, pair_channels), bf16),
                pltpu.VMEM((4, run, run, pair_channels), bf16),
                pltpu.SemaphoreType.DMA((4,)),
            ],
            input_output_aliases={10: 0} if extra else {},
            compiler_params=params,
            name="finish",
        )(*operands, *extra)
    return result


def solution(mesh):
    in_specs = (
        P("seq", None, "row"),
        P("seq", "row", "col"),
        P(),
        P(),
        P(("row", "seq"), "col", None),
        P(),
        P(),
        P(),
        P(),
        P(),
    )
    out_specs = P(("row", "seq"), "col", None)
    return jax.shard_map(
        on_device, mesh=mesh, in_specs=in_specs, out_specs=out_specs, check_vma=False
    )
```

```python
import functools

import jax
import jax.numpy as jnp
from jax import lax
from jax.experimental import pallas as pl
from jax.experimental.pallas import tpu as pltpu
from jax.sharding import PartitionSpec as P

epsilon = 1e-05
axes = ("row", "col", "seq")


def update_kernel(places, shares, low, last, scale, *refs):
    left_places, right_places, share_rows, source_rows, group_len, operands = places
    refs = list(refs)
    place_ref = refs.pop(0)
    data_refs = [refs.pop(0) for _ in range(operands)]
    bias_ref, partial_ref = (refs.pop(0), refs.pop(0)) if last else (None, None)
    weight_ref = refs.pop(0)
    update_ref = refs.pop() if last else None
    outer_ref = refs.pop()
    lhs_ref = refs.pop()
    out_refs = refs
    groups = len(left_places)
    row_count, _, lanes = outer_ref.shape
    channels = share_rows * shares // row_count
    per = source_rows // group_len
    sources = len(right_places[0])
    half = lanes // 2
    pair_channels = weight_ref.shape[0] // 2
    lane_low = lax.broadcasted_iota(jnp.int32, (pair_channels, lanes), 1) < half
    for dy in range(shares):
        begin = pl.multiple_of((place_ref[2] ^ dy) * share_rows, share_rows)
        for dz in range(groups):
            operand, first = left_places[dz][dy]
            lhs_ref[pl.ds(begin, share_rows), dz * group_len : (dz + 1) * group_len] = data_refs[
                operand
            ][first : first + share_rows]

    def right_tile(item):
        source, rest = divmod(item, per)
        tiles = []
        for dz in range(groups):
            operand, first = right_places[dz][source]
            first += rest * group_len
            tiles.append(data_refs[operand][first : first + group_len])
        return jnp.concatenate(tiles, axis=0)

    for pair in range(sources * per // 2):
        right = jnp.concatenate([right_tile(2 * pair), right_tile(2 * pair + 1)], axis=1)
        outer = jnp.dot(lhs_ref[...], right, preferred_element_type=jnp.float32)
        outer = outer.astype(jnp.bfloat16)
        for part in range(2):
            item = 2 * pair + part
            outer_ref[:, item * channels : (item + 1) * channels, :] = outer[
                :, part * lanes : (part + 1) * lanes
            ].reshape(row_count, channels, lanes)

    @pl.loop(0, row_count // 8)
    def _(step):
        for two in range(4):
            index = step * 4 + two
            both = jnp.concatenate([outer_ref[2 * index], outer_ref[2 * index + 1]], axis=1)
            proj = jnp.dot(weight_ref[...], both, preferred_element_type=jnp.float32)
            a0 = proj[:pair_channels, :lanes]
            a1 = proj[:pair_channels, lanes:]
            b0 = proj[pair_channels:, :lanes]
            b1 = proj[pair_channels:, lanes:]
            cell = jnp.where(lane_low, a0, b1) + pltpu.roll(
                jnp.where(lane_low, a1, b0), half, 1
            )
            if last:
                cell = (cell + partial_ref[index]) * scale + bias_ref[...]
                update_ref[pl.ds(2 * index, 2)] = (
                    cell.astype(jnp.bfloat16).T.reshape(2, half, pair_channels)
                )
            else:
                out_refs[0][index] = cell

    if last:
        core, z_low, z_high = place_ref[0], place_ref[1], place_ref[3]
        run = row_count // 2
        out_refs[0][...] = update_ref[pl.ds(z_high * run, run)]
        out_refs[1][...] = update_ref[pl.ds((1 - z_high) * run, run)]
        for dz in range(low):
            for flip in range(2):
                begin = (core ^ flip) * (half // 2) + (z_low ^ dz) * run
                out_refs[2 + 2 * dz + flip][...] = update_ref[
                    :, pl.ds(pl.multiple_of(begin, run), run), :
                ]


def finish_kernel(low, dz, *refs):
    place_ref, pair_ref, own_ref, other_ref, mirror_low, mirror_high = refs[:6]
    up_ref, down_ref, vector_ref, swap_ref = refs[6:10]
    out_ref, middle_ref, done_ref, sems = refs[-4:]
    mirror_refs = (mirror_low, mirror_high)
    run, columns, pair_channels = pair_ref.shape
    half = columns // 2
    core, z_low, z_high = place_ref[0], place_ref[1], place_ref[3]
    cells = run * run
    gain = vector_ref[:, :pair_channels]
    down_bias = vector_ref[:, pair_channels : 2 * pair_channels]
    up_bias = vector_ref[:, 2 * pair_channels :]
    begins = []
    for flip in range(2):
        for part in range(2):
            index = 2 * flip + part
            local = (core ^ flip) * (half // 2) + (z_low ^ dz) * run
            local = pl.multiple_of(local, run)
            begin = (core ^ flip) * half + (part * low + (z_low ^ dz)) * run
            begin = pl.multiple_of(begin, run)
            begins.append(begin)
            piece = mirror_refs[flip][part * run : (part + 1) * run]
            mirrored = jnp.dot(
                swap_ref[...],
                piece.reshape(cells, pair_channels),
                preferred_element_type=jnp.float32,
            )
            direct = jnp.where(
                z_high == part,
                own_ref[:, pl.ds(local, run), :],
                other_ref[:, pl.ds(local, run), :],
            ).reshape(cells, pair_channels)
            residual = pair_ref[:, pl.ds(begin, run), :].reshape(cells, pair_channels)
            middle_ref[index * cells : (index + 1) * cells] = (
                residual.astype(jnp.float32) + 0.5 * (direct.astype(jnp.float32) + mirrored)
            ).astype(jnp.bfloat16)

    values = middle_ref[...].astype(jnp.float32)
    center = jnp.mean(values, axis=1, keepdims=True)
    moved = values - center
    spread = jnp.mean(jnp.square(moved), axis=1, keepdims=True)
    normed = moved * lax.rsqrt(spread + epsilon) * gain
    hidden = jnp.dot(
        normed.astype(jnp.bfloat16), up_ref[...], preferred_element_type=jnp.float32
    )
    hidden = jnp.maximum(hidden + up_bias, 0.0).astype(jnp.bfloat16)
    result = jnp.dot(hidden, down_ref[...], preferred_element_type=jnp.float32)
    result = (values + result + down_bias).astype(jnp.bfloat16)
    done_ref[...] = result.reshape(4, run, run, pair_channels)
    copies = [
        pltpu.make_async_copy(
            done_ref.at[index], out_ref.at[:, pl.ds(begins[index], run), :], sems.at[index]
        )
        for index in range(4)
    ]
    for copy in copies:
        copy.start()
    for copy in copies:
        copy.wait()


def on_device(
    left_piece,
    right_piece,
    proj_weight,
    proj_bias,
    pair_rep,
    norm_gain,
    up_weight,
    up_bias,
    down_weight,
    down_bias,
):
    rows = lax.axis_size("row")
    cols = lax.axis_size("col")
    groups = lax.axis_size("seq")
    xs = rows // 2
    low = groups // 2
    row, col, seq = (lax.axis_index(name) for name in axes)
    core, z_low, z_high = row % 2, seq % low, seq // low
    run, columns, pair_channels = pair_rep.shape
    group_len, channels, _ = left_piece.shape
    e1 = right_piece.shape[1] // 2
    half = columns // 2
    bf16 = jnp.bfloat16

    def pick(value, index, axis=0):
        return lax.dynamic_index_in_dim(value, index, axis, False)

    def swap(value, name, size, flip):
        return lax.ppermute(value, name, [(i, i ^ flip) for i in range(size)])

    right = right_piece.reshape(group_len, e1, 2, 2, 2, half // 2).transpose(4, 1, 0, 2, 3, 5)
    source_rows = e1 * group_len
    right = right.reshape(2, source_rows, 2 * half)
    share_rows = 2 * run // cols * channels
    left = left_piece.transpose(2, 1, 0).reshape(2, low, run, channels, group_len)
    left = left.transpose(1, 0, 2, 3, 4).reshape(low, cols, share_rows, group_len)
    left = pick(left, col, 1)

    def after(value, *earlier):
        return lax.optimization_barrier((value, earlier))[0] if earlier else value

    right_sends = [pick(right, z_high ^ (dz // low)) for dz in range(groups)]
    left_sends = [pick(left, z_low ^ (dz % low)) for dz in range(groups)]
    rights, lefts = {0: right_sends[0]}, {0: left_sends[0]}
    crossed = {dz: [] for dz in range(groups)}
    shared = {dz: [] for dz in range(groups)}

    def along(sends, dz, *earlier):
        return swap(after(sends[dz], *earlier), "seq", groups, dz)

    def over_x(dz, *earlier):
        for dx in range(1, xs):
            value = swap(after(rights[dz], *earlier), "row", rows, 2 * dx)
            crossed[dz].append(value)
            earlier = (value,)
        return earlier

    def over_y(dz, *earlier):
        for dy in range(1, cols):
            value = swap(after(lefts[dz], *earlier), "col", cols, dy)
            shared[dz].append(value)
            earlier = (value,)
        return earlier

    rights[3] = along(right_sends, 3)
    rights[1] = along(right_sends, 1)
    last_x = over_x(0, rights[1])
    last_y = over_y(0)
    lefts[3] = along(left_sends, 3, rights[1])
    lefts[1] = along(left_sends, 1)
    last_x = over_x(1, *last_x)
    lefts[2] = along(left_sends, 2, rights[3])
    last_x = over_x(3, *last_x)
    last_y = over_y(1, *last_y)
    rights[2] = along(right_sends, 2, lefts[3])
    last_y = over_y(3, *last_y)
    cored, cored_too = {}, {}
    for dz in (0, 1, 3):
        cored[dz] = swap(after(rights[dz], lefts[3]), "row", rows, 1)
        cored_too[dz] = [swap(after(value, lefts[2]), "row", rows, 1) for value in crossed[dz]]
    last_y = over_y(2, *last_y)
    rights[2] = after(rights[2], *last_y)
    over_x(2)
    cored[2] = swap(rights[2], "row", rows, 1)
    cored_too[2] = [swap(value, "row", rows, 1) for value in crossed[2]]

    data, others = [], []
    left_places = {dz: [] for dz in range(groups)}
    right_places = {dz: [] for dz in range(groups)}
    other_places = {dz: [] for dz in range(groups)}

    def place_in(store, table, dz, value):
        table[dz].append((len(store), 0))
        store.append(value)

    for dz in range(groups):
        for value in [lefts[dz]] + shared[dz]:
            place_in(data, left_places, dz, value)
        for value in (rights[dz], cored[dz]):
            place_in(data, right_places, dz, value)
        for pair in zip(crossed[dz], cored_too[dz]):
            for value in pair:
                place_in(others, other_places, dz, value)

    weight = proj_weight.reshape(channels, rows, e1, 2, pair_channels)
    weight = weight.transpose(1, 3, 4, 2, 0)
    weight = jnp.stack([pick(weight, row ^ m) for m in range(rows)], axis=2)
    weight = weight.reshape(2 * pair_channels, channels * channels // 2)
    split = channels * channels // 2 // xs

    place = jnp.stack([core, z_low, col, z_high]).astype(jnp.int32)
    vmem = pl.BlockSpec(memory_space=pltpu.VMEM)
    smem = pl.BlockSpec(memory_space=pltpu.SMEM)
    params = pltpu.CompilerParams(vmem_limit_bytes=40 * 1024 * 1024)
    scale = 1.0 / (group_len * groups)
    lhs = pltpu.VMEM((2 * run * channels, groups * group_len), bf16)

    def tabled(table):
        return [table[dz] for dz in range(groups)]

    sizes = (share_rows, source_rows, group_len)
    places = (tabled(left_places), tabled(right_places)) + sizes + (len(data),)
    outer_size = 4 * run * channels * split * half
    cost = pl.CostEstimate(
        flops=2 * outer_size * (groups * group_len + 2 * pair_channels),
        bytes_accessed=2 * outer_size,
        transcendentals=0,
    )
    partial = pl.pallas_call(
        functools.partial(update_kernel, places, cols, low, False, scale),
        out_shape=jax.ShapeDtypeStruct((run, pair_channels, 2 * half), jnp.float32),
        in_specs=[smem] + [vmem] * (len(data) + 1),
        out_specs=vmem,
        scratch_shapes=[lhs, pltpu.VMEM((2 * run, split, 2 * half), bf16)],
        compiler_params=params,
        cost_estimate=cost,
        name="update_first",
    )(place, *data, weight[:, :split])
    shifted = [[(o + len(data), f) for o, f in other_places[dz]] for dz in range(groups)]
    places = (tabled(left_places), shifted) + sizes + (len(data) + len(others),)
    bias = jnp.broadcast_to(proj_bias[:, None], (pair_channels, 2 * half))
    outs = pl.pallas_call(
        functools.partial(update_kernel, places, cols, low, True, scale),
        out_shape=[jax.ShapeDtypeStruct((run, half, pair_channels), bf16)] * 2
        + [jax.ShapeDtypeStruct((2 * run, run, pair_channels), bf16)] * (2 * low),
        in_specs=[smem] + [vmem] * (len(data) + len(others) + 3),
        out_specs=[vmem] * (2 + 2 * low),
        scratch_shapes=[
            lhs,
            pltpu.VMEM((2 * run, (xs - 1) * split, 2 * half), bf16),
            pltpu.VMEM((2 * run, half, pair_channels), bf16),
        ],
        compiler_params=params,
        cost_estimate=cost,
        name="update_last",
    )(place, *data, *others, bias, partial, weight[:, split:])

    update_other = swap(outs[1], "seq", groups, low)
    mirrors = []
    for dz in range(low):
        for flip in range(2):
            pairs = []
            for r in range(rows):
                for c in range(cols):
                    for q in range(groups):
                        source = (r * cols + c) * groups + q
                        target = 2 * c + (r % 2 ^ flip)
                        target = (target * cols + r // 2) * groups + (q ^ dz)
                        pairs.append((source, target))
            mirrors.append(lax.ppermute(outs[2 + 2 * dz + flip], axes, pairs))

    vectors = jnp.concatenate([norm_gain, down_bias, up_bias]).reshape(1, -1)
    cell = jnp.arange(run * run)
    mirror_cell = cell % run * run + cell // run
    swap_cells = (mirror_cell[:, None] == cell[None, :]).astype(bf16)
    anywhere = pl.BlockSpec(memory_space=pl.ANY)
    result = None
    for dz in range(low):
        operands = [
            place,
            pair_rep,
            outs[0],
            update_other,
            mirrors[2 * dz],
            mirrors[2 * dz + 1],
            up_weight,
            down_weight,
            vectors,
            swap_cells,
        ]
        extra = [] if result is None else [result]
        result = pl.pallas_call(
            functools.partial(finish_kernel, low, dz),
            out_shape=jax.ShapeDtypeStruct(pair_rep.shape, bf16),
            in_specs=[smem] + [vmem] * 9 + [anywhere] * len(extra),
            out_specs=anywhere,
            scratch_shapes=[
                pltpu.VMEM((4 * run * run, pair_channels), bf16),
                pltpu.VMEM((4, run, run, pair_channels), bf16),
                pltpu.SemaphoreType.DMA((4,)),
            ],
            input_output_aliases={10: 0} if extra else {},
            compiler_params=params,
            name="finish",
        )(*operands, *extra)
    return result


def solution(mesh):
    in_specs = (
        P("seq", None, "row"),
        P("seq", "row", "col"),
        P(),
        P(),
        P(("row", "seq"), "col", None),
        P(),
        P(),
        P(),
        P(),
        P(),
    )
    out_specs = P(("row", "seq"), "col", None)
    return jax.shard_map(
        on_device, mesh=mesh, in_specs=in_specs, out_specs=out_specs, check_vma=False
    )
```

```python
import functools

import jax
import jax.numpy as jnp
from jax import lax
from jax.experimental import pallas as pl
from jax.experimental.pallas import tpu as pltpu
from jax.sharding import PartitionSpec as P

epsilon = 1e-05
axes = ("row", "col", "seq")


def update_kernel(places, shares, low, last, scale, *refs):
    left_count, right_places, share_rows, source_rows, group_len, run = places
    groups = len(right_places)
    sources = len(right_places[0])
    refs = list(refs)
    place_ref = refs.pop(0)
    left_refs = [refs.pop(0) for _ in range(left_count)]
    data_refs = [refs.pop(0) for _ in range(groups * sources)]
    bias_ref, weight_ref = refs.pop(0), refs.pop(0)
    first_ref = refs.pop(0) if last else None
    update_ref = refs.pop() if last else refs[0]
    outer_ref = refs.pop()
    lhs_ref = refs.pop()
    out_refs = refs
    row_count, _, lanes = outer_ref.shape
    blocks = left_count // groups
    channels = share_rows * blocks // row_count
    share = share_rows // channels
    per = source_rows // group_len
    half = lanes // 2
    pair_channels = weight_ref.shape[0] // 2
    lane_low = lax.broadcasted_iota(jnp.int32, (pair_channels, lanes), 1) < half
    for block in range(blocks):
        for dz in range(groups):
            lhs_ref[
                block * share_rows : (block + 1) * share_rows,
                dz * group_len : (dz + 1) * group_len,
            ] = left_refs[dz * blocks + block][...]

    def right_tile(item):
        source, rest = divmod(item, per)
        tiles = []
        for dz in range(groups):
            first = rest * group_len
            tiles.append(data_refs[right_places[dz][source]][first : first + group_len])
        return jnp.concatenate(tiles, axis=0)

    for pair in range(sources * per // 2):
        right = jnp.concatenate([right_tile(2 * pair), right_tile(2 * pair + 1)], axis=1)
        outer = jnp.dot(lhs_ref[...], right, preferred_element_type=jnp.float32)
        outer = outer.astype(jnp.bfloat16)
        for part in range(2):
            item = 2 * pair + part
            outer_ref[:, item * channels : (item + 1) * channels, :] = outer[
                :, part * lanes : (part + 1) * lanes
            ].reshape(row_count, channels, lanes)

    unroll = min(4, row_count // 2)

    @pl.loop(0, row_count // (2 * unroll))
    def _(step):
        for two in range(unroll):
            index = step * unroll + two
            both = jnp.concatenate([outer_ref[2 * index], outer_ref[2 * index + 1]], axis=1)
            proj = jnp.dot(weight_ref[...], both, preferred_element_type=jnp.float32)
            a0 = proj[:pair_channels, :lanes]
            a1 = proj[:pair_channels, lanes:]
            b0 = proj[pair_channels:, :lanes]
            b1 = proj[pair_channels:, lanes:]
            cell = jnp.where(lane_low, a0, b1) + pltpu.roll(
                jnp.where(lane_low, a1, b0), half, 1
            )
            cell = (cell * scale + bias_ref[...]).astype(jnp.bfloat16)
            begin = 2 * index
            if last:
                begin = (place_ref[2] ^ (1 + begin // share)) * share + begin % share
            update_ref[pl.ds(begin, 2)] = cell.T.reshape(2, half, pair_channels)

    if last:
        update_ref[pl.ds(place_ref[2] * share, share)] = first_ref[...]
        core, z_low, z_high = place_ref[0], place_ref[1], place_ref[3]
        out_refs[0][...] = update_ref[pl.ds(z_high * run, run)]
        out_refs[1][...] = update_ref[pl.ds((1 - z_high) * run, run)]
        for dz in range(low):
            for flip in range(2):
                begin = (core ^ flip) * (half // 2) + (z_low ^ dz) * run
                out_refs[2 + 2 * dz + flip][...] = update_ref[
                    :, pl.ds(pl.multiple_of(begin, run), run), :
                ]


def finish_kernel(low, dz, *refs):
    place_ref, pair_ref, own_ref, other_ref, mirror_low, mirror_high = refs[:6]
    up_ref, down_ref, vector_ref, swap_ref = refs[6:10]
    out_ref, middle_ref, done_ref, sems = refs[-4:]
    mirror_refs = (mirror_low, mirror_high)
    run, columns, pair_channels = pair_ref.shape
    half = columns // 2
    core, z_low, z_high = place_ref[0], place_ref[1], place_ref[3]
    cells = run * run
    gain = vector_ref[:, :pair_channels]
    down_bias = vector_ref[:, pair_channels : 2 * pair_channels]
    up_bias = vector_ref[:, 2 * pair_channels :]
    begins = []
    for flip in range(2):
        for part in range(2):
            index = 2 * flip + part
            local = (core ^ flip) * (half // 2) + (z_low ^ dz) * run
            local = pl.multiple_of(local, run)
            begin = (core ^ flip) * half + (part * low + (z_low ^ dz)) * run
            begin = pl.multiple_of(begin, run)
            begins.append(begin)
            piece = mirror_refs[flip][part * run : (part + 1) * run]
            mirrored = jnp.dot(
                swap_ref[...],
                piece.reshape(cells, pair_channels),
                preferred_element_type=jnp.float32,
            )
            direct = jnp.where(
                z_high == part,
                own_ref[:, pl.ds(local, run), :],
                other_ref[:, pl.ds(local, run), :],
            ).reshape(cells, pair_channels)
            residual = pair_ref[:, pl.ds(begin, run), :].reshape(cells, pair_channels)
            middle_ref[index * cells : (index + 1) * cells] = (
                residual.astype(jnp.float32) + 0.5 * (direct.astype(jnp.float32) + mirrored)
            ).astype(jnp.bfloat16)

    values = middle_ref[...].astype(jnp.float32)
    center = jnp.mean(values, axis=1, keepdims=True)
    moved = values - center
    spread = jnp.mean(jnp.square(moved), axis=1, keepdims=True)
    normed = moved * lax.rsqrt(spread + epsilon) * gain
    hidden = jnp.dot(
        normed.astype(jnp.bfloat16), up_ref[...], preferred_element_type=jnp.float32
    )
    hidden = jnp.maximum(hidden + up_bias, 0.0).astype(jnp.bfloat16)
    result = jnp.dot(hidden, down_ref[...], preferred_element_type=jnp.float32)
    result = (values + result + down_bias).astype(jnp.bfloat16)
    done_ref[...] = result.reshape(4, run, run, pair_channels)
    copies = [
        pltpu.make_async_copy(
            done_ref.at[index], out_ref.at[:, pl.ds(begins[index], run), :], sems.at[index]
        )
        for index in range(4)
    ]
    for copy in copies:
        copy.start()
    for copy in copies:
        copy.wait()


def on_device(
    left_piece,
    right_piece,
    proj_weight,
    proj_bias,
    pair_rep,
    norm_gain,
    up_weight,
    up_bias,
    down_weight,
    down_bias,
):
    rows = lax.axis_size("row")
    cols = lax.axis_size("col")
    groups = lax.axis_size("seq")
    xs = rows // 2
    low = groups // 2
    row, col, seq = (lax.axis_index(name) for name in axes)
    core, z_low, z_high = row % 2, seq % low, seq // low
    run, columns, pair_channels = pair_rep.shape
    group_len, channels, _ = left_piece.shape
    e1 = right_piece.shape[1] // 2
    half = columns // 2
    bf16 = jnp.bfloat16

    def pick(value, index, axis=0):
        return lax.dynamic_index_in_dim(value, index, axis, False)

    def swap(value, name, size, flip):
        return lax.ppermute(value, name, [(i, i ^ flip) for i in range(size)])

    right = right_piece.reshape(group_len, e1, 2, 2, 2, half // 2).transpose(4, 1, 0, 2, 3, 5)
    source_rows = e1 * group_len
    right = right.reshape(2, source_rows, 2 * half)
    share_rows = 2 * run // cols * channels
    left = left_piece.transpose(2, 1, 0).reshape(2, low, run, channels, group_len)
    left = left.transpose(1, 0, 2, 3, 4).reshape(low, cols, share_rows, group_len)
    left = pick(left, col, 1)

    def after(value, *earlier):
        return lax.optimization_barrier((value, earlier))[0] if earlier else value

    right_sends = [pick(right, z_high ^ (dz // low)) for dz in range(groups)]
    left_sends = [pick(left, z_low ^ (dz % low)) for dz in range(groups)]
    rights, lefts = {0: right_sends[0]}, {0: left_sends[0]}
    crossed = {dz: [] for dz in range(groups)}
    shared = {dz: [] for dz in range(groups)}

    def along(sends, dz, *earlier):
        return swap(after(sends[dz], *earlier), "seq", groups, dz)

    def over_x(dz, *earlier):
        for dx in range(1, xs):
            value = swap(after(rights[dz], *earlier), "row", rows, 2 * dx)
            crossed[dz].append(value)
            earlier = (value,)
        return earlier

    def over_y(dz, *earlier):
        for dy in range(1, cols):
            value = swap(after(lefts[dz], *earlier), "col", cols, dy)
            shared[dz].append(value)
            earlier = (value,)
        return earlier

    rights[3] = along(right_sends, 3)
    rights[1] = along(right_sends, 1)
    last_x = over_x(0)
    last_x = over_x(1, *last_x)
    lefts[3] = along(left_sends, 3, rights[1])
    lefts[1] = along(left_sends, 1, rights[1])
    last_y = over_y(0, rights[1])
    lefts[2] = along(left_sends, 2, rights[3])
    rights[2] = swap(rights[3], "seq", groups, 1)
    last_x = over_x(3, *last_x)
    last_y = over_y(1, *last_y)
    last_y = over_y(3, *last_y)
    over_x(2, lefts[3], *last_x)
    over_y(2, *last_y)
    cored, cored_too = {}, {}
    for dz in (0, 1, 3, 2):
        behind = (shared[3], lefts[2]) if dz == 2 else (rights[3], lefts[3])
        cored[dz] = swap(after(rights[dz], behind[0]), "row", rows, 1)
        cored_too[dz] = [swap(after(value, behind[1]), "row", rows, 1) for value in crossed[dz]]

    data, right_places = [], []
    for dz in range(groups):
        values = [rights[dz], cored[dz]]
        for pair in zip(crossed[dz], cored_too[dz]):
            values += pair
        right_places.append(list(range(len(data), len(data) + len(values))))
        data += values
    first_lefts = [lefts[dz] for dz in range(groups)]
    last_lefts = [value for dz in range(groups) for value in shared[dz]]

    weight = proj_weight.reshape(channels, rows, e1, 2, pair_channels)
    weight = weight.transpose(1, 3, 4, 2, 0)
    weight = jnp.stack([pick(weight, row ^ m) for m in range(rows)], axis=2)
    weight = weight.reshape(2 * pair_channels, channels * channels // 2)

    place = jnp.stack([core, z_low, col, z_high]).astype(jnp.int32)
    vmem = pl.BlockSpec(memory_space=pltpu.VMEM)
    smem = pl.BlockSpec(memory_space=pltpu.SMEM)
    params = pltpu.CompilerParams(vmem_limit_bytes=40 * 1024 * 1024)
    scale = 1.0 / (group_len * groups)
    bias = jnp.broadcast_to(proj_bias[:, None], (pair_channels, 2 * half))
    share = share_rows // channels

    def update_call(last, left_values, extra, out_shape, out_specs, scratch):
        row_count = share * len(left_values) // groups
        outer_size = row_count * channels * channels * half
        places = (len(left_values), right_places, share_rows, source_rows, group_len, run)
        return pl.pallas_call(
            functools.partial(update_kernel, places, cols, low, last, scale),
            out_shape=out_shape,
            in_specs=[smem] + [vmem] * (len(left_values) + len(data) + 2 + len(extra)),
            out_specs=out_specs,
            scratch_shapes=[
                pltpu.VMEM((row_count * channels, groups * group_len), bf16),
                pltpu.VMEM((row_count, channels * channels // 2, 2 * half), bf16),
            ]
            + scratch,
            compiler_params=params,
            cost_estimate=pl.CostEstimate(
                flops=2 * outer_size * (groups * group_len + 2 * pair_channels),
                bytes_accessed=2 * outer_size,
                transcendentals=0,
            ),
            name="update_last" if last else "update_first",
        )(place, *left_values, *data, bias, weight, *extra)

    first = update_call(
        False, first_lefts, [], jax.ShapeDtypeStruct((share, half, pair_channels), bf16), vmem, []
    )
    outs = update_call(
        True,
        last_lefts,
        [first],
        [jax.ShapeDtypeStruct((run, half, pair_channels), bf16)] * 2
        + [jax.ShapeDtypeStruct((2 * run, run, pair_channels), bf16)] * (2 * low),
        [vmem] * (2 + 2 * low),
        [pltpu.VMEM((2 * run, half, pair_channels), bf16)],
    )

    update_other = swap(outs[1], "seq", groups, low)
    mirrors = []
    for dz in range(low):
        for flip in range(2):
            pairs = []
            for r in range(rows):
                for c in range(cols):
                    for q in range(groups):
                        source = (r * cols + c) * groups + q
                        target = 2 * c + (r % 2 ^ flip)
                        target = (target * cols + r // 2) * groups + (q ^ dz)
                        pairs.append((source, target))
            mirrors.append(lax.ppermute(outs[2 + 2 * dz + flip], axes, pairs))

    vectors = jnp.concatenate([norm_gain, down_bias, up_bias]).reshape(1, -1)
    cell = jnp.arange(run * run)
    mirror_cell = cell % run * run + cell // run
    swap_cells = (mirror_cell[:, None] == cell[None, :]).astype(bf16)
    anywhere = pl.BlockSpec(memory_space=pl.ANY)
    result = None
    for dz in range(low):
        operands = [
            place,
            pair_rep,
            outs[0],
            update_other,
            mirrors[2 * dz],
            mirrors[2 * dz + 1],
            up_weight,
            down_weight,
            vectors,
            swap_cells,
        ]
        extra = [] if result is None else [result]
        result = pl.pallas_call(
            functools.partial(finish_kernel, low, dz),
            out_shape=jax.ShapeDtypeStruct(pair_rep.shape, bf16),
            in_specs=[smem] + [vmem] * 9 + [anywhere] * len(extra),
            out_specs=anywhere,
            scratch_shapes=[
                pltpu.VMEM((4 * run * run, pair_channels), bf16),
                pltpu.VMEM((4, run, run, pair_channels), bf16),
                pltpu.SemaphoreType.DMA((4,)),
            ],
            input_output_aliases={10: 0} if extra else {},
            compiler_params=params,
            name="finish",
        )(*operands, *extra)
    return result


def solution(mesh):
    in_specs = (
        P("seq", None, "row"),
        P("seq", "row", "col"),
        P(),
        P(),
        P(("row", "seq"), "col", None),
        P(),
        P(),
        P(),
        P(),
        P(),
    )
    out_specs = P(("row", "seq"), "col", None)
    return jax.shard_map(
        on_device, mesh=mesh, in_specs=in_specs, out_specs=out_specs, check_vma=False
    )
```

```python
import functools

import jax
import jax.numpy as jnp
from jax import lax
from jax.experimental import pallas as pl
from jax.experimental.pallas import tpu as pltpu
from jax.sharding import PartitionSpec as P

epsilon = 1e-05
axes = ("row", "col", "seq")


def update_kernel(places, shares, low, last, scale, *refs):
    left_count, right_places, share_rows, source_rows, group_len, run = places
    groups = len(right_places)
    sources = len(right_places[0])
    refs = list(refs)
    place_ref = refs.pop(0)
    left_refs = [refs.pop(0) for _ in range(left_count)]
    data_refs = [refs.pop(0) for _ in range(groups * sources)]
    bias_ref, weight_ref = refs.pop(0), refs.pop(0)
    first_ref = refs.pop(0) if last else None
    update_ref = refs.pop() if last else refs[0]
    outer_ref = refs.pop()
    lhs_ref = refs.pop()
    out_refs = refs
    row_count, _, lanes = outer_ref.shape
    blocks = left_count // groups
    channels = share_rows * blocks // row_count
    share = share_rows // channels
    per = source_rows // group_len
    half = lanes // 2
    pair_channels = weight_ref.shape[0] // 2
    lane_low = lax.broadcasted_iota(jnp.int32, (pair_channels, lanes), 1) < half
    for block in range(blocks):
        for dz in range(groups):
            lhs_ref[
                block * share_rows : (block + 1) * share_rows,
                dz * group_len : (dz + 1) * group_len,
            ] = left_refs[dz * blocks + block][...]

    def right_tile(item):
        source, rest = divmod(item, per)
        tiles = []
        for dz in range(groups):
            first = rest * group_len
            tiles.append(data_refs[right_places[dz][source]][first : first + group_len])
        return jnp.concatenate(tiles, axis=0)

    for pair in range(sources * per // 2):
        right = jnp.concatenate([right_tile(2 * pair), right_tile(2 * pair + 1)], axis=1)
        outer = jnp.dot(lhs_ref[...], right, preferred_element_type=jnp.float32)
        outer = outer.astype(jnp.bfloat16)
        for part in range(2):
            item = 2 * pair + part
            outer_ref[:, item * channels : (item + 1) * channels, :] = outer[
                :, part * lanes : (part + 1) * lanes
            ].reshape(row_count, channels, lanes)

    unroll = min(4, row_count // 2)

    @pl.loop(0, row_count // (2 * unroll))
    def _(step):
        for two in range(unroll):
            index = step * unroll + two
            both = jnp.concatenate([outer_ref[2 * index], outer_ref[2 * index + 1]], axis=1)
            proj = jnp.dot(weight_ref[...], both, preferred_element_type=jnp.float32)
            a0 = proj[:pair_channels, :lanes]
            a1 = proj[:pair_channels, lanes:]
            b0 = proj[pair_channels:, :lanes]
            b1 = proj[pair_channels:, lanes:]
            cell = jnp.where(lane_low, a0, b1) + pltpu.roll(
                jnp.where(lane_low, a1, b0), half, 1
            )
            cell = (cell * scale + bias_ref[...]).astype(jnp.bfloat16)
            begin = 2 * index
            if last:
                begin = (place_ref[2] ^ (1 + begin // share)) * share + begin % share
            update_ref[pl.ds(begin, 2)] = cell.T.reshape(2, half, pair_channels)

    if last:
        update_ref[pl.ds(place_ref[2] * share, share)] = first_ref[...]
        core, z_low, z_high = place_ref[0], place_ref[1], place_ref[3]
        out_refs[0][...] = update_ref[pl.ds(z_high * run, run)]
        out_refs[1][...] = update_ref[pl.ds((1 - z_high) * run, run)]
        for dz in range(low):
            for flip in range(2):
                begin = (core ^ flip) * (half // 2) + (z_low ^ dz) * run
                out_refs[2 + 2 * dz + flip][...] = update_ref[
                    :, pl.ds(pl.multiple_of(begin, run), run), :
                ]


def finish_kernel(low, other, *refs):
    place_ref, pair_ref, direct_ref = refs[:3]
    mirror_refs = refs[3 : 3 + 2 * low]
    up_ref, down_ref, vector_ref, swap_ref = refs[3 + 2 * low : 7 + 2 * low]
    out_ref, done_ref, sems = refs[-3:]
    run, columns, pair_channels = pair_ref.shape
    half = columns // 2
    core, z_low, part = place_ref[0], place_ref[1], place_ref[3] ^ other
    cells = run * run
    gain = vector_ref[:, :pair_channels]
    down_bias = vector_ref[:, pair_channels : 2 * pair_channels]
    up_bias = vector_ref[:, 2 * pair_channels :]
    ones = jnp.full((2 * pair_channels, pair_channels), 1.0 / pair_channels, jnp.bfloat16)
    copies = []
    for dz in range(low):
        middles = []
        begins = []
        for flip in range(2):
            local = (core ^ flip) * (half // 2) + (z_low ^ dz) * run
            local = pl.multiple_of(local, run)
            begin = (core ^ flip) * half + (part * low + (z_low ^ dz)) * run
            begin = pl.multiple_of(begin, run)
            begins.append(begin)
            piece = mirror_refs[2 * dz + flip][pl.ds(part * run, run)]
            mirrored = jnp.dot(
                swap_ref[...],
                piece.reshape(cells, pair_channels),
                preferred_element_type=jnp.float32,
            )
            direct = direct_ref[:, pl.ds(local, run), :].reshape(cells, pair_channels)
            residual = pair_ref[:, pl.ds(begin, run), :].reshape(cells, pair_channels)
            middles.append(
                (
                    residual.astype(jnp.float32) + 0.5 * (direct.astype(jnp.float32) + mirrored)
                ).astype(jnp.bfloat16)
            )
        middle = jnp.concatenate(middles, axis=0)
        values = middle.astype(jnp.float32)
        center = jnp.dot(middle, ones[:pair_channels], preferred_element_type=jnp.float32)
        moved = values - center
        square = jnp.square(moved)
        high = square.astype(jnp.bfloat16)
        rest = (square - high.astype(jnp.float32)).astype(jnp.bfloat16)
        spread = jnp.dot(
            jnp.concatenate([high, rest], axis=1), ones, preferred_element_type=jnp.float32
        )
        normed = moved * lax.rsqrt(spread + epsilon) * gain
        hidden = jnp.dot(
            normed.astype(jnp.bfloat16), up_ref[...], preferred_element_type=jnp.float32
        )
        hidden = jnp.maximum(hidden + up_bias, 0.0).astype(jnp.bfloat16)
        result = jnp.dot(hidden, down_ref[...], preferred_element_type=jnp.float32)
        result = (values + result + down_bias).astype(jnp.bfloat16)
        for flip in range(2):
            index = 2 * dz + flip
            done_ref[index] = result[flip * cells : (flip + 1) * cells].reshape(
                run, run, pair_channels
            )
            copy = pltpu.make_async_copy(
                done_ref.at[index], out_ref.at[:, pl.ds(begins[flip], run), :], sems.at[index]
            )
            copy.start()
            copies.append(copy)
    for copy in copies:
        copy.wait()


def on_device(
    left_piece,
    right_piece,
    proj_weight,
    proj_bias,
    pair_rep,
    norm_gain,
    up_weight,
    up_bias,
    down_weight,
    down_bias,
):
    rows = lax.axis_size("row")
    cols = lax.axis_size("col")
    groups = lax.axis_size("seq")
    xs = rows // 2
    low = groups // 2
    row, col, seq = (lax.axis_index(name) for name in axes)
    core, z_low, z_high = row % 2, seq % low, seq // low
    run, columns, pair_channels = pair_rep.shape
    group_len, channels, _ = left_piece.shape
    e1 = right_piece.shape[1] // 2
    half = columns // 2
    bf16 = jnp.bfloat16

    def pick(value, index, axis=0):
        return lax.dynamic_index_in_dim(value, index, axis, False)

    def swap(value, name, size, flip):
        return lax.ppermute(value, name, [(i, i ^ flip) for i in range(size)])

    right = right_piece.reshape(group_len, e1, 2, 2, 2, half // 2).transpose(4, 1, 0, 2, 3, 5)
    source_rows = e1 * group_len
    right = right.reshape(2, source_rows, 2 * half)
    share_rows = 2 * run // cols * channels
    left = left_piece.transpose(2, 1, 0).reshape(2, low, run, channels, group_len)
    left = left.transpose(1, 0, 2, 3, 4).reshape(low, cols, share_rows, group_len)
    left = pick(left, col, 1)

    def after(value, *earlier):
        return lax.optimization_barrier((value, earlier))[0] if earlier else value

    mine, theirs = lax.optimization_barrier((pick(right, z_high), pick(right, 1 - z_high)))
    left_sends = [pick(left, z_low ^ (dz % low)) for dz in range(groups)]
    right_sends = [theirs if dz >= low else mine for dz in range(groups)]
    rights, lefts = {0: right_sends[0]}, {0: left_sends[0]}
    crossed = {dz: [] for dz in range(groups)}
    shared = {dz: [] for dz in range(groups)}

    def along(sends, dz, *earlier):
        return swap(after(sends[dz], *earlier), "seq", groups, dz)

    def over_x(dz, *earlier):
        for dx in range(1, xs):
            value = swap(after(rights[dz], *earlier), "row", rows, 2 * dx)
            crossed[dz].append(value)
            earlier = (value,)
        return earlier

    def over_y(dz, *earlier):
        for dy in range(1, cols):
            value = swap(after(lefts[dz], *earlier), "col", cols, dy)
            shared[dz].append(value)
            earlier = (value,)
        return earlier

    rights[3] = along(right_sends, 3)
    rights[1] = along(right_sends, 1)
    last_x = over_x(0)
    last_x = over_x(1, *last_x)
    lefts[3] = along(left_sends, 3, rights[1])
    last_y = over_y(0)
    lefts[1] = along(left_sends, 1, *last_y)
    lefts[2] = along(left_sends, 2, rights[3])
    rights[2] = swap(rights[3], "seq", groups, 1)
    last_x = over_x(3, *last_x)
    last_y = over_y(1, *last_y)
    last_y = over_y(3, *last_y)
    over_x(2, lefts[3], *last_x)
    over_y(2, *last_y)
    cored, cored_too = {}, {}
    for dz in (0, 1, 3, 2):
        behind = (shared[3], lefts[2]) if dz == 2 else (rights[3], lefts[3])
        cored[dz] = swap(after(rights[dz], behind[0]), "row", rows, 1)
        cored_too[dz] = [swap(after(value, behind[1]), "row", rows, 1) for value in crossed[dz]]

    data, right_places = [], []
    for dz in range(groups):
        values = [rights[dz], cored[dz]]
        for pair in zip(crossed[dz], cored_too[dz]):
            values += pair
        right_places.append(list(range(len(data), len(data) + len(values))))
        data += values
    first_lefts = [lefts[dz] for dz in range(groups)]
    last_lefts = [value for dz in range(groups) for value in shared[dz]]

    weight = proj_weight.reshape(channels, rows, e1, 2, pair_channels)
    weight = weight.transpose(1, 3, 4, 2, 0)
    weight = jnp.stack([pick(weight, row ^ m) for m in range(rows)], axis=2)
    weight = weight.reshape(2 * pair_channels, channels * channels // 2)

    place = jnp.stack([core, z_low, col, z_high]).astype(jnp.int32)
    vmem = pl.BlockSpec(memory_space=pltpu.VMEM)
    smem = pl.BlockSpec(memory_space=pltpu.SMEM)
    params = pltpu.CompilerParams(vmem_limit_bytes=40 * 1024 * 1024)
    scale = 1.0 / (group_len * groups)
    bias = jnp.broadcast_to(proj_bias[:, None], (pair_channels, 2 * half))
    share = share_rows // channels

    def update_call(last, left_values, extra, out_shape, out_specs, scratch):
        row_count = share * len(left_values) // groups
        outer_size = row_count * channels * channels * half
        places = (len(left_values), right_places, share_rows, source_rows, group_len, run)
        return pl.pallas_call(
            functools.partial(update_kernel, places, cols, low, last, scale),
            out_shape=out_shape,
            in_specs=[smem] + [vmem] * (len(left_values) + len(data) + 2 + len(extra)),
            out_specs=out_specs,
            scratch_shapes=[
                pltpu.VMEM((row_count * channels, groups * group_len), bf16),
                pltpu.VMEM((row_count, channels * channels // 2, 2 * half), bf16),
            ]
            + scratch,
            compiler_params=params,
            cost_estimate=pl.CostEstimate(
                flops=2 * outer_size * (groups * group_len + 2 * pair_channels),
                bytes_accessed=2 * outer_size,
                transcendentals=0,
            ),
            name="update_last" if last else "update_first",
        )(place, *left_values, *data, bias, weight, *extra)

    first = update_call(
        False, first_lefts, [], jax.ShapeDtypeStruct((share, half, pair_channels), bf16), vmem, []
    )
    outs = update_call(
        True,
        last_lefts,
        [first],
        [jax.ShapeDtypeStruct((run, half, pair_channels), bf16)] * 2
        + [jax.ShapeDtypeStruct((2 * run, run, pair_channels), bf16)] * (2 * low),
        [vmem] * (2 + 2 * low),
        [pltpu.VMEM((2 * run, half, pair_channels), bf16)],
    )

    mirrors = []
    for dz in range(low):
        for flip in range(2):
            pairs = []
            for r in range(rows):
                for c in range(cols):
                    for q in range(groups):
                        source = (r * cols + c) * groups + q
                        target = 2 * c + (r % 2 ^ flip)
                        target = (target * cols + r // 2) * groups + (q ^ dz)
                        pairs.append((source, target))
            mirrors.append(lax.ppermute(outs[2 + 2 * dz + flip], axes, pairs))
    update_other = swap(outs[1], "seq", groups, low)

    vectors = jnp.concatenate([norm_gain, down_bias, up_bias]).reshape(1, -1)
    cell = jnp.arange(run * run)
    mirror_cell = cell % run * run + cell // run
    swap_cells = (mirror_cell[:, None] == cell[None, :]).astype(bf16)
    anywhere = pl.BlockSpec(memory_space=pl.ANY)
    result = None
    for other in range(2):
        operands = [
            place,
            pair_rep,
            update_other if other else outs[0],
            *mirrors,
            up_weight,
            down_weight,
            vectors,
            swap_cells,
        ]
        extra = [] if result is None else [result]
        result = pl.pallas_call(
            functools.partial(finish_kernel, low, other),
            out_shape=jax.ShapeDtypeStruct(pair_rep.shape, bf16),
            in_specs=[smem] + [vmem] * (len(operands) - 1) + [anywhere] * len(extra),
            out_specs=anywhere,
            scratch_shapes=[
                pltpu.VMEM((2 * low, run, run, pair_channels), bf16),
                pltpu.SemaphoreType.DMA((2 * low,)),
            ],
            input_output_aliases={len(operands): 0} if extra else {},
            compiler_params=params,
            cost_estimate=pl.CostEstimate(
                flops=64 * run * columns * pair_channels * up_bias.size,
                bytes_accessed=2 * pair_rep.size,
                transcendentals=0,
            ),
            name="finish",
        )(*operands, *extra)
    return result


def solution(mesh):
    in_specs = (
        P("seq", None, "row"),
        P("seq", "row", "col"),
        P(),
        P(),
        P(("row", "seq"), "col", None),
        P(),
        P(),
        P(),
        P(),
        P(),
    )
    out_specs = P(("row", "seq"), "col", None)
    return jax.shard_map(
        on_device, mesh=mesh, in_specs=in_specs, out_specs=out_specs, check_vma=False
    )
```

```python
import functools

import jax
import jax.numpy as jnp
from jax import lax
from jax.experimental import pallas as pl
from jax.experimental.pallas import tpu as pltpu
from jax.sharding import PartitionSpec as P

epsilon = 1e-05
axes = ("row", "col", "seq")


def update_kernel(places, shares, low, last, scale, *refs):
    blocks, data_count, right_places, share_rows, source_rows, group_len, run = places
    groups = len(right_places)
    sources = len(right_places[0])
    refs = list(refs)
    place_ref = refs.pop(0)
    left_refs = [refs.pop(0) for _ in range(2 * blocks if last else 1)]
    data_refs = [refs.pop(0) for _ in range(data_count)]
    bias_ref, weight_ref = refs.pop(0), refs.pop(0)
    first_ref = refs.pop(0) if last else None
    update_ref = refs.pop() if last else refs[0]
    outer_ref = refs.pop()
    lhs_ref = refs.pop() if last else left_refs[0]
    out_refs = refs
    row_count, _, lanes = outer_ref.shape
    low = groups // 2
    channels = share_rows * blocks // row_count
    share = share_rows // channels
    per = source_rows // group_len
    half = lanes // 2
    pair_channels = weight_ref.shape[0] // 2
    lane_low = lax.broadcasted_iota(jnp.int32, (pair_channels, lanes), 1) < half
    for block in range(blocks if last else 0):
        for dz in range(groups):
            lhs_ref[
                block * share_rows : (block + 1) * share_rows,
                dz * group_len : (dz + 1) * group_len,
            ] = left_refs[2 * block + dz // low][
                dz % low * share_rows : (dz % low + 1) * share_rows
            ]

    def right_tile(item):
        source, rest = divmod(item, per)
        tiles = []
        for dz in range(groups):
            operand, first = right_places[dz][source]
            first += rest * group_len
            tiles.append(data_refs[operand][first : first + group_len])
        return jnp.concatenate(tiles, axis=0)

    for pair in range(sources * per // 2):
        right = jnp.concatenate([right_tile(2 * pair), right_tile(2 * pair + 1)], axis=1)
        outer = jnp.dot(lhs_ref[...], right, preferred_element_type=jnp.float32)
        outer = outer.astype(jnp.bfloat16)
        for part in range(2):
            item = 2 * pair + part
            outer_ref[:, item * channels : (item + 1) * channels, :] = outer[
                :, part * lanes : (part + 1) * lanes
            ].reshape(row_count, channels, lanes)

    unroll = min(4, row_count // 2)

    @pl.loop(0, row_count // (2 * unroll))
    def _(step):
        for two in range(unroll):
            index = step * unroll + two
            both = jnp.concatenate([outer_ref[2 * index], outer_ref[2 * index + 1]], axis=1)
            proj = jnp.dot(weight_ref[...], both, preferred_element_type=jnp.float32)
            a0 = proj[:pair_channels, :lanes]
            a1 = proj[:pair_channels, lanes:]
            b0 = proj[pair_channels:, :lanes]
            b1 = proj[pair_channels:, lanes:]
            cell = jnp.where(lane_low, a0, b1) + pltpu.roll(
                jnp.where(lane_low, a1, b0), half, 1
            )
            cell = (cell * scale + bias_ref[...]).astype(jnp.bfloat16)
            begin = 2 * index
            if last:
                begin = (place_ref[2] ^ (1 + begin // share)) * share + begin % share
            update_ref[pl.ds(begin, 2)] = cell.T.reshape(2, half, pair_channels)

    if last:
        update_ref[pl.ds(place_ref[2] * share, share)] = first_ref[...]
        core, z_low, z_high = place_ref[0], place_ref[1], place_ref[3]
        out_refs[0][...] = update_ref[pl.ds(z_high * run, run)]
        out_refs[1][...] = update_ref[pl.ds((1 - z_high) * run, run)]
        for dz in range(low):
            for flip in range(2):
                begin = (core ^ flip) * (half // 2) + (z_low ^ dz) * run
                out_refs[2 + 2 * dz + flip][...] = update_ref[
                    :, pl.ds(pl.multiple_of(begin, run), run), :
                ]


def pack_kernel(first_ref, second_ref, out_ref):
    rows = first_ref.shape[0]
    out_ref[:rows] = first_ref[...]
    out_ref[rows:] = second_ref[...]


def pack(first, second):
    rows, lanes = first.shape
    return pl.pallas_call(
        pack_kernel,
        out_shape=jax.ShapeDtypeStruct((2 * rows, lanes), first.dtype),
        in_specs=[pl.BlockSpec(memory_space=pltpu.VMEM)] * 2,
        out_specs=pl.BlockSpec(memory_space=pltpu.VMEM),
        name="pack",
    )(first, second)


def arrange_kernel(near_ref, far_ref, out_ref):
    rows, lanes = out_ref.shape[0], near_ref.shape[1]
    count = near_ref.shape[0] // rows
    for index in range(2 * count):
        ref = near_ref if index < count else far_ref
        begin = index % count * rows
        out_ref[:, index * lanes : (index + 1) * lanes] = ref[begin : begin + rows]


def arrange(lefts, groups):
    rows, lanes = lefts[0].shape
    rows //= groups // 2
    return pl.pallas_call(
        arrange_kernel,
        out_shape=jax.ShapeDtypeStruct((rows, groups * lanes), lefts[0].dtype),
        in_specs=[pl.BlockSpec(memory_space=pltpu.VMEM)] * 2,
        out_specs=pl.BlockSpec(memory_space=pltpu.VMEM),
        cost_estimate=pl.CostEstimate(
            flops=rows * groups * lanes * 8 * lanes * groups * 4,
            bytes_accessed=4 * rows * groups * lanes,
            transcendentals=0,
        ),
        name="arrange",
    )(*lefts)


def finish_kernel(low, other, *refs):
    place_ref, pair_ref, direct_ref = refs[:3]
    mirror_refs = refs[3 : 3 + 2 * low]
    up_ref, down_ref, vector_ref, swap_ref = refs[3 + 2 * low : 7 + 2 * low]
    out_ref, done_ref, sems = refs[-3:]
    run, columns, pair_channels = pair_ref.shape
    half = columns // 2
    core, z_low, part = place_ref[0], place_ref[1], place_ref[3] ^ other
    cells = run * run
    gain = vector_ref[:, :pair_channels]
    down_bias = vector_ref[:, pair_channels : 2 * pair_channels]
    up_bias = vector_ref[:, 2 * pair_channels :]
    ones = jnp.full((2 * pair_channels, pair_channels), 1.0 / pair_channels, jnp.bfloat16)
    copies = []
    for dz in range(low):
        middles = []
        begins = []
        for flip in range(2):
            local = (core ^ flip) * (half // 2) + (z_low ^ dz) * run
            local = pl.multiple_of(local, run)
            begin = (core ^ flip) * half + (part * low + (z_low ^ dz)) * run
            begin = pl.multiple_of(begin, run)
            begins.append(begin)
            piece = mirror_refs[2 * dz + flip][pl.ds(part * run, run)]
            mirrored = jnp.dot(
                swap_ref[...],
                piece.reshape(cells, pair_channels),
                preferred_element_type=jnp.float32,
            )
            direct = direct_ref[:, pl.ds(local, run), :].reshape(cells, pair_channels)
            residual = pair_ref[:, pl.ds(begin, run), :].reshape(cells, pair_channels)
            middles.append(
                (
                    residual.astype(jnp.float32) + 0.5 * (direct.astype(jnp.float32) + mirrored)
                ).astype(jnp.bfloat16)
            )
        middle = jnp.concatenate(middles, axis=0)
        values = middle.astype(jnp.float32)
        center = jnp.dot(middle, ones[:pair_channels], preferred_element_type=jnp.float32)
        moved = values - center
        square = jnp.square(moved)
        high = square.astype(jnp.bfloat16)
        rest = (square - high.astype(jnp.float32)).astype(jnp.bfloat16)
        spread = jnp.dot(
            jnp.concatenate([high, rest], axis=1), ones, preferred_element_type=jnp.float32
        )
        normed = moved * lax.rsqrt(spread + epsilon) * gain
        hidden = jnp.dot(
            normed.astype(jnp.bfloat16), up_ref[...], preferred_element_type=jnp.float32
        )
        hidden = jnp.maximum(hidden + up_bias, 0.0).astype(jnp.bfloat16)
        result = jnp.dot(hidden, down_ref[...], preferred_element_type=jnp.float32)
        result = (values + result + down_bias).astype(jnp.bfloat16)
        for flip in range(2):
            index = 2 * dz + flip
            done_ref[index] = result[flip * cells : (flip + 1) * cells].reshape(
                run, run, pair_channels
            )
            copy = pltpu.make_async_copy(
                done_ref.at[index], out_ref.at[:, pl.ds(begins[flip], run), :], sems.at[index]
            )
            copy.start()
            copies.append(copy)
    for copy in copies:
        copy.wait()


def on_device(
    left_piece,
    right_piece,
    proj_weight,
    proj_bias,
    pair_rep,
    norm_gain,
    up_weight,
    up_bias,
    down_weight,
    down_bias,
):
    rows = lax.axis_size("row")
    cols = lax.axis_size("col")
    groups = lax.axis_size("seq")
    xs = rows // 2
    low = groups // 2
    row, col, seq = (lax.axis_index(name) for name in axes)
    core, z_low, z_high = row % 2, seq % low, seq // low
    run, columns, pair_channels = pair_rep.shape
    group_len, channels, _ = left_piece.shape
    e1 = right_piece.shape[1] // 2
    half = columns // 2
    bf16 = jnp.bfloat16

    def pick(value, index, axis=0):
        return lax.dynamic_index_in_dim(value, index, axis, False)

    def swap(value, name, size, flip):
        return lax.ppermute(value, name, [(i, i ^ flip) for i in range(size)])

    right = right_piece.reshape(group_len, e1, 2, 2, 2, half // 2).transpose(4, 1, 0, 2, 3, 5)
    source_rows = e1 * group_len
    right = right.reshape(2, source_rows, 2 * half)
    share_rows = 2 * run // cols * channels
    left = left_piece.transpose(2, 1, 0).reshape(2, low, run, channels, group_len)
    left = left.transpose(1, 0, 2, 3, 4).reshape(low, cols, share_rows, group_len)
    left = pick(left, col, 1)

    def after(value, *earlier):
        return lax.optimization_barrier((value, earlier))[0] if earlier else value

    mine, theirs = pick(right, z_high), pick(right, 1 - z_high)
    own, crossing = pick(left, z_low), pick(left, 1 - z_low)
    far = swap(theirs, "seq", groups, low)
    near = swap(crossing, "seq", groups, 1)
    lefts = [pack(own, near)]
    lefts.append(swap(lefts[0], "seq", groups, low))
    rights = [pack(mine, after(far, lefts[0]))]
    rights.append(swap(rights[0], "seq", groups, 1))
    shares = [[swap(lefts[0], "col", cols, dy)] for dy in range(1, cols)]
    data = []
    right_places = {dz: [] for dz in range(groups)}

    def hold(values, pair):
        for position, dz in enumerate(pair):
            value = values[position] if len(values) > 1 else values[0]
            if not any(value is item for item in data):
                data.append(value)
            index = next(i for i, item in enumerate(data) if item is value)
            right_places[dz].append((index, position * source_rows if len(values) == 1 else 0))

    near_pair, far_pair = (0, low), (1, low + 1)
    near_crosses = [swap(rights[0], "row", rows, 2 * dx) for dx in range(1, xs)]
    far_crosses = [swap(rights[1], "row", rows, 2 * dx) for dx in range(1, xs)]
    for cross in [rights[0]] + near_crosses:
        hold([cross], near_pair)
        hold([swap(cross, "row", rows, 1)], near_pair)
    hold([rights[1]], far_pair)
    first_lhs = arrange(lefts, groups)
    exchanged = swap(after(rights[1], shares), "row", rows, 1)
    hold([exchanged], far_pair)
    for cross in far_crosses:
        hold([cross], far_pair)
        hold([swap(after(cross, exchanged, first_lhs), "row", rows, 1)], far_pair)
    for dy in range(1, cols):
        shares[dy - 1].append(swap(lefts[1], "col", cols, dy))
    right_places = [right_places[dz] for dz in range(groups)]
    last_lefts = [value for pair in shares for value in pair]

    weight = proj_weight.reshape(channels, rows, e1, 2, pair_channels)
    weight = weight.transpose(1, 3, 4, 2, 0)
    weight = jnp.stack([pick(weight, row ^ m) for m in range(rows)], axis=2)
    weight = weight.reshape(2 * pair_channels, channels * channels // 2)

    place = jnp.stack([core, z_low, col, z_high]).astype(jnp.int32)
    vmem = pl.BlockSpec(memory_space=pltpu.VMEM)
    smem = pl.BlockSpec(memory_space=pltpu.SMEM)
    params = pltpu.CompilerParams(vmem_limit_bytes=40 * 1024 * 1024)
    scale = 1.0 / (group_len * groups)
    bias = jnp.broadcast_to(proj_bias[:, None], (pair_channels, 2 * half))
    share = share_rows // channels

    def update_call(last, left_values, extra, out_shape, out_specs, scratch):
        blocks = max(len(left_values) // 2, 1)
        row_count = share * blocks
        outer_size = row_count * channels * channels * half
        places = (blocks, len(data), right_places, share_rows, source_rows, group_len, run)
        return pl.pallas_call(
            functools.partial(update_kernel, places, cols, low, last, scale),
            out_shape=out_shape,
            in_specs=[smem] + [vmem] * (len(left_values) + len(data) + 2 + len(extra)),
            out_specs=out_specs,
            scratch_shapes=scratch[:-1]
            + [
                pltpu.VMEM((row_count, channels * channels // 2, 2 * half), bf16),
            ]
            + scratch[-1:],
            compiler_params=params,
            cost_estimate=pl.CostEstimate(
                flops=2 * outer_size * (groups * group_len + 2 * pair_channels),
                bytes_accessed=2 * outer_size,
                transcendentals=0,
            ),
            name="update_last" if last else "update_first",
        )(place, *left_values, *data, bias, weight, *extra)

    first = update_call(
        False, [first_lhs], [], jax.ShapeDtypeStruct((share, half, pair_channels), bf16), vmem, []
    )
    outs = update_call(
        True,
        last_lefts,
        [first],
        [jax.ShapeDtypeStruct((run, half, pair_channels), bf16)] * 2
        + [jax.ShapeDtypeStruct((2 * run, run, pair_channels), bf16)] * (2 * low),
        [vmem] * (2 + 2 * low),
        [
            pltpu.VMEM(((2 * run - share) * channels, groups * group_len), bf16),
            pltpu.VMEM((2 * run, half, pair_channels), bf16),
        ],
    )

    mirrors = []
    for dz in range(low):
        for flip in range(2):
            pairs = []
            for r in range(rows):
                for c in range(cols):
                    for q in range(groups):
                        source = (r * cols + c) * groups + q
                        target = 2 * c + (r % 2 ^ flip)
                        target = (target * cols + r // 2) * groups + (q ^ dz)
                        pairs.append((source, target))
            mirrors.append(lax.ppermute(outs[2 + 2 * dz + flip], axes, pairs))
    update_other = swap(outs[1], "seq", groups, low)

    vectors = jnp.concatenate([norm_gain, down_bias, up_bias]).reshape(1, -1)
    cell = jnp.arange(run * run)
    mirror_cell = cell % run * run + cell // run
    swap_cells = (mirror_cell[:, None] == cell[None, :]).astype(bf16)
    anywhere = pl.BlockSpec(memory_space=pl.ANY)
    result = None
    for other in range(2):
        operands = [
            place,
            pair_rep,
            update_other if other else outs[0],
            *mirrors,
            up_weight,
            down_weight,
            vectors,
            swap_cells,
        ]
        extra = [] if result is None else [result]
        result = pl.pallas_call(
            functools.partial(finish_kernel, low, other),
            out_shape=jax.ShapeDtypeStruct(pair_rep.shape, bf16),
            in_specs=[smem] + [vmem] * (len(operands) - 1) + [anywhere] * len(extra),
            out_specs=anywhere,
            scratch_shapes=[
                pltpu.VMEM((2 * low, run, run, pair_channels), bf16),
                pltpu.SemaphoreType.DMA((2 * low,)),
            ],
            input_output_aliases={len(operands): 0} if extra else {},
            compiler_params=params,
            cost_estimate=pl.CostEstimate(
                flops=64 * run * columns * pair_channels * up_bias.size,
                bytes_accessed=2 * pair_rep.size,
                transcendentals=0,
            ),
            name="finish",
        )(*operands, *extra)
    return result


def solution(mesh):
    in_specs = (
        P("seq", None, "row"),
        P("seq", "row", "col"),
        P(),
        P(),
        P(("row", "seq"), "col", None),
        P(),
        P(),
        P(),
        P(),
        P(),
    )
    out_specs = P(("row", "seq"), "col", None)
    return jax.shard_map(
        on_device, mesh=mesh, in_specs=in_specs, out_specs=out_specs, check_vma=False
    )
```

```python
import functools

import jax
import jax.numpy as jnp
from jax import lax
from jax.experimental import pallas as pl
from jax.experimental.pallas import tpu as pltpu
from jax.sharding import PartitionSpec as P

epsilon = 1e-05
axes = ("row", "col", "seq")


def update_kernel(places, shares, low, last, scale, *refs):
    blocks, data_count, right_places, share_rows, source_rows, group_len, run = places
    groups = len(right_places)
    sources = len(right_places[0])
    refs = list(refs)
    place_ref = refs.pop(0)
    left_refs = [refs.pop(0) for _ in range(2 * blocks if last else 1)]
    data_refs = [refs.pop(0) for _ in range(data_count)]
    bias_ref, weight_ref = refs.pop(0), refs.pop(0)
    first_ref = refs.pop(0) if last else None
    update_ref = refs.pop() if last else refs[0]
    outer_ref = refs.pop()
    lhs_ref = refs.pop() if last else left_refs[0]
    out_refs = refs
    row_count, _, lanes = outer_ref.shape
    low = groups // 2
    channels = share_rows * blocks // row_count
    share = share_rows // channels
    per = source_rows // group_len
    half = lanes // 2
    pair_channels = weight_ref.shape[0] // 2
    lane_low = lax.broadcasted_iota(jnp.int32, (pair_channels, lanes), 1) < half
    for block in range(blocks if last else 0):
        for dz in range(groups):
            lhs_ref[
                block * share_rows : (block + 1) * share_rows,
                dz * group_len : (dz + 1) * group_len,
            ] = left_refs[2 * block + dz // low][
                dz % low * share_rows : (dz % low + 1) * share_rows
            ]

    def right_tile(item):
        source, rest = divmod(item, per)
        tiles = []
        for dz in range(groups):
            operand, first = right_places[dz][source]
            first += rest * group_len
            tiles.append(data_refs[operand][first : first + group_len])
        return jnp.concatenate(tiles, axis=0)

    for pair in range(sources * per // 2):
        right = jnp.concatenate([right_tile(2 * pair), right_tile(2 * pair + 1)], axis=1)
        outer = jnp.dot(lhs_ref[...], right, preferred_element_type=jnp.float32)
        outer = outer.astype(jnp.bfloat16)
        for part in range(2):
            item = 2 * pair + part
            outer_ref[:, item * channels : (item + 1) * channels, :] = outer[
                :, part * lanes : (part + 1) * lanes
            ].reshape(row_count, channels, lanes)

    unroll = min(4, row_count // 2)

    @pl.loop(0, row_count // (2 * unroll))
    def _(step):
        for two in range(unroll):
            index = step * unroll + two
            both = jnp.concatenate([outer_ref[2 * index], outer_ref[2 * index + 1]], axis=1)
            proj = jnp.dot(weight_ref[...], both, preferred_element_type=jnp.float32)
            a0 = proj[:pair_channels, :lanes]
            a1 = proj[:pair_channels, lanes:]
            b0 = proj[pair_channels:, :lanes]
            b1 = proj[pair_channels:, lanes:]
            cell = jnp.where(lane_low, a0, b1) + pltpu.roll(
                jnp.where(lane_low, a1, b0), half, 1
            )
            cell = (cell * scale + bias_ref[...]).astype(jnp.bfloat16)
            begin = 2 * index
            if last:
                begin = (place_ref[2] ^ (1 + begin // share)) * share + begin % share
            update_ref[pl.ds(begin, 2)] = cell.T.reshape(2, half, pair_channels)

    if last:
        update_ref[pl.ds(place_ref[2] * share, share)] = first_ref[...]
        core, z_low, z_high = place_ref[0], place_ref[1], place_ref[3]
        out_refs[0][...] = update_ref[pl.ds(z_high * run, run)]
        out_refs[1][...] = update_ref[pl.ds((1 - z_high) * run, run)]
        for dz in range(low):
            for flip in range(2):
                begin = (core ^ flip) * (half // 2) + (z_low ^ dz) * run
                out_refs[2 + 2 * dz + flip][...] = update_ref[
                    :, pl.ds(pl.multiple_of(begin, run), run), :
                ]


def pack_kernel(*refs):
    rows = refs[0].shape[0]
    for index, ref in enumerate(refs[:-1]):
        refs[-1][index * rows : (index + 1) * rows] = ref[...]


def pack(*values):
    rows, lanes = values[0].shape
    return pl.pallas_call(
        pack_kernel,
        out_shape=jax.ShapeDtypeStruct((len(values) * rows, lanes), values[0].dtype),
        in_specs=[pl.BlockSpec(memory_space=pltpu.VMEM)] * len(values),
        out_specs=pl.BlockSpec(memory_space=pltpu.VMEM),
        compiler_params=pltpu.CompilerParams(vmem_limit_bytes=4 * 1024 * 1024),
        name="pack",
    )(*values)


def arrange_kernel(near_ref, far_ref, out_ref):
    rows, lanes = out_ref.shape[0], near_ref.shape[1]
    count = near_ref.shape[0] // rows
    for index in range(2 * count):
        ref = near_ref if index < count else far_ref
        begin = index % count * rows
        out_ref[:, index * lanes : (index + 1) * lanes] = ref[begin : begin + rows]


def arrange(lefts, groups):
    rows, lanes = lefts[0].shape
    rows //= groups // 2
    return pl.pallas_call(
        arrange_kernel,
        out_shape=jax.ShapeDtypeStruct((rows, groups * lanes), lefts[0].dtype),
        in_specs=[pl.BlockSpec(memory_space=pltpu.VMEM)] * 2,
        out_specs=pl.BlockSpec(memory_space=pltpu.VMEM),
        compiler_params=pltpu.CompilerParams(vmem_limit_bytes=4 * 1024 * 1024),
        cost_estimate=pl.CostEstimate(
            flops=rows * groups * lanes * 8 * lanes * groups * 1,
            bytes_accessed=4 * rows * groups * lanes,
            transcendentals=0,
        ),
        name="arrange",
    )(*lefts)


def finish_kernel(low, other, *refs):
    place_ref, pair_ref, direct_ref = refs[:3]
    mirror_refs = refs[3 : 3 + 2 * low]
    up_ref, down_ref, vector_ref, swap_ref = refs[3 + 2 * low : 7 + 2 * low]
    out_ref, done_ref, sems = refs[-3:]
    run, columns, pair_channels = pair_ref.shape
    half = columns // 2
    core, z_low, part = place_ref[0], place_ref[1], place_ref[3] ^ other
    cells = run * run
    gain = vector_ref[:, :pair_channels]
    down_bias = vector_ref[:, pair_channels : 2 * pair_channels]
    up_bias = vector_ref[:, 2 * pair_channels :]
    ones = jnp.full((2 * pair_channels, pair_channels), 1.0 / pair_channels, jnp.bfloat16)
    copies = []
    for dz in range(low):
        middles = []
        begins = []
        for flip in range(2):
            local = (core ^ flip) * (half // 2) + (z_low ^ dz) * run
            local = pl.multiple_of(local, run)
            begin = (core ^ flip) * half + (part * low + (z_low ^ dz)) * run
            begin = pl.multiple_of(begin, run)
            begins.append(begin)
            piece = mirror_refs[2 * dz + flip][pl.ds(part * run, run)]
            mirrored = jnp.dot(
                swap_ref[...],
                piece.reshape(cells, pair_channels),
                preferred_element_type=jnp.float32,
            )
            direct = direct_ref[:, pl.ds(local, run), :].reshape(cells, pair_channels)
            residual = pair_ref[:, pl.ds(begin, run), :].reshape(cells, pair_channels)
            middles.append(
                (
                    residual.astype(jnp.float32) + 0.5 * (direct.astype(jnp.float32) + mirrored)
                ).astype(jnp.bfloat16)
            )
        middle = jnp.concatenate(middles, axis=0)
        values = middle.astype(jnp.float32)
        center = jnp.dot(middle, ones[:pair_channels], preferred_element_type=jnp.float32)
        moved = values - center
        square = jnp.square(moved)
        high = square.astype(jnp.bfloat16)
        rest = (square - high.astype(jnp.float32)).astype(jnp.bfloat16)
        spread = jnp.dot(
            jnp.concatenate([high, rest], axis=1), ones, preferred_element_type=jnp.float32
        )
        normed = moved * lax.rsqrt(spread + epsilon) * gain
        hidden = jnp.dot(
            normed.astype(jnp.bfloat16), up_ref[...], preferred_element_type=jnp.float32
        )
        hidden = jnp.maximum(hidden + up_bias, 0.0).astype(jnp.bfloat16)
        result = jnp.dot(hidden, down_ref[...], preferred_element_type=jnp.float32)
        result = (values + result + down_bias).astype(jnp.bfloat16)
        for flip in range(2):
            index = 2 * dz + flip
            done_ref[index] = result[flip * cells : (flip + 1) * cells].reshape(
                run, run, pair_channels
            )
            copy = pltpu.make_async_copy(
                done_ref.at[index], out_ref.at[:, pl.ds(begins[flip], run), :], sems.at[index]
            )
            copy.start()
            copies.append(copy)
    for copy in copies:
        copy.wait()


def on_device(
    left_piece,
    right_piece,
    proj_weight,
    proj_bias,
    pair_rep,
    norm_gain,
    up_weight,
    up_bias,
    down_weight,
    down_bias,
):
    rows = lax.axis_size("row")
    cols = lax.axis_size("col")
    groups = lax.axis_size("seq")
    xs = rows // 2
    low = groups // 2
    row, col, seq = (lax.axis_index(name) for name in axes)
    core, z_low, z_high = row % 2, seq % low, seq // low
    run, columns, pair_channels = pair_rep.shape
    group_len, channels, _ = left_piece.shape
    e1 = right_piece.shape[1] // 2
    half = columns // 2
    bf16 = jnp.bfloat16

    def pick(value, index, axis=0):
        return lax.dynamic_index_in_dim(value, index, axis, False)

    def swap(value, name, size, flip):
        return lax.ppermute(value, name, [(i, i ^ flip) for i in range(size)])

    right = right_piece.reshape(group_len, e1, 2, 2, 2, half // 2).transpose(4, 1, 0, 2, 3, 5)
    source_rows = e1 * group_len
    right = right.reshape(2, source_rows, 2 * half)
    share_rows = 2 * run // cols * channels
    left = left_piece.transpose(2, 1, 0).reshape(2, low, run, channels, group_len)
    left = left.transpose(1, 0, 2, 3, 4).reshape(low, cols, share_rows, group_len)
    left = pick(left, col, 1)

    def after(value, *earlier):
        return lax.optimization_barrier((value, earlier))[0] if earlier else value

    mine, theirs = pick(right, z_high), pick(right, 1 - z_high)
    own, crossing = pick(left, z_low), pick(left, 1 - z_low)
    near = swap(crossing, "seq", groups, 1)
    blocks = {0: mine}
    blocks[low + 1] = swap(theirs, "seq", groups, low + 1)
    blocks[1] = swap(mine, "seq", groups, 1)
    blocks[low] = swap(blocks[low + 1], "seq", groups, 1)
    lefts = [pack(own, near)]
    lefts.append(swap(lefts[0], "seq", groups, low))
    shares = [[swap(lefts[0], "col", cols, dy)] for dy in range(1, cols)]
    first_lhs = arrange(lefts, groups)
    data = []
    right_places = {dz: [] for dz in range(groups)}
    order = (0, 1, low + 1, low)
    crosses = {dz: [blocks[dz]] for dz in order}
    last = ()
    for dz in order:
        for dx in range(1, xs):
            behind = last + (tuple(map(tuple, shares)) if dz == low else ())
            crosses[dz].append(swap(after(blocks[dz], *behind), "row", rows, 2 * dx))
            last = (crosses[dz][-1],)
    for position in range(xs):
        values = [crosses[dz][position] for dz in order]
        for dz, value in zip(order, values):
            right_places[dz].append((len(data), 0))
            data.append(value)
        count = len(order) if position == 0 else len(order) - 1
        exchanged = swap(pack(*values[:count]), "row", rows, 1)
        for index, dz in enumerate(order[:count]):
            right_places[dz].append((len(data), index * source_rows))
        data.append(exchanged)
        if count < len(order):
            right_places[low].append((len(data), 0))
            data.append(swap(after(values[-1], first_lhs), "row", rows, 1))
    for dy in range(1, cols):
        shares[dy - 1].append(swap(lefts[1], "col", cols, dy))
    right_places = [right_places[dz] for dz in range(groups)]
    last_lefts = [value for pair in shares for value in pair]

    weight = proj_weight.reshape(channels, rows, e1, 2, pair_channels)
    weight = weight.transpose(1, 3, 4, 2, 0)
    weight = jnp.stack([pick(weight, row ^ m) for m in range(rows)], axis=2)
    weight = weight.reshape(2 * pair_channels, channels * channels // 2)

    place = jnp.stack([core, z_low, col, z_high]).astype(jnp.int32)
    vmem = pl.BlockSpec(memory_space=pltpu.VMEM)
    smem = pl.BlockSpec(memory_space=pltpu.SMEM)
    params = pltpu.CompilerParams(vmem_limit_bytes=40 * 1024 * 1024)
    scale = 1.0 / (group_len * groups)
    bias = jnp.broadcast_to(proj_bias[:, None], (pair_channels, 2 * half))
    share = share_rows // channels

    def update_call(last, left_values, extra, out_shape, out_specs, scratch):
        blocks = max(len(left_values) // 2, 1)
        row_count = share * blocks
        outer_size = row_count * channels * channels * half
        places = (blocks, len(data), right_places, share_rows, source_rows, group_len, run)
        return pl.pallas_call(
            functools.partial(update_kernel, places, cols, low, last, scale),
            out_shape=out_shape,
            in_specs=[smem] + [vmem] * (len(left_values) + len(data) + 2 + len(extra)),
            out_specs=out_specs,
            scratch_shapes=scratch[:-1]
            + [
                pltpu.VMEM((row_count, channels * channels // 2, 2 * half), bf16),
            ]
            + scratch[-1:],
            compiler_params=params,
            cost_estimate=pl.CostEstimate(
                flops=2 * outer_size * (groups * group_len + 2 * pair_channels),
                bytes_accessed=2 * outer_size,
                transcendentals=0,
            ),
            name="update_last" if last else "update_first",
        )(place, *left_values, *data, bias, weight, *extra)

    first = update_call(
        False, [first_lhs], [], jax.ShapeDtypeStruct((share, half, pair_channels), bf16), vmem, []
    )
    outs = update_call(
        True,
        last_lefts,
        [first],
        [jax.ShapeDtypeStruct((run, half, pair_channels), bf16)] * 2
        + [jax.ShapeDtypeStruct((2 * run, run, pair_channels), bf16)] * (2 * low),
        [vmem] * (2 + 2 * low),
        [
            pltpu.VMEM(((2 * run - share) * channels, groups * group_len), bf16),
            pltpu.VMEM((2 * run, half, pair_channels), bf16),
        ],
    )

    mirrors = []
    for dz in range(low):
        for flip in range(2):
            pairs = []
            for r in range(rows):
                for c in range(cols):
                    for q in range(groups):
                        source = (r * cols + c) * groups + q
                        target = 2 * c + (r % 2 ^ flip)
                        target = (target * cols + r // 2) * groups + (q ^ dz)
                        pairs.append((source, target))
            mirrors.append(lax.ppermute(outs[2 + 2 * dz + flip], axes, pairs))
    update_other = swap(outs[1], "seq", groups, low)

    vectors = jnp.concatenate([norm_gain, down_bias, up_bias]).reshape(1, -1)
    cell = jnp.arange(run * run)
    mirror_cell = cell % run * run + cell // run
    swap_cells = (mirror_cell[:, None] == cell[None, :]).astype(bf16)
    anywhere = pl.BlockSpec(memory_space=pl.ANY)
    result = None
    for other in range(2):
        operands = [
            place,
            pair_rep,
            update_other if other else outs[0],
            *mirrors,
            up_weight,
            down_weight,
            vectors,
            swap_cells,
        ]
        extra = [] if result is None else [result]
        result = pl.pallas_call(
            functools.partial(finish_kernel, low, other),
            out_shape=jax.ShapeDtypeStruct(pair_rep.shape, bf16),
            in_specs=[smem] + [vmem] * (len(operands) - 1) + [anywhere] * len(extra),
            out_specs=anywhere,
            scratch_shapes=[
                pltpu.VMEM((2 * low, run, run, pair_channels), bf16),
                pltpu.SemaphoreType.DMA((2 * low,)),
            ],
            input_output_aliases={len(operands): 0} if extra else {},
            compiler_params=params,
            name="finish",
        )(*operands, *extra)
    return result


def solution(mesh):
    in_specs = (
        P("seq", None, "row"),
        P("seq", "row", "col"),
        P(),
        P(),
        P(("row", "seq"), "col", None),
        P(),
        P(),
        P(),
        P(),
        P(),
    )
    out_specs = P(("row", "seq"), "col", None)
    return jax.shard_map(
        on_device, mesh=mesh, in_specs=in_specs, out_specs=out_specs, check_vma=False
    )
```

```python
import functools

import jax
import jax.numpy as jnp
from jax import lax
from jax.experimental import pallas as pl
from jax.experimental.pallas import tpu as pltpu
from jax.sharding import PartitionSpec as P

epsilon = 1e-05
axes = ("row", "col", "seq")


def update_kernel(places, shares, low, last, scale, *refs):
    blocks, data_count, right_places, share_rows, source_rows, group_len, run = places
    groups = len(right_places)
    sources = len(right_places[0])
    refs = list(refs)
    place_ref = refs.pop(0)
    left_refs = [refs.pop(0) for _ in range(3 * blocks if last else 1)]
    data_refs = [refs.pop(0) for _ in range(data_count)]
    bias_ref, weight_ref = refs.pop(0), refs.pop(0)
    first_ref = refs.pop(0) if last else None
    update_ref = refs.pop() if last else refs[0]
    outer_ref = refs.pop()
    lhs_ref = refs.pop() if last else left_refs[0]
    out_refs = refs
    row_count, _, lanes = outer_ref.shape
    low = groups // 2
    channels = share_rows * blocks // row_count
    share = share_rows // channels
    per = source_rows // group_len
    half = lanes // 2
    pair_channels = weight_ref.shape[0] // 2
    lane_low = lax.broadcasted_iota(jnp.int32, (pair_channels, lanes), 1) < half
    for block in range(blocks if last else 0):
        for dz in range(groups):
            index = 3 * block + max(0, dz - low + 1)
            begin = dz * share_rows if dz < low else 0
            lhs_ref[
                block * share_rows : (block + 1) * share_rows,
                dz * group_len : (dz + 1) * group_len,
            ] = left_refs[index][begin : begin + share_rows]

    def right_tile(item):
        source, rest = divmod(item, per)
        tiles = []
        for dz in range(groups):
            operand, first = right_places[dz][source]
            first += rest * group_len
            tiles.append(data_refs[operand][first : first + group_len])
        return jnp.concatenate(tiles, axis=0)

    for pair in range(sources * per // 2):
        right = jnp.concatenate([right_tile(2 * pair), right_tile(2 * pair + 1)], axis=1)
        outer = jnp.dot(lhs_ref[...], right, preferred_element_type=jnp.float32)
        outer = outer.astype(jnp.bfloat16)
        for part in range(2):
            item = 2 * pair + part
            outer_ref[:, item * channels : (item + 1) * channels, :] = outer[
                :, part * lanes : (part + 1) * lanes
            ].reshape(row_count, channels, lanes)

    unroll = min(4, row_count // 2)

    @pl.loop(0, row_count // (2 * unroll))
    def _(step):
        for two in range(unroll):
            index = step * unroll + two
            both = jnp.concatenate([outer_ref[2 * index], outer_ref[2 * index + 1]], axis=1)
            proj = jnp.dot(weight_ref[...], both, preferred_element_type=jnp.float32)
            a0 = proj[:pair_channels, :lanes]
            a1 = proj[:pair_channels, lanes:]
            b0 = proj[pair_channels:, :lanes]
            b1 = proj[pair_channels:, lanes:]
            cell = jnp.where(lane_low, a0, b1) + pltpu.roll(
                jnp.where(lane_low, a1, b0), half, 1
            )
            cell = (cell * scale + bias_ref[...]).astype(jnp.bfloat16)
            begin = 2 * index
            if last:
                begin = (place_ref[2] ^ (1 + begin // share)) * share + begin % share
            update_ref[pl.ds(begin, 2)] = cell.T.reshape(2, half, pair_channels)

    if last:
        update_ref[pl.ds(place_ref[2] * share, share)] = first_ref[...]
        core, z_low, z_high = place_ref[0], place_ref[1], place_ref[3]
        out_refs[0][...] = update_ref[pl.ds(z_high * run, run)]
        out_refs[1][...] = update_ref[pl.ds((1 - z_high) * run, run)]
        for dz in range(low):
            for flip in range(2):
                begin = (core ^ flip) * (half // 2) + (z_low ^ dz) * run
                out_refs[2 + 2 * dz + flip][...] = update_ref[
                    :, pl.ds(pl.multiple_of(begin, run), run), :
                ]


def pack_kernel(*refs):
    rows = refs[0].shape[0]
    for index, ref in enumerate(refs[:-1]):
        refs[-1][index * rows : (index + 1) * rows] = ref[...]


def pack(*values):
    rows, lanes = values[0].shape
    return pl.pallas_call(
        pack_kernel,
        out_shape=jax.ShapeDtypeStruct((len(values) * rows, lanes), values[0].dtype),
        in_specs=[pl.BlockSpec(memory_space=pltpu.VMEM)] * len(values),
        out_specs=pl.BlockSpec(memory_space=pltpu.VMEM),
        compiler_params=pltpu.CompilerParams(vmem_limit_bytes=4 * 1024 * 1024),
        name="pack",
    )(*values)


def arrange_kernel(*refs):
    out_ref = refs[-1]
    rows, lanes = out_ref.shape[0], refs[0].shape[1]
    index = 0
    for ref in refs[:-1]:
        for begin in range(0, ref.shape[0], rows):
            out_ref[:, index * lanes : (index + 1) * lanes] = ref[begin : begin + rows]
            index += 1


def arrange(lefts, groups):
    lanes = lefts[0].shape[1]
    rows = sum(value.shape[0] for value in lefts) // groups
    return pl.pallas_call(
        arrange_kernel,
        out_shape=jax.ShapeDtypeStruct((rows, groups * lanes), lefts[0].dtype),
        in_specs=[pl.BlockSpec(memory_space=pltpu.VMEM)] * len(lefts),
        out_specs=pl.BlockSpec(memory_space=pltpu.VMEM),
        compiler_params=pltpu.CompilerParams(vmem_limit_bytes=4 * 1024 * 1024),
        cost_estimate=pl.CostEstimate(
            flops=rows * groups * lanes * 8 * lanes * groups * 4,
            bytes_accessed=4 * rows * groups * lanes,
            transcendentals=0,
        ),
        name="arrange",
    )(*lefts)


def finish_kernel(low, other, *refs):
    place_ref, pair_ref, direct_ref = refs[:3]
    mirror_refs = refs[3 : 3 + 2 * low]
    up_ref, down_ref, vector_ref, swap_ref = refs[3 + 2 * low : 7 + 2 * low]
    out_ref, done_ref, sems = refs[-3:]
    run, columns, pair_channels = pair_ref.shape
    half = columns // 2
    core, z_low, part = place_ref[0], place_ref[1], place_ref[3] ^ other
    cells = run * run
    gain = vector_ref[:, :pair_channels]
    down_bias = vector_ref[:, pair_channels : 2 * pair_channels]
    up_bias = vector_ref[:, 2 * pair_channels :]
    ones = jnp.full((2 * pair_channels, pair_channels), 1.0 / pair_channels, jnp.bfloat16)
    copies = []
    for dz in range(low):
        middles = []
        begins = []
        for flip in range(2):
            local = (core ^ flip) * (half // 2) + (z_low ^ dz) * run
            local = pl.multiple_of(local, run)
            begin = (core ^ flip) * half + (part * low + (z_low ^ dz)) * run
            begin = pl.multiple_of(begin, run)
            begins.append(begin)
            piece = mirror_refs[2 * dz + flip][pl.ds(part * run, run)]
            mirrored = jnp.dot(
                swap_ref[...],
                piece.reshape(cells, pair_channels),
                preferred_element_type=jnp.float32,
            )
            direct = direct_ref[:, pl.ds(local, run), :].reshape(cells, pair_channels)
            residual = pair_ref[:, pl.ds(begin, run), :].reshape(cells, pair_channels)
            middles.append(
                (
                    residual.astype(jnp.float32) + 0.5 * (direct.astype(jnp.float32) + mirrored)
                ).astype(jnp.bfloat16)
            )
        middle = jnp.concatenate(middles, axis=0)
        values = middle.astype(jnp.float32)
        center = jnp.dot(middle, ones[:pair_channels], preferred_element_type=jnp.float32)
        moved = values - center
        square = jnp.square(moved)
        high = square.astype(jnp.bfloat16)
        rest = (square - high.astype(jnp.float32)).astype(jnp.bfloat16)
        spread = jnp.dot(
            jnp.concatenate([high, rest], axis=1), ones, preferred_element_type=jnp.float32
        )
        normed = moved * lax.rsqrt(spread + epsilon) * gain
        hidden = jnp.dot(
            normed.astype(jnp.bfloat16), up_ref[...], preferred_element_type=jnp.float32
        )
        hidden = jnp.maximum(hidden + up_bias, 0.0).astype(jnp.bfloat16)
        result = jnp.dot(hidden, down_ref[...], preferred_element_type=jnp.float32)
        result = (values + result + down_bias).astype(jnp.bfloat16)
        for flip in range(2):
            index = 2 * dz + flip
            done_ref[index] = result[flip * cells : (flip + 1) * cells].reshape(
                run, run, pair_channels
            )
            copy = pltpu.make_async_copy(
                done_ref.at[index], out_ref.at[:, pl.ds(begins[flip], run), :], sems.at[index]
            )
            copy.start()
            copies.append(copy)
    for copy in copies:
        copy.wait()


def on_device(
    left_piece,
    right_piece,
    proj_weight,
    proj_bias,
    pair_rep,
    norm_gain,
    up_weight,
    up_bias,
    down_weight,
    down_bias,
):
    rows = lax.axis_size("row")
    cols = lax.axis_size("col")
    groups = lax.axis_size("seq")
    xs = rows // 2
    low = groups // 2
    row, col, seq = (lax.axis_index(name) for name in axes)
    core, z_low, z_high = row % 2, seq % low, seq // low
    run, columns, pair_channels = pair_rep.shape
    group_len, channels, _ = left_piece.shape
    e1 = right_piece.shape[1] // 2
    half = columns // 2
    bf16 = jnp.bfloat16

    def pick(value, index, axis=0):
        return lax.dynamic_index_in_dim(value, index, axis, False)

    def swap(value, name, size, flip):
        return lax.ppermute(value, name, [(i, i ^ flip) for i in range(size)])

    right = right_piece.reshape(group_len, e1, 2, 2, 2, half // 2).transpose(4, 1, 0, 2, 3, 5)
    source_rows = e1 * group_len
    right = right.reshape(2, source_rows, 2 * half)
    share_rows = 2 * run // cols * channels
    left = left_piece.transpose(2, 1, 0).reshape(2, low, run, channels, group_len)
    left = left.transpose(1, 0, 2, 3, 4).reshape(low, cols, share_rows, group_len)
    left = pick(left, col, 1)

    def after(value, *earlier):
        return lax.optimization_barrier((value, earlier))[0] if earlier else value

    mine, theirs = pick(right, z_high), pick(right, 1 - z_high)
    own, crossing = pick(left, z_low), pick(left, 1 - z_low)
    near = swap(crossing, "seq", groups, 1)
    blocks = {0: mine}
    blocks[low + 1] = swap(theirs, "seq", groups, low + 1)
    blocks[1] = swap(mine, "seq", groups, 1)
    blocks[low] = swap(blocks[low + 1], "seq", groups, 1)
    weight = proj_weight.reshape(channels, rows, e1, 2, pair_channels)
    weight = weight.transpose(1, 3, 4, 2, 0)
    weight = jnp.stack([pick(weight, row ^ m) for m in range(rows)], axis=2)
    weight = weight.reshape(2 * pair_channels, channels * channels // 2)
    bias = jnp.broadcast_to(proj_bias[:, None], (pair_channels, 2 * half))
    vectors = jnp.concatenate([norm_gain, down_bias, up_bias]).reshape(1, -1)
    cell = jnp.arange(run * run)
    mirror_cell = cell % run * run + cell // run
    swap_cells = (mirror_cell[:, None] == cell[None, :]).astype(bf16)
    weight, bias, vectors, swap_cells = constants = lax.optimization_barrier(
        (weight, bias, vectors, swap_cells)
    )
    lefts = [pack(own, near)]
    fars = [swap(own, "seq", groups, low), swap(near, "seq", groups, low)]
    shares = [[swap(lefts[0], "col", cols, dy)] for dy in range(1, cols)]
    near_shares = [pair[0] for pair in shares]
    for dy in range(1, cols):
        shares[dy - 1] += [swap(value, "col", cols, dy) for value in fars]
    far_shares = [pair[1] for pair in shares]
    first_lhs = arrange([lefts[0]] + fars, groups)
    data = []
    right_places = {dz: [] for dz in range(groups)}
    order = (0, 1, low + 1, low)
    crosses = {dz: [blocks[dz]] for dz in order}
    last = ()
    for dz in order:
        for dx in range(1, xs):
            behind = last + ((near_shares, constants) if dz == low else ())
            crosses[dz].append(swap(after(blocks[dz], *behind), "row", rows, 2 * dx))
            last = (crosses[dz][-1],)
    for position in range(xs):
        values = [crosses[dz][position] for dz in order]
        for dz, value in zip(order, values):
            right_places[dz].append((len(data), 0))
            data.append(value)
        count = len(order) if position == 0 else len(order) - 1
        exchanged = swap(pack(*values[:count]), "row", rows, 1)
        for index, dz in enumerate(order[:count]):
            right_places[dz].append((len(data), index * source_rows))
        data.append(exchanged)
        if count < len(order):
            right_places[low].append((len(data), 0))
            data.append(swap(after(values[-1], first_lhs, far_shares), "row", rows, 1))
    right_places = [right_places[dz] for dz in range(groups)]
    last_lefts = [value for pair in shares for value in pair]

    place = jnp.stack([core, z_low, col, z_high]).astype(jnp.int32)
    vmem = pl.BlockSpec(memory_space=pltpu.VMEM)
    smem = pl.BlockSpec(memory_space=pltpu.SMEM)
    params = pltpu.CompilerParams(vmem_limit_bytes=16 * 1024 * 1024)
    scale = 1.0 / (group_len * groups)
    share = share_rows // channels

    def update_call(last, left_values, extra, out_shape, out_specs, scratch):
        blocks = max(len(left_values) // 3, 1)
        row_count = share * blocks
        outer_size = row_count * channels * channels * half
        places = (blocks, len(data), right_places, share_rows, source_rows, group_len, run)
        return pl.pallas_call(
            functools.partial(update_kernel, places, cols, low, last, scale),
            out_shape=out_shape,
            in_specs=[smem] + [vmem] * (len(left_values) + len(data) + 2 + len(extra)),
            out_specs=out_specs,
            scratch_shapes=scratch[:-1]
            + [
                pltpu.VMEM((row_count, channels * channels // 2, 2 * half), bf16),
            ]
            + scratch[-1:],
            compiler_params=params,
            cost_estimate=pl.CostEstimate(
                flops=2 * outer_size * (groups * group_len + 2 * pair_channels),
                bytes_accessed=2 * outer_size,
                transcendentals=0,
            ),
            name="update_last" if last else "update_first",
        )(place, *left_values, *data, bias, weight, *extra)

    first = update_call(
        False, [first_lhs], [], jax.ShapeDtypeStruct((share, half, pair_channels), bf16), vmem, []
    )
    outs = update_call(
        True,
        last_lefts,
        [first],
        [jax.ShapeDtypeStruct((run, half, pair_channels), bf16)] * 2
        + [jax.ShapeDtypeStruct((2 * run, run, pair_channels), bf16)] * (2 * low),
        [vmem] * (2 + 2 * low),
        [
            pltpu.VMEM(((2 * run - share) * channels, groups * group_len), bf16),
            pltpu.VMEM((2 * run, half, pair_channels), bf16),
        ],
    )

    mirrors = []
    for dz in range(low):
        for flip in range(2):
            pairs = []
            for r in range(rows):
                for c in range(cols):
                    for q in range(groups):
                        source = (r * cols + c) * groups + q
                        target = 2 * c + (r % 2 ^ flip)
                        target = (target * cols + r // 2) * groups + (q ^ dz)
                        pairs.append((source, target))
            mirrors.append(lax.ppermute(outs[2 + 2 * dz + flip], axes, pairs))
    update_other = swap(outs[1], "seq", groups, low)

    anywhere = pl.BlockSpec(memory_space=pl.ANY)
    result = None
    for other in range(2):
        operands = [
            place,
            pair_rep,
            update_other if other else outs[0],
            *mirrors,
            up_weight,
            down_weight,
            vectors,
            swap_cells,
        ]
        extra = [] if result is None else [result]
        result = pl.pallas_call(
            functools.partial(finish_kernel, low, other),
            out_shape=jax.ShapeDtypeStruct(pair_rep.shape, bf16),
            in_specs=[smem] + [vmem] * (len(operands) - 1) + [anywhere] * len(extra),
            out_specs=anywhere,
            scratch_shapes=[
                pltpu.VMEM((2 * low, run, run, pair_channels), bf16),
                pltpu.SemaphoreType.DMA((2 * low,)),
            ],
            input_output_aliases={len(operands): 0} if extra else {},
            compiler_params=params,
            name="finish",
        )(*operands, *extra)
    return result


def solution(mesh):
    in_specs = (
        P("seq", None, "row"),
        P("seq", "row", "col"),
        P(),
        P(),
        P(("row", "seq"), "col", None),
        P(),
        P(),
        P(),
        P(),
        P(),
    )
    out_specs = P(("row", "seq"), "col", None)
    return jax.shard_map(
        on_device, mesh=mesh, in_specs=in_specs, out_specs=out_specs, check_vma=False
    )
```

```python
import functools

import jax
import jax.numpy as jnp
from jax import lax
from jax.experimental import pallas as pl
from jax.experimental.pallas import tpu as pltpu
from jax.sharding import PartitionSpec as P

epsilon = 1e-05
axes = ("row", "col", "seq")


def update_kernel(places, shares, low, last, scale, *refs):
    blocks, data_count, right_places, share_rows, source_rows, group_len, run = places
    groups = len(right_places)
    sources = len(right_places[0])
    refs = list(refs)
    place_ref = refs.pop(0)
    left_refs = [refs.pop(0) for _ in range(3 * blocks if last else 1)]
    data_refs = [refs.pop(0) for _ in range(data_count)]
    bias_ref, weight_ref = refs.pop(0), refs.pop(0)
    first_ref = refs.pop(0) if last else None
    update_ref = refs.pop() if last else refs[0]
    outer_ref = refs.pop()
    lhs_ref = refs.pop() if last else left_refs[0]
    out_refs = refs
    row_count, _, lanes = outer_ref.shape
    low = groups // 2
    channels = share_rows * blocks // row_count
    share = share_rows // channels
    per = source_rows // group_len
    half = lanes // 2
    pair_channels = weight_ref.shape[0] // 2
    lane_low = lax.broadcasted_iota(jnp.int32, (pair_channels, lanes), 1) < half
    for block in range(blocks if last else 0):
        for dz in range(groups):
            index = 3 * block + max(0, dz - low + 1)
            begin = dz * share_rows if dz < low else 0
            lhs_ref[
                block * share_rows : (block + 1) * share_rows,
                dz * group_len : (dz + 1) * group_len,
            ] = left_refs[index][begin : begin + share_rows]

    def right_tile(item):
        source, rest = divmod(item, per)
        tiles = []
        for dz in range(groups):
            operand, first = right_places[dz][source]
            first += rest * group_len
            tiles.append(data_refs[operand][first : first + group_len])
        return jnp.concatenate(tiles, axis=0)

    for pair in range(sources * per // 2):
        right = jnp.concatenate([right_tile(2 * pair), right_tile(2 * pair + 1)], axis=1)
        outer = jnp.dot(lhs_ref[...], right, preferred_element_type=jnp.float32)
        outer = outer.astype(jnp.bfloat16)
        for part in range(2):
            item = 2 * pair + part
            outer_ref[:, item * channels : (item + 1) * channels, :] = outer[
                :, part * lanes : (part + 1) * lanes
            ].reshape(row_count, channels, lanes)

    unroll = min(4, row_count // 2)

    @pl.loop(0, row_count // (2 * unroll))
    def _(step):
        for two in range(unroll):
            index = step * unroll + two
            both = jnp.concatenate([outer_ref[2 * index], outer_ref[2 * index + 1]], axis=1)
            proj = jnp.dot(weight_ref[...], both, preferred_element_type=jnp.float32)
            a0 = proj[:pair_channels, :lanes]
            a1 = proj[:pair_channels, lanes:]
            b0 = proj[pair_channels:, :lanes]
            b1 = proj[pair_channels:, lanes:]
            cell = jnp.where(lane_low, a0, b1) + pltpu.roll(
                jnp.where(lane_low, a1, b0), half, 1
            )
            cell = (cell * scale + bias_ref[...]).astype(jnp.bfloat16)
            begin = 2 * index
            if last:
                begin = (place_ref[2] ^ (1 + begin // share)) * share + begin % share
            update_ref[pl.ds(begin, 2)] = cell.T.reshape(2, half, pair_channels)

    if last:
        update_ref[pl.ds(place_ref[2] * share, share)] = first_ref[...]
        core, z_low, z_high = place_ref[0], place_ref[1], place_ref[3]
        out_refs[0][...] = update_ref[pl.ds(z_high * run, run)]
        out_refs[1][...] = update_ref[pl.ds((1 - z_high) * run, run)]
        for dz in range(low):
            for flip in range(2):
                begin = (core ^ flip) * (half // 2) + (z_low ^ dz) * run
                out_refs[2 + 2 * dz + flip][...] = update_ref[
                    :, pl.ds(pl.multiple_of(begin, run), run), :
                ]


def pack_kernel(*refs):
    rows = refs[0].shape[0]
    for index, ref in enumerate(refs[:-1]):
        refs[-1][index * rows : (index + 1) * rows] = ref[...]


def pack(*values):
    rows, lanes = values[0].shape
    return pl.pallas_call(
        pack_kernel,
        out_shape=jax.ShapeDtypeStruct((len(values) * rows, lanes), values[0].dtype),
        in_specs=[pl.BlockSpec(memory_space=pltpu.VMEM)] * len(values),
        out_specs=pl.BlockSpec(memory_space=pltpu.VMEM),
        compiler_params=pltpu.CompilerParams(vmem_limit_bytes=4 * 1024 * 1024),
        name="pack",
    )(*values)


def arrange_kernel(*refs):
    out_ref = refs[-1]
    rows, lanes = out_ref.shape[0], refs[0].shape[1]
    index = 0
    for ref in refs[:-1]:
        for begin in range(0, ref.shape[0], rows):
            out_ref[:, index * lanes : (index + 1) * lanes] = ref[begin : begin + rows]
            index += 1


def arrange(lefts, groups):
    lanes = lefts[0].shape[1]
    rows = sum(value.shape[0] for value in lefts) // groups
    return pl.pallas_call(
        arrange_kernel,
        out_shape=jax.ShapeDtypeStruct((rows, groups * lanes), lefts[0].dtype),
        in_specs=[pl.BlockSpec(memory_space=pltpu.VMEM)] * len(lefts),
        out_specs=pl.BlockSpec(memory_space=pltpu.VMEM),
        compiler_params=pltpu.CompilerParams(vmem_limit_bytes=4 * 1024 * 1024),
        cost_estimate=pl.CostEstimate(
            flops=rows * groups * lanes * 8 * lanes * groups * 4,
            bytes_accessed=4 * rows * groups * lanes,
            transcendentals=0,
        ),
        name="arrange",
    )(*lefts)


def finish_kernel(low, other, *refs):
    place_ref, pair_ref, direct_ref = refs[:3]
    mirror_refs = refs[3 : 3 + 2 * low]
    up_ref, down_ref, vector_ref, swap_ref = refs[3 + 2 * low : 7 + 2 * low]
    out_ref, done_ref, sems = refs[-3:]
    run, columns, pair_channels = pair_ref.shape
    half = columns // 2
    core, z_low, part = place_ref[0], place_ref[1], place_ref[3] ^ other
    cells = run * run
    gain = vector_ref[:, :pair_channels]
    down_bias = vector_ref[:, pair_channels : 2 * pair_channels]
    up_bias = vector_ref[:, 2 * pair_channels :]
    ones = jnp.full((2 * pair_channels, pair_channels), 1.0 / pair_channels, jnp.bfloat16)
    copies = []
    for dz in range(low):
        middles = []
        begins = []
        for flip in range(2):
            local = (core ^ flip) * (half // 2) + (z_low ^ dz) * run
            local = pl.multiple_of(local, run)
            begin = (core ^ flip) * half + (part * low + (z_low ^ dz)) * run
            begin = pl.multiple_of(begin, run)
            begins.append(begin)
            piece = mirror_refs[2 * dz + flip][pl.ds(part * run, run)]
            mirrored = jnp.dot(
                swap_ref[...],
                piece.reshape(cells, pair_channels),
                preferred_element_type=jnp.float32,
            )
            direct = direct_ref[:, pl.ds(local, run), :].reshape(cells, pair_channels)
            residual = pair_ref[:, pl.ds(begin, run), :].reshape(cells, pair_channels)
            middles.append(
                (
                    residual.astype(jnp.float32) + 0.5 * (direct.astype(jnp.float32) + mirrored)
                ).astype(jnp.bfloat16)
            )
        middle = jnp.concatenate(middles, axis=0)
        values = middle.astype(jnp.float32)
        center = jnp.dot(middle, ones[:pair_channels], preferred_element_type=jnp.float32)
        moved = values - center
        square = jnp.square(moved)
        high = square.astype(jnp.bfloat16)
        rest = (square - high.astype(jnp.float32)).astype(jnp.bfloat16)
        spread = jnp.dot(
            jnp.concatenate([high, rest], axis=1), ones, preferred_element_type=jnp.float32
        )
        normed = moved * lax.rsqrt(spread + epsilon) * gain
        hidden = jnp.dot(
            normed.astype(jnp.bfloat16), up_ref[...], preferred_element_type=jnp.float32
        )
        hidden = jnp.maximum(hidden + up_bias, 0.0).astype(jnp.bfloat16)
        result = jnp.dot(hidden, down_ref[...], preferred_element_type=jnp.float32)
        result = (values + result + down_bias).astype(jnp.bfloat16)
        for flip in range(2):
            index = 2 * dz + flip
            done_ref[index] = result[flip * cells : (flip + 1) * cells].reshape(
                run, run, pair_channels
            )
            copy = pltpu.make_async_copy(
                done_ref.at[index], out_ref.at[:, pl.ds(begins[flip], run), :], sems.at[index]
            )
            copy.start()
            copies.append(copy)
    for copy in copies:
        copy.wait()


def on_device(
    left_piece,
    right_piece,
    proj_weight,
    proj_bias,
    pair_rep,
    norm_gain,
    up_weight,
    up_bias,
    down_weight,
    down_bias,
):
    rows = lax.axis_size("row")
    cols = lax.axis_size("col")
    groups = lax.axis_size("seq")
    xs = rows // 2
    low = groups // 2
    row, col, seq = (lax.axis_index(name) for name in axes)
    core, z_low, z_high = row % 2, seq % low, seq // low
    run, columns, pair_channels = pair_rep.shape
    group_len, channels, _ = left_piece.shape
    e1 = right_piece.shape[1] // 2
    half = columns // 2
    bf16 = jnp.bfloat16

    def pick(value, index, axis=0):
        return lax.dynamic_index_in_dim(value, index, axis, False)

    def swap(value, name, size, flip):
        return lax.ppermute(value, name, [(i, i ^ flip) for i in range(size)])

    right = right_piece.reshape(group_len, e1, 2, 2, 2, half // 2).transpose(4, 1, 0, 2, 3, 5)
    source_rows = e1 * group_len
    right = right.reshape(2, source_rows, 2 * half)
    share_rows = 2 * run // cols * channels
    left = left_piece.transpose(2, 1, 0).reshape(2, low, run, channels, group_len)
    left = left.transpose(1, 0, 2, 3, 4).reshape(low, cols, share_rows, group_len)
    left = pick(left, col, 1)

    def after(value, *earlier):
        return lax.optimization_barrier((value, earlier))[0] if earlier else value

    mine, theirs = pick(right, z_high), pick(right, 1 - z_high)
    own, crossing = pick(left, z_low), pick(left, 1 - z_low)
    near = swap(crossing, "seq", groups, 1)
    blocks = {0: mine}
    blocks[low + 1] = swap(theirs, "seq", groups, low + 1)
    blocks[1] = swap(mine, "seq", groups, 1)
    blocks[low] = swap(blocks[low + 1], "seq", groups, 1)
    weight = proj_weight.reshape(channels, rows, e1, 2, pair_channels)
    weight = weight.transpose(1, 3, 4, 2, 0)
    weight = jnp.stack([pick(weight, row ^ m) for m in range(rows)], axis=2)
    weight = weight.reshape(2 * pair_channels, channels * channels // 2)
    bias = jnp.broadcast_to(proj_bias[:, None], (pair_channels, 2 * half))
    vectors = jnp.concatenate([norm_gain, down_bias, up_bias]).reshape(1, -1)
    cell = jnp.arange(run * run)
    mirror_cell = cell % run * run + cell // run
    swap_cells = (mirror_cell[:, None] == cell[None, :]).astype(bf16)
    lefts = [pack(own, near)]
    fars = [swap(own, "seq", groups, low), swap(near, "seq", groups, low)]
    shares = [[swap(lefts[0], "col", cols, dy)] for dy in range(1, cols)]
    near_shares = [pair[0] for pair in shares]
    for dy in range(1, cols):
        shares[dy - 1] += [swap(value, "col", cols, dy) for value in fars]
    far_shares = [pair[1] for pair in shares]
    first_lhs = arrange([lefts[0]] + fars, groups)
    data = []
    right_places = {dz: [] for dz in range(groups)}
    order = (0, 1, low + 1, low)
    crosses = {dz: [blocks[dz]] for dz in order}
    last = ()
    for dz in order:
        for dx in range(1, xs):
            behind = last + ((near_shares,) if dz == low else ())
            crosses[dz].append(swap(after(blocks[dz], *behind), "row", rows, 2 * dx))
            last = (crosses[dz][-1],)
    for position in range(xs):
        values = [crosses[dz][position] for dz in order]
        count = len(order) if position == 0 else len(order) - 1
        packed = pack(*values[:count])
        for value in (packed, swap(packed, "row", rows, 1)):
            for index, dz in enumerate(order[:count]):
                right_places[dz].append((len(data), index * source_rows))
            data.append(value)
        if count < len(order):
            exchanged = swap(after(values[-1], first_lhs, far_shares), "row", rows, 1)
            for value in (values[-1], exchanged):
                right_places[low].append((len(data), 0))
                data.append(value)
    right_places = [right_places[dz] for dz in range(groups)]
    last_lefts = [value for pair in shares for value in pair]

    place = jnp.stack([core, z_low, col, z_high]).astype(jnp.int32)
    vmem = pl.BlockSpec(memory_space=pltpu.VMEM)
    smem = pl.BlockSpec(memory_space=pltpu.SMEM)
    params = pltpu.CompilerParams(vmem_limit_bytes=16 * 1024 * 1024)
    scale = 1.0 / (group_len * groups)
    share = share_rows // channels

    def update_call(last, left_values, extra, out_shape, out_specs, scratch):
        blocks = max(len(left_values) // 3, 1)
        row_count = share * blocks
        outer_size = row_count * channels * channels * half
        places = (blocks, len(data), right_places, share_rows, source_rows, group_len, run)
        return pl.pallas_call(
            functools.partial(update_kernel, places, cols, low, last, scale),
            out_shape=out_shape,
            in_specs=[smem] + [vmem] * (len(left_values) + len(data) + 2 + len(extra)),
            out_specs=out_specs,
            scratch_shapes=scratch[:-1]
            + [
                pltpu.VMEM((row_count, channels * channels // 2, 2 * half), bf16),
            ]
            + scratch[-1:],
            compiler_params=params,
            cost_estimate=pl.CostEstimate(
                flops=2 * outer_size * (groups * group_len + 2 * pair_channels),
                bytes_accessed=2 * outer_size,
                transcendentals=0,
            ),
            name="update_last" if last else "update_first",
        )(place, *left_values, *data, bias, weight, *extra)

    first = update_call(
        False, [first_lhs], [], jax.ShapeDtypeStruct((share, half, pair_channels), bf16), vmem, []
    )
    outs = update_call(
        True,
        last_lefts,
        [first],
        [jax.ShapeDtypeStruct((run, half, pair_channels), bf16)] * 2
        + [jax.ShapeDtypeStruct((2 * run, run, pair_channels), bf16)] * (2 * low),
        [vmem] * (2 + 2 * low),
        [
            pltpu.VMEM(((2 * run - share) * channels, groups * group_len), bf16),
            pltpu.VMEM((2 * run, half, pair_channels), bf16),
        ],
    )

    mirrors = []
    for dz in range(low):
        for flip in range(2):
            pairs = []
            for r in range(rows):
                for c in range(cols):
                    for q in range(groups):
                        source = (r * cols + c) * groups + q
                        target = 2 * c + (r % 2 ^ flip)
                        target = (target * cols + r // 2) * groups + (q ^ dz)
                        pairs.append((source, target))
            mirrors.append(lax.ppermute(outs[2 + 2 * dz + flip], axes, pairs))
    update_other = swap(outs[1], "seq", groups, low)

    anywhere = pl.BlockSpec(memory_space=pl.ANY)
    result = None
    for other in range(2):
        operands = [
            place,
            pair_rep,
            update_other if other else outs[0],
            *mirrors,
            up_weight,
            down_weight,
            vectors,
            swap_cells,
        ]
        extra = [] if result is None else [result]
        result = pl.pallas_call(
            functools.partial(finish_kernel, low, other),
            out_shape=jax.ShapeDtypeStruct(pair_rep.shape, bf16),
            in_specs=[smem] + [vmem] * (len(operands) - 1) + [anywhere] * len(extra),
            out_specs=anywhere,
            scratch_shapes=[
                pltpu.VMEM((2 * low, run, run, pair_channels), bf16),
                pltpu.SemaphoreType.DMA((2 * low,)),
            ],
            input_output_aliases={len(operands): 0} if extra else {},
            compiler_params=params,
            name="finish",
        )(*operands, *extra)
    return result


def solution(mesh):
    in_specs = (
        P("seq", None, "row"),
        P("seq", "row", "col"),
        P(),
        P(),
        P(("row", "seq"), "col", None),
        P(),
        P(),
        P(),
        P(),
        P(),
    )
    out_specs = P(("row", "seq"), "col", None)
    return jax.shard_map(
        on_device, mesh=mesh, in_specs=in_specs, out_specs=out_specs, check_vma=False
    )
```

```python
import functools

import jax
import jax.numpy as jnp
from jax import lax
from jax.experimental import pallas as pl
from jax.experimental.pallas import tpu as pltpu
from jax.sharding import PartitionSpec as P

epsilon = 1e-05
axes = ("row", "col", "seq")


def update_kernel(places, shares, low, last, scale, *refs):
    blocks, data_count, right_places, share_rows, source_rows, group_len, run = places
    groups = len(right_places)
    sources = len(right_places[0])
    refs = list(refs)
    place_ref = refs.pop(0)
    left_refs = [refs.pop(0) for _ in range(3 * blocks)]
    data_refs = [refs.pop(0) for _ in range(data_count)]
    bias_ref, weight_ref = refs.pop(0), refs.pop(0)
    first_ref = refs.pop(0)
    update_ref = refs.pop() if last else refs[0]
    outer_ref = refs.pop()
    lhs_ref = refs.pop()
    out_refs = refs
    row_count, _, lanes = outer_ref.shape
    low = groups // 2
    channels = share_rows * blocks // row_count
    share = share_rows // channels
    per = source_rows // group_len
    half = lanes // 2
    pair_channels = weight_ref.shape[0] // 2
    lane_low = lax.broadcasted_iota(jnp.int32, (pair_channels, lanes), 1) < half
    for block in range(blocks):
        for dz in range(groups):
            index = 3 * block + max(0, dz - low + 1)
            begin = dz * share_rows if dz < low else 0
            lhs_ref[
                block * share_rows : (block + 1) * share_rows,
                dz * group_len : (dz + 1) * group_len,
            ] = left_refs[index][begin : begin + share_rows]

    def right_tile(item):
        source, rest = divmod(item, per)
        tiles = []
        for dz in range(groups):
            operand, first = right_places[dz][source]
            first += rest * group_len
            tiles.append(data_refs[operand][first : first + group_len])
        return jnp.concatenate(tiles, axis=0)

    for pair in range(sources * per // 2):
        right = jnp.concatenate([right_tile(2 * pair), right_tile(2 * pair + 1)], axis=1)
        outer = jnp.dot(lhs_ref[...], right, preferred_element_type=jnp.float32)
        outer = outer.astype(jnp.bfloat16)
        for part in range(2):
            item = 2 * pair + part
            outer_ref[:, item * channels : (item + 1) * channels, :] = outer[
                :, part * lanes : (part + 1) * lanes
            ].reshape(row_count, channels, lanes)

    unroll = min(4, row_count // 2)

    @pl.loop(0, row_count // (2 * unroll))
    def _(step):
        for two in range(unroll):
            index = step * unroll + two
            both = jnp.concatenate([outer_ref[2 * index], outer_ref[2 * index + 1]], axis=1)
            proj = jnp.dot(weight_ref[...], both, preferred_element_type=jnp.float32)
            a0 = proj[:pair_channels, :lanes]
            a1 = proj[:pair_channels, lanes:]
            b0 = proj[pair_channels:, :lanes]
            b1 = proj[pair_channels:, lanes:]
            cell = jnp.where(lane_low, a0, b1) + pltpu.roll(
                jnp.where(lane_low, a1, b0), half, 1
            )
            cell = (cell * scale + bias_ref[...]).astype(jnp.bfloat16)
            begin = 2 * index
            if last:
                begin = (place_ref[2] ^ (1 + begin // share)) * share + begin % share
            update_ref[pl.ds(begin, 2)] = cell.T.reshape(2, half, pair_channels)

    if last:
        update_ref[pl.ds(place_ref[2] * share, share)] = first_ref[...]
        core, z_low, z_high = place_ref[0], place_ref[1], place_ref[3]
        out_refs[0][...] = update_ref[pl.ds(z_high * run, run)]
        quarter = half // 2

        def mirrored(slot, dz, flip):
            begin = (core ^ flip) * quarter + (z_low ^ dz) * run
            out_refs[1 + slot][...] = update_ref[:, pl.ds(pl.multiple_of(begin, run), run), :]

        def direct(slot, part):
            for index in range(low):
                begin = part * quarter + index * run
                out_refs[1 + slot][index * run : (index + 1) * run] = update_ref[
                    pl.ds((1 - z_high) * run, run), begin : begin + run, :
                ]

        for side in range(2):

            @pl.when(core == side)
            def _():
                for dz in range(2):
                    mirrored(2 * dz + side, dz, 0)
                    direct(2 * dz + 1 - side, dz)

        for dz in range(low):
            mirrored(4 + dz, dz, 1)


def pack_kernel(*refs):
    rows = refs[0].shape[0]
    for index, ref in enumerate(refs[:-1]):
        refs[-1][index * rows : (index + 1) * rows] = ref[...]


def pack(*values):
    rows, lanes = values[0].shape
    return pl.pallas_call(
        pack_kernel,
        out_shape=jax.ShapeDtypeStruct((len(values) * rows, lanes), values[0].dtype),
        in_specs=[pl.BlockSpec(memory_space=pltpu.VMEM)] * len(values),
        out_specs=pl.BlockSpec(memory_space=pltpu.VMEM),
        compiler_params=pltpu.CompilerParams(vmem_limit_bytes=4 * 1024 * 1024),
        name="pack",
    )(*values)


def arrived_kernel(first_ref, second_ref, out_ref):
    rows = out_ref.shape[0] // 2
    out_ref[:rows] = first_ref[:rows]
    out_ref[rows:] = second_ref[:rows]


def arrived(first, second, flops):
    return pl.pallas_call(
        arrived_kernel,
        out_shape=jax.ShapeDtypeStruct((32, first.shape[1]), first.dtype),
        in_specs=[pl.BlockSpec(memory_space=pltpu.VMEM)] * 2,
        out_specs=pl.BlockSpec(memory_space=pltpu.VMEM),
        compiler_params=pltpu.CompilerParams(vmem_limit_bytes=4 * 1024 * 1024),
        cost_estimate=pl.CostEstimate(
            flops=flops, bytes_accessed=4 * first.size, transcendentals=0
        ),
        name="arrived",
    )(first, second)


def finish_kernel(low, *refs):
    place_ref, pair_ref, own_ref = refs[:3]
    slot_refs, mirror_refs = refs[3:7], refs[7 : 7 + low]
    up_ref, down_ref, vector_ref, swap_ref = refs[7 + low : 11 + low]
    out_ref, done_ref, sems = refs[-3:]
    run, columns, pair_channels = pair_ref.shape
    half = columns // 2
    core, z_low, z_high = place_ref[0], place_ref[1], place_ref[3]
    cells = run * run
    gain = vector_ref[:, :pair_channels]
    down_bias = vector_ref[:, pair_channels : 2 * pair_channels]
    up_bias = vector_ref[:, 2 * pair_channels :]
    ones = jnp.full((2 * pair_channels, pair_channels), 1.0 / pair_channels, jnp.bfloat16)

    def chosen(first, second, rows):
        return jnp.where(core == 0, slot_refs[first][rows], slot_refs[second][rows])

    copies = []
    for chunk in range(2 * low):
        other, dz = divmod(chunk, low)
        part = z_high ^ other
        middles = []
        begins = []
        for flip in range(2):
            local = (core ^ flip) * (half // 2) + (z_low ^ dz) * run
            local = pl.multiple_of(local, run)
            begin = (core ^ flip) * half + (part * low + (z_low ^ dz)) * run
            begin = pl.multiple_of(begin, run)
            begins.append(begin)
            rows = pl.ds(part * run, run)
            if flip == 0:
                piece = chosen(2 * dz, 2 * dz + 1, rows)
            else:
                piece = mirror_refs[dz][rows]
            mirrored = jnp.dot(
                swap_ref[...],
                piece.reshape(cells, pair_channels),
                preferred_element_type=jnp.float32,
            )
            if other == 0:
                direct = own_ref[:, pl.ds(local, run), :]
            else:
                rows = pl.ds((z_low ^ dz) * run, run)
                direct = chosen(1, 2, rows) if flip == 0 else chosen(3, 0, rows)
            direct = direct.reshape(cells, pair_channels)
            residual = pair_ref[:, pl.ds(begin, run), :].reshape(cells, pair_channels)
            middles.append(
                (
                    residual.astype(jnp.float32) + 0.5 * (direct.astype(jnp.float32) + mirrored)
                ).astype(jnp.bfloat16)
            )
        middle = jnp.concatenate(middles, axis=0)
        values = middle.astype(jnp.float32)
        center = jnp.dot(middle, ones[:pair_channels], preferred_element_type=jnp.float32)
        moved = values - center
        square = jnp.square(moved)
        high = square.astype(jnp.bfloat16)
        rest = (square - high.astype(jnp.float32)).astype(jnp.bfloat16)
        spread = jnp.dot(
            jnp.concatenate([high, rest], axis=1), ones, preferred_element_type=jnp.float32
        )
        normed = moved * lax.rsqrt(spread + epsilon) * gain
        hidden = jnp.dot(
            normed.astype(jnp.bfloat16), up_ref[...], preferred_element_type=jnp.float32
        )
        hidden = jnp.maximum(hidden + up_bias, 0.0).astype(jnp.bfloat16)
        result = jnp.dot(hidden, down_ref[...], preferred_element_type=jnp.float32)
        result = (values + result + down_bias).astype(jnp.bfloat16)
        for flip in range(2):
            index = 2 * chunk + flip
            done_ref[index] = result[flip * cells : (flip + 1) * cells].reshape(
                run, run, pair_channels
            )
            copy = pltpu.make_async_copy(
                done_ref.at[index], out_ref.at[:, pl.ds(begins[flip], run), :], sems.at[index]
            )
            copy.start()
            copies.append(copy)
    for copy in copies:
        copy.wait()


def on_device(
    left_piece,
    right_piece,
    proj_weight,
    proj_bias,
    pair_rep,
    norm_gain,
    up_weight,
    up_bias,
    down_weight,
    down_bias,
):
    rows = lax.axis_size("row")
    cols = lax.axis_size("col")
    groups = lax.axis_size("seq")
    xs = rows // 2
    low = groups // 2
    row, col, seq = (lax.axis_index(name) for name in axes)
    core, z_low, z_high = row % 2, seq % low, seq // low
    run, columns, pair_channels = pair_rep.shape
    group_len, channels, _ = left_piece.shape
    e1 = right_piece.shape[1] // 2
    half = columns // 2
    bf16 = jnp.bfloat16

    def pick(value, index, axis=0):
        return lax.dynamic_index_in_dim(value, index, axis, False)

    def swap(value, name, size, flip):
        return lax.ppermute(value, name, [(i, i ^ flip) for i in range(size)])

    right = right_piece.reshape(group_len, e1, 2, 2, 2, half // 2).transpose(4, 1, 0, 2, 3, 5)
    source_rows = e1 * group_len
    right = right.reshape(2, source_rows, 2 * half)
    share_rows = 2 * run // cols * channels
    left = left_piece.transpose(2, 1, 0).reshape(2, low, run, channels, group_len)
    left = left.transpose(1, 0, 2, 3, 4).reshape(low, cols, share_rows, group_len)
    left = pick(left, col, 1)

    def after(value, *earlier):
        return lax.optimization_barrier((value, earlier))[0] if earlier else value

    mine, theirs = pick(right, z_high), pick(right, 1 - z_high)
    own, crossing = pick(left, z_low), pick(left, 1 - z_low)
    near = swap(crossing, "seq", groups, 1)
    blocks = {0: mine}
    blocks[low + 1] = swap(theirs, "seq", groups, low + 1)
    blocks[1] = swap(mine, "seq", groups, 1)
    blocks[low] = swap(blocks[low + 1], "seq", groups, 1)
    weight = proj_weight.reshape(channels, rows, e1, 2, pair_channels)
    weight = weight.transpose(1, 3, 4, 2, 0)
    weight = jnp.stack([pick(weight, row ^ m) for m in range(rows)], axis=2)
    weight = weight.reshape(2 * pair_channels, channels * channels // 2)
    bias = jnp.broadcast_to(proj_bias[:, None], (pair_channels, 2 * half))
    vectors = jnp.concatenate([norm_gain, down_bias, up_bias]).reshape(1, -1)
    cell = jnp.arange(run * run)
    mirror_cell = cell % run * run + cell // run
    swap_cells = (mirror_cell[:, None] == cell[None, :]).astype(bf16)
    lefts = [pack(own, near)]
    fars = [swap(own, "seq", groups, low), swap(near, "seq", groups, low)]
    shares = [[swap(lefts[0], "col", cols, dy)] for dy in range(1, cols)]
    near_shares = [pair[0] for pair in shares]
    for dy in range(1, cols):
        shares[dy - 1] += [swap(value, "col", cols, dy) for value in fars]
    far_shares = [pair[1] for pair in shares]
    far_tile = arrived(*fars, 32 * (share_rows * groups * group_len) * groups * group_len // 4)
    data = []
    right_places = {dz: [] for dz in range(groups)}
    order = (0, 1, low + 1, low)
    crosses = {dz: [blocks[dz]] for dz in order}
    last = ()
    for dz in order:
        for dx in range(1, xs):
            behind = last + ((near_shares,) if dz == low else ())
            crosses[dz].append(swap(after(blocks[dz], *behind), "row", rows, 2 * dx))
            last = (crosses[dz][-1],)
    for position in range(xs):
        values = [crosses[dz][position] for dz in order]
        count = len(order) if position == 0 else len(order) - 1
        packed = pack(*values[:count])
        for value in (packed, swap(packed, "row", rows, 1)):
            for index, dz in enumerate(order[:count]):
                right_places[dz].append((len(data), index * source_rows))
            data.append(value)
        if count < len(order):
            exchanged = swap(after(values[-1], far_tile, far_shares), "row", rows, 1)
            for value in (values[-1], exchanged):
                right_places[low].append((len(data), 0))
                data.append(value)
    right_places = [right_places[dz] for dz in range(groups)]
    last_lefts = [value for pair in shares for value in pair]

    place = jnp.stack([core, z_low, col, z_high]).astype(jnp.int32)
    vmem = pl.BlockSpec(memory_space=pltpu.VMEM)
    smem = pl.BlockSpec(memory_space=pltpu.SMEM)
    params = pltpu.CompilerParams(vmem_limit_bytes=16 * 1024 * 1024)
    scale = 1.0 / (group_len * groups)
    share = share_rows // channels

    def update_call(last, left_values, extra, out_shape, out_specs, scratch):
        blocks = len(left_values) // 3
        row_count = share * blocks
        outer_size = row_count * channels * channels * half
        places = (blocks, len(data), right_places, share_rows, source_rows, group_len, run)
        return pl.pallas_call(
            functools.partial(update_kernel, places, cols, low, last, scale),
            out_shape=out_shape,
            in_specs=[smem] + [vmem] * (len(left_values) + len(data) + 2 + len(extra)),
            out_specs=out_specs,
            scratch_shapes=[
                pltpu.VMEM((row_count * channels, groups * group_len), bf16),
                pltpu.VMEM((row_count, channels * channels // 2, 2 * half), bf16),
            ]
            + scratch,
            compiler_params=params,
            cost_estimate=pl.CostEstimate(
                flops=2 * outer_size * (groups * group_len + 2 * pair_channels),
                bytes_accessed=2 * outer_size,
                transcendentals=0,
            ),
            name="update_last" if last else "update_first",
        )(place, *left_values, *data, bias, weight, *extra)

    first = update_call(
        False, [lefts[0]] + fars, [far_tile], jax.ShapeDtypeStruct((share, half, pair_channels), bf16), vmem, []
    )
    outs = update_call(
        True,
        last_lefts,
        [first],
        [jax.ShapeDtypeStruct((run, half, pair_channels), bf16)]
        + [jax.ShapeDtypeStruct((2 * run, run, pair_channels), bf16)] * (4 + low),
        [vmem] * (5 + low),
        [pltpu.VMEM((2 * run, half, pair_channels), bf16)],
    )

    def mirrored_place(r, c, q, dz, flip):
        return ((2 * c + (r % 2 ^ flip)) * cols + r // 2) * groups + (q ^ dz)

    def exchange(slot):
        pairs = []
        for r in range(rows):
            for c in range(cols):
                for q in range(groups):
                    source = (r * cols + c) * groups + q
                    if slot >= 4:
                        target = mirrored_place(r, c, q, slot - 4, 1)
                    elif r % 2 == slot % 2:
                        target = mirrored_place(r, c, q, slot // 2, 0)
                    else:
                        target = (r * cols + c) * groups + (q ^ low)
                    pairs.append((source, target))
        return lax.ppermute(outs[1 + slot], axes, pairs)

    operands = [place, pair_rep, outs[0]]
    operands += [exchange(slot) for slot in range(4 + low)]
    operands += [up_weight, down_weight, vectors, swap_cells]
    result = pl.pallas_call(
        functools.partial(finish_kernel, low),
        out_shape=jax.ShapeDtypeStruct(pair_rep.shape, bf16),
        in_specs=[smem] + [vmem] * (len(operands) - 1),
        out_specs=pl.BlockSpec(memory_space=pl.ANY),
        scratch_shapes=[
            pltpu.VMEM((4 * low, run, run, pair_channels), bf16),
            pltpu.SemaphoreType.DMA((4 * low,)),
        ],
        compiler_params=params,
        name="finish",
    )(*operands)
    return result


def solution(mesh):
    in_specs = (
        P("seq", None, "row"),
        P("seq", "row", "col"),
        P(),
        P(),
        P(("row", "seq"), "col", None),
        P(),
        P(),
        P(),
        P(),
        P(),
    )
    out_specs = P(("row", "seq"), "col", None)
    return jax.shard_map(
        on_device, mesh=mesh, in_specs=in_specs, out_specs=out_specs, check_vma=False
    )
```

```python
import functools

import jax
import jax.numpy as jnp
from jax import lax
from jax.experimental import pallas as pl
from jax.experimental.pallas import tpu as pltpu
from jax.sharding import PartitionSpec as P

epsilon = 1e-05
axes = ("row", "col", "seq")


def update_kernel(places, shares, low, last, scale, *refs):
    blocks, data_count, right_places, share_rows, source_rows, group_len, run = places
    groups = len(right_places)
    sources = len(right_places[0])
    refs = list(refs)
    place_ref = refs.pop(0)
    left_refs = [refs.pop(0) for _ in range(3 * blocks)]
    data_refs = [refs.pop(0) for _ in range(data_count)]
    bias_ref, weight_ref = refs.pop(0), refs.pop(0)
    first_ref = refs.pop(0)
    refs = refs[1:] if last else refs
    update_ref = refs.pop() if last else refs[0]
    outer_ref = refs.pop()
    lhs_ref = refs.pop()
    out_refs = refs
    row_count, _, lanes = outer_ref.shape
    low = groups // 2
    channels = share_rows * blocks // row_count
    share = share_rows // channels
    per = source_rows // group_len
    half = lanes // 2
    pair_channels = weight_ref.shape[0] // 2
    lane_low = lax.broadcasted_iota(jnp.int32, (pair_channels, lanes), 1) < half
    for block in range(blocks):
        for dz in range(groups):
            index = 3 * block + max(0, dz - low + 1)
            begin = dz * share_rows if dz < low else 0
            lhs_ref[
                block * share_rows : (block + 1) * share_rows,
                dz * group_len : (dz + 1) * group_len,
            ] = left_refs[index][begin : begin + share_rows]

    def right_tile(item):
        source, rest = divmod(item, per)
        tiles = []
        for dz in range(groups):
            operand, first = right_places[dz][source]
            first += rest * group_len
            tiles.append(data_refs[operand][first : first + group_len])
        return jnp.concatenate(tiles, axis=0)

    for pair in range(sources * per // 2):
        right = jnp.concatenate([right_tile(2 * pair), right_tile(2 * pair + 1)], axis=1)
        outer = jnp.dot(lhs_ref[...], right, preferred_element_type=jnp.float32)
        outer = outer.astype(jnp.bfloat16)
        for part in range(2):
            item = 2 * pair + part
            outer_ref[:, item * channels : (item + 1) * channels, :] = outer[
                :, part * lanes : (part + 1) * lanes
            ].reshape(row_count, channels, lanes)

    unroll = min(4, row_count // 2)

    @pl.loop(0, row_count // (2 * unroll))
    def _(step):
        for two in range(unroll):
            index = step * unroll + two
            both = jnp.concatenate([outer_ref[2 * index], outer_ref[2 * index + 1]], axis=1)
            proj = jnp.dot(weight_ref[...], both, preferred_element_type=jnp.float32)
            a0 = proj[:pair_channels, :lanes]
            a1 = proj[:pair_channels, lanes:]
            b0 = proj[pair_channels:, :lanes]
            b1 = proj[pair_channels:, lanes:]
            cell = jnp.where(lane_low, a0, b1) + pltpu.roll(
                jnp.where(lane_low, a1, b0), half, 1
            )
            cell = (cell * scale + bias_ref[...]).astype(jnp.bfloat16)
            begin = 2 * index
            if last:
                begin = (place_ref[2] ^ (1 + begin // share)) * share + begin % share
            update_ref[pl.ds(begin, 2)] = cell.T.reshape(2, half, pair_channels)

    if last:
        update_ref[pl.ds(place_ref[2] * share, share)] = first_ref[...]
        core, z_low, z_high = place_ref[0], place_ref[1], place_ref[3]
        out_refs[0][...] = update_ref[pl.ds(z_high * run, run)]
        quarter = half // 2

        def mirrored(slot, dz, flip):
            begin = (core ^ flip) * quarter + (z_low ^ dz) * run
            out_refs[1 + slot][...] = update_ref[:, pl.ds(pl.multiple_of(begin, run), run), :]

        def direct(slot, part):
            for index in range(low):
                begin = part * quarter + index * run
                out_refs[1 + slot][index * run : (index + 1) * run] = update_ref[
                    pl.ds((1 - z_high) * run, run), begin : begin + run, :
                ]

        for side in range(2):

            @pl.when(core == side)
            def _():
                for dz in range(2):
                    mirrored(2 * dz + side, dz, 0)
                    direct(2 * dz + 1 - side, dz)

        for dz in range(low):
            mirrored(4 + dz, dz, 1)


def pack_kernel(*refs):
    rows = refs[0].shape[0]
    for index, ref in enumerate(refs[:-1]):
        refs[-1][index * rows : (index + 1) * rows] = ref[...]


def pack(*values):
    rows, lanes = values[0].shape
    return pl.pallas_call(
        pack_kernel,
        out_shape=jax.ShapeDtypeStruct((len(values) * rows, lanes), values[0].dtype),
        in_specs=[pl.BlockSpec(memory_space=pltpu.VMEM)] * len(values),
        out_specs=pl.BlockSpec(memory_space=pltpu.VMEM),
        compiler_params=pltpu.CompilerParams(vmem_limit_bytes=4 * 1024 * 1024),
        name="pack",
    )(*values)


def arrived_kernel(first_ref, second_ref, out_ref):
    rows = out_ref.shape[0] // 2
    out_ref[:rows] = first_ref[:rows]
    out_ref[rows:] = second_ref[:rows]


def arrived(first, second, flops):
    return pl.pallas_call(
        arrived_kernel,
        out_shape=jax.ShapeDtypeStruct((32, first.shape[1]), first.dtype),
        in_specs=[pl.BlockSpec(memory_space=pltpu.VMEM)] * 2,
        out_specs=pl.BlockSpec(memory_space=pltpu.VMEM),
        compiler_params=pltpu.CompilerParams(vmem_limit_bytes=4 * 1024 * 1024),
        cost_estimate=pl.CostEstimate(
            flops=flops, bytes_accessed=4 * first.size, transcendentals=0
        ),
        name="arrived",
    )(first, second)


def finish_kernel(low, *refs):
    place_ref, pair_ref, own_ref = refs[:3]
    slot_refs, mirror_refs = refs[3:7], refs[7 : 7 + low]
    up_ref, down_ref, vector_ref, swap_ref = refs[7 + low : 11 + low]
    out_ref, done_ref, sems = refs[-3:]
    run, columns, pair_channels = pair_ref.shape
    half = columns // 2
    core, z_low, z_high = place_ref[0], place_ref[1], place_ref[3]
    cells = run * run
    gain = vector_ref[:, :pair_channels]
    down_bias = vector_ref[:, pair_channels : 2 * pair_channels]
    up_bias = vector_ref[:, 2 * pair_channels :]

    def chosen(first, second, rows):
        return jnp.where(core == 0, slot_refs[first][rows], slot_refs[second][rows])

    copies = []
    for chunk in range(2 * low):
        other, dz = divmod(chunk, low)
        part = z_high ^ other
        middles = []
        begins = []
        for flip in range(2):
            local = (core ^ flip) * (half // 2) + (z_low ^ dz) * run
            local = pl.multiple_of(local, run)
            begin = (core ^ flip) * half + (part * low + (z_low ^ dz)) * run
            begin = pl.multiple_of(begin, run)
            begins.append(begin)
            rows = pl.ds(part * run, run)
            if flip == 0:
                piece = chosen(2 * dz, 2 * dz + 1, rows)
            else:
                piece = mirror_refs[dz][rows]
            mirrored = jnp.dot(
                swap_ref[...],
                piece.reshape(cells, pair_channels),
                preferred_element_type=jnp.float32,
            )
            if other == 0:
                direct = own_ref[:, pl.ds(local, run), :]
            else:
                rows = pl.ds((z_low ^ dz) * run, run)
                direct = chosen(1, 2, rows) if flip == 0 else chosen(3, 0, rows)
            direct = direct.reshape(cells, pair_channels)
            residual = pair_ref[:, pl.ds(begin, run), :].reshape(cells, pair_channels)
            middles.append(
                (
                    residual.astype(jnp.float32) + 0.5 * (direct.astype(jnp.float32) + mirrored)
                ).astype(jnp.bfloat16)
            )
        middle = jnp.concatenate(middles, axis=0)
        values = middle.astype(jnp.float32)
        center = jnp.mean(values, axis=1, keepdims=True)
        moved = values - center
        spread = jnp.mean(jnp.square(moved), axis=1, keepdims=True)
        normed = moved * lax.rsqrt(spread + epsilon) * gain
        hidden = jnp.dot(
            normed.astype(jnp.bfloat16), up_ref[...], preferred_element_type=jnp.float32
        )
        hidden = jnp.maximum(hidden + up_bias, 0.0).astype(jnp.bfloat16)
        result = jnp.dot(hidden, down_ref[...], preferred_element_type=jnp.float32)
        result = (values + result + down_bias).astype(jnp.bfloat16)
        for flip in range(2):
            index = 2 * chunk + flip
            done_ref[index] = result[flip * cells : (flip + 1) * cells].reshape(
                run, run, pair_channels
            )
            copy = pltpu.make_async_copy(
                done_ref.at[index], out_ref.at[:, pl.ds(begins[flip], run), :], sems.at[index]
            )
            copy.start()
            copies.append(copy)
    for copy in copies:
        copy.wait()


def on_device(
    left_piece,
    right_piece,
    proj_weight,
    proj_bias,
    pair_rep,
    norm_gain,
    up_weight,
    up_bias,
    down_weight,
    down_bias,
):
    rows = lax.axis_size("row")
    cols = lax.axis_size("col")
    groups = lax.axis_size("seq")
    xs = rows // 2
    low = groups // 2
    row, col, seq = (lax.axis_index(name) for name in axes)
    core, z_low, z_high = row % 2, seq % low, seq // low
    run, columns, pair_channels = pair_rep.shape
    group_len, channels, _ = left_piece.shape
    e1 = right_piece.shape[1] // 2
    half = columns // 2
    bf16 = jnp.bfloat16

    def pick(value, index, axis=0):
        return lax.dynamic_index_in_dim(value, index, axis, False)

    def swap(value, name, size, flip):
        return lax.ppermute(value, name, [(i, i ^ flip) for i in range(size)])

    right = right_piece.reshape(group_len, e1, 2, 2, 2, half // 2).transpose(4, 1, 0, 2, 3, 5)
    source_rows = e1 * group_len
    right = right.reshape(2, source_rows, 2 * half)
    share_rows = 2 * run // cols * channels
    left = left_piece.transpose(2, 1, 0).reshape(2, low, run, channels, group_len)
    left = left.transpose(1, 0, 2, 3, 4).reshape(low, cols, share_rows, group_len)
    left = pick(left, col, 1)

    def after(value, *earlier):
        return lax.optimization_barrier((value, earlier))[0] if earlier else value

    mine, theirs = pick(right, z_high), pick(right, 1 - z_high)
    own, crossing = pick(left, z_low), pick(left, 1 - z_low)
    near = swap(crossing, "seq", groups, 1)
    blocks = {0: mine}
    blocks[low + 1] = swap(theirs, "seq", groups, low + 1)
    blocks[1] = swap(mine, "seq", groups, 1)
    blocks[low] = swap(blocks[low + 1], "seq", groups, 1)
    weight = proj_weight.reshape(channels, rows, e1, 2, pair_channels)
    weight = weight.transpose(1, 3, 4, 2, 0)
    weight = jnp.stack([pick(weight, row ^ m) for m in range(rows)], axis=2)
    weight = weight.reshape(2 * pair_channels, channels * channels // 2)
    bias = jnp.broadcast_to(proj_bias[:, None], (pair_channels, 2 * half))
    vectors = jnp.concatenate([norm_gain, down_bias, up_bias]).reshape(1, -1)
    cell = jnp.arange(run * run)
    mirror_cell = cell % run * run + cell // run
    swap_cells = (mirror_cell[:, None] == cell[None, :]).astype(bf16)
    lefts = [pack(own, near)]
    fars = [swap(own, "seq", groups, low), swap(near, "seq", groups, low)]
    shares = [[swap(lefts[0], "col", cols, dy)] for dy in range(1, cols)]
    near_shares = [pair[0] for pair in shares]
    for dy in range(1, cols):
        shares[dy - 1] += [swap(value, "col", cols, dy) for value in fars]
    far_shares = [pair[1] for pair in shares]
    far_tile = arrived(*fars, 10 * (share_rows * groups * group_len) * groups * group_len)
    share_tile = arrived(shares[0][1], shares[0][-1], 4 * (share_rows * groups * group_len) * groups * group_len)
    data = []
    right_places = {dz: [] for dz in range(groups)}
    order = (0, 1, low + 1, low)
    crosses = {dz: [blocks[dz]] for dz in order}
    last = ()
    for dz in order:
        for dx in range(1, xs):
            behind = last + ((near_shares, weight) if dz == low else ())
            crosses[dz].append(swap(after(blocks[dz], *behind), "row", rows, 2 * dx))
            last = (crosses[dz][-1],)
    for position in range(xs):
        values = [crosses[dz][position] for dz in order]
        count = len(order) if position == 0 else len(order) - 1
        packed = pack(*values[:count])
        for value in (packed, swap(packed, "row", rows, 1)):
            for index, dz in enumerate(order[:count]):
                right_places[dz].append((len(data), index * source_rows))
            data.append(value)
        if count < len(order):
            exchanged = swap(after(values[-1], far_tile, far_shares), "row", rows, 1)
            for value in (values[-1], exchanged):
                right_places[low].append((len(data), 0))
                data.append(value)
    right_places = [right_places[dz] for dz in range(groups)]
    last_lefts = [value for pair in shares for value in pair]

    place = jnp.stack([core, z_low, col, z_high]).astype(jnp.int32)
    vmem = pl.BlockSpec(memory_space=pltpu.VMEM)
    smem = pl.BlockSpec(memory_space=pltpu.SMEM)
    params = pltpu.CompilerParams(vmem_limit_bytes=16 * 1024 * 1024)
    scale = 1.0 / (group_len * groups)
    share = share_rows // channels

    def update_call(last, left_values, extra, out_shape, out_specs, scratch):
        blocks = len(left_values) // 3
        row_count = share * blocks
        outer_size = row_count * channels * channels * half
        places = (blocks, len(data), right_places, share_rows, source_rows, group_len, run)
        return pl.pallas_call(
            functools.partial(update_kernel, places, cols, low, last, scale),
            out_shape=out_shape,
            in_specs=[smem] + [vmem] * (len(left_values) + len(data) + 2 + len(extra)),
            out_specs=out_specs,
            scratch_shapes=[
                pltpu.VMEM((row_count * channels, groups * group_len), bf16),
                pltpu.VMEM((row_count, channels * channels // 2, 2 * half), bf16),
            ]
            + scratch,
            compiler_params=params,
            cost_estimate=pl.CostEstimate(
                flops=2 * outer_size * (groups * group_len + 2 * pair_channels),
                bytes_accessed=2 * outer_size,
                transcendentals=0,
            ),
            name="update_last" if last else "update_first",
        )(place, *left_values, *data, bias, weight, *extra)

    first = update_call(
        False, [lefts[0]] + fars, [far_tile], jax.ShapeDtypeStruct((share, half, pair_channels), bf16), vmem, []
    )
    outs = update_call(
        True,
        last_lefts,
        [first, share_tile],
        [jax.ShapeDtypeStruct((run, half, pair_channels), bf16)]
        + [jax.ShapeDtypeStruct((2 * run, run, pair_channels), bf16)] * (4 + low),
        [vmem] * (5 + low),
        [pltpu.VMEM((2 * run, half, pair_channels), bf16)],
    )

    def mirrored_place(r, c, q, dz, flip):
        return ((2 * c + (r % 2 ^ flip)) * cols + r // 2) * groups + (q ^ dz)

    def exchange(slot):
        pairs = []
        for r in range(rows):
            for c in range(cols):
                for q in range(groups):
                    source = (r * cols + c) * groups + q
                    if slot >= 4:
                        target = mirrored_place(r, c, q, slot - 4, 1)
                    elif r % 2 == slot % 2:
                        target = mirrored_place(r, c, q, slot // 2, 0)
                    else:
                        target = (r * cols + c) * groups + (q ^ low)
                    pairs.append((source, target))
        return lax.ppermute(outs[1 + slot], axes, pairs)

    operands = [place, pair_rep, outs[0]]
    operands += [exchange(slot) for slot in range(4 + low)]
    operands += [up_weight, down_weight, vectors, swap_cells]
    result = pl.pallas_call(
        functools.partial(finish_kernel, low),
        out_shape=jax.ShapeDtypeStruct(pair_rep.shape, bf16),
        in_specs=[smem] + [vmem] * (len(operands) - 1),
        out_specs=pl.BlockSpec(memory_space=pl.ANY),
        scratch_shapes=[
            pltpu.VMEM((4 * low, run, run, pair_channels), bf16),
            pltpu.SemaphoreType.DMA((4 * low,)),
        ],
        compiler_params=params,
        name="finish",
    )(*operands)
    return result


def solution(mesh):
    in_specs = (
        P("seq", None, "row"),
        P("seq", "row", "col"),
        P(),
        P(),
        P(("row", "seq"), "col", None),
        P(),
        P(),
        P(),
        P(),
        P(),
    )
    out_specs = P(("row", "seq"), "col", None)
    return jax.shard_map(
        on_device, mesh=mesh, in_specs=in_specs, out_specs=out_specs, check_vma=False
    )
```

```python
import functools

import jax
import jax.numpy as jnp
from jax import lax
from jax.experimental import pallas as pl
from jax.experimental.pallas import tpu as pltpu
from jax.sharding import PartitionSpec as P

epsilon = 1e-05
axes = ("row", "col", "seq")


def update_kernel(places, shares, low, last, scale, *refs):
    blocks, data_count, right_places, share_rows, source_rows, group_len, run = places
    groups = len(right_places)
    sources = len(right_places[0])
    refs = list(refs)
    place_ref = refs.pop(0)
    left_refs = [refs.pop(0) for _ in range(3 * blocks)]
    data_refs = [refs.pop(0) for _ in range(data_count)]
    bias_ref, weight_ref = refs.pop(0), refs.pop(0)
    first_ref = refs.pop(0)
    refs = refs[1:] if last else refs
    update_ref = refs.pop() if last else refs[0]
    outer_ref = refs.pop()
    lhs_ref = refs.pop()
    out_refs = refs
    row_count, _, lanes = outer_ref.shape
    low = groups // 2
    channels = share_rows * blocks // row_count
    share = share_rows // channels
    per = source_rows // group_len
    half = lanes // 2
    pair_channels = weight_ref.shape[0] // 2
    lane_low = lax.broadcasted_iota(jnp.int32, (pair_channels, lanes), 1) < half
    for block in range(blocks):
        for dz in range(groups):
            index = 3 * block + max(0, dz - low + 1)
            begin = dz * share_rows if dz < low else 0
            lhs_ref[
                block * share_rows : (block + 1) * share_rows,
                dz * group_len : (dz + 1) * group_len,
            ] = left_refs[index][begin : begin + share_rows]

    def right_tile(item):
        source, rest = divmod(item, per)
        tiles = []
        for dz in range(groups):
            operand, first = right_places[dz][source]
            first += rest * group_len
            tiles.append(data_refs[operand][first : first + group_len])
        return jnp.concatenate(tiles, axis=0)

    for pair in range(sources * per // 2):
        right = jnp.concatenate([right_tile(2 * pair), right_tile(2 * pair + 1)], axis=1)
        outer = jnp.dot(lhs_ref[...], right, preferred_element_type=jnp.float32)
        outer = outer.astype(jnp.bfloat16)
        for part in range(2):
            item = 2 * pair + part
            outer_ref[:, item * channels : (item + 1) * channels, :] = outer[
                :, part * lanes : (part + 1) * lanes
            ].reshape(row_count, channels, lanes)

    unroll = min(4, row_count // 2)

    @pl.loop(0, row_count // (2 * unroll))
    def _(step):
        for two in range(unroll):
            index = step * unroll + two
            both = jnp.concatenate([outer_ref[2 * index], outer_ref[2 * index + 1]], axis=1)
            proj = jnp.dot(weight_ref[...], both, preferred_element_type=jnp.float32)
            a0 = proj[:pair_channels, :lanes]
            a1 = proj[:pair_channels, lanes:]
            b0 = proj[pair_channels:, :lanes]
            b1 = proj[pair_channels:, lanes:]
            cell = jnp.where(lane_low, a0, b1) + pltpu.roll(
                jnp.where(lane_low, a1, b0), half, 1
            )
            cell = (cell * scale + bias_ref[...]).astype(jnp.bfloat16)
            begin = 2 * index
            if last:
                begin = (place_ref[2] ^ (1 + begin // share)) * share + begin % share
            update_ref[pl.ds(begin, 2)] = cell.T.reshape(2, half, pair_channels)

    if last:
        update_ref[pl.ds(place_ref[2] * share, share)] = first_ref[...]
        core, z_low, z_high = place_ref[0], place_ref[1], place_ref[3]
        out_refs[0][...] = update_ref[pl.ds(z_high * run, run)]
        quarter = half // 2

        def mirrored(slot, dz, flip):
            begin = (core ^ flip) * quarter + (z_low ^ dz) * run
            out_refs[1 + slot][...] = update_ref[:, pl.ds(pl.multiple_of(begin, run), run), :]

        def direct(slot, part):
            for index in range(low):
                begin = part * quarter + index * run
                out_refs[1 + slot][index * run : (index + 1) * run] = update_ref[
                    pl.ds((1 - z_high) * run, run), begin : begin + run, :
                ]

        for side in range(2):

            @pl.when(core == side)
            def _():
                for dz in range(2):
                    mirrored(2 * dz + side, dz, 0)
                    direct(2 * dz + 1 - side, dz)

        for dz in range(low):
            mirrored(4 + dz, dz, 1)


def pack_kernel(*refs):
    rows = refs[0].shape[0]
    for index, ref in enumerate(refs[:-1]):
        refs[-1][index * rows : (index + 1) * rows] = ref[...]


def pack(*values):
    rows, lanes = values[0].shape
    return pl.pallas_call(
        pack_kernel,
        out_shape=jax.ShapeDtypeStruct((len(values) * rows, lanes), values[0].dtype),
        in_specs=[pl.BlockSpec(memory_space=pltpu.VMEM)] * len(values),
        out_specs=pl.BlockSpec(memory_space=pltpu.VMEM),
        compiler_params=pltpu.CompilerParams(vmem_limit_bytes=4 * 1024 * 1024),
        name="pack",
    )(*values)


def arrived_kernel(first_ref, second_ref, out_ref):
    rows = out_ref.shape[0] // 2
    out_ref[:rows] = first_ref[:rows]
    out_ref[rows:] = second_ref[:rows]


def arrived(first, second, flops):
    return pl.pallas_call(
        arrived_kernel,
        out_shape=jax.ShapeDtypeStruct((32, first.shape[1]), first.dtype),
        in_specs=[pl.BlockSpec(memory_space=pltpu.VMEM)] * 2,
        out_specs=pl.BlockSpec(memory_space=pltpu.VMEM),
        compiler_params=pltpu.CompilerParams(vmem_limit_bytes=4 * 1024 * 1024),
        cost_estimate=pl.CostEstimate(
            flops=flops, bytes_accessed=4 * first.size, transcendentals=0
        ),
        name="arrived",
    )(first, second)


def finish_kernel(low, *refs):
    place_ref, pair_ref, own_ref = refs[:3]
    slot_refs, mirror_refs = refs[3:7], refs[7 : 7 + low]
    up_ref, down_ref, vector_ref, swap_ref = refs[7 + low : 11 + low]
    out_ref, done_ref, sems = refs[-3:]
    run, columns, pair_channels = pair_ref.shape
    half = columns // 2
    core, z_low, z_high = place_ref[0], place_ref[1], place_ref[3]
    cells = run * run
    gain = vector_ref[:, :pair_channels]
    down_bias = vector_ref[:, pair_channels : 2 * pair_channels]
    up_bias = vector_ref[:, 2 * pair_channels :]
    ones = jnp.full((2 * pair_channels, pair_channels), 1.0 / pair_channels, jnp.bfloat16)

    def chosen(first, second, rows):
        return jnp.where(core == 0, slot_refs[first][rows], slot_refs[second][rows])

    copies = []
    for chunk in range(2 * low):
        other, dz = divmod(chunk, low)
        part = z_high ^ other
        middles = []
        begins = []
        for flip in range(2):
            local = (core ^ flip) * (half // 2) + (z_low ^ dz) * run
            local = pl.multiple_of(local, run)
            begin = (core ^ flip) * half + (part * low + (z_low ^ dz)) * run
            begin = pl.multiple_of(begin, run)
            begins.append(begin)
            rows = pl.ds(part * run, run)
            if flip == 0:
                piece = chosen(2 * dz, 2 * dz + 1, rows)
            else:
                piece = mirror_refs[dz][rows]
            mirrored = jnp.dot(
                swap_ref[...],
                piece.reshape(cells, pair_channels),
                preferred_element_type=jnp.float32,
            )
            if other == 0:
                direct = own_ref[:, pl.ds(local, run), :]
            else:
                rows = pl.ds((z_low ^ dz) * run, run)
                direct = chosen(1, 2, rows) if flip == 0 else chosen(3, 0, rows)
            direct = direct.reshape(cells, pair_channels)
            residual = pair_ref[:, pl.ds(begin, run), :].reshape(cells, pair_channels)
            middles.append(
                (
                    residual.astype(jnp.float32) + 0.5 * (direct.astype(jnp.float32) + mirrored)
                ).astype(jnp.bfloat16)
            )
        middle = jnp.concatenate(middles, axis=0)
        values = middle.astype(jnp.float32)
        center = jnp.dot(middle, ones[:pair_channels], preferred_element_type=jnp.float32)
        moved = values - center
        square = jnp.square(moved)
        high = square.astype(jnp.bfloat16)
        rest = (square - high.astype(jnp.float32)).astype(jnp.bfloat16)
        spread = jnp.dot(
            jnp.concatenate([high, rest], axis=1), ones, preferred_element_type=jnp.float32
        )
        normed = moved * lax.rsqrt(spread + epsilon) * gain
        hidden = jnp.dot(
            normed.astype(jnp.bfloat16), up_ref[...], preferred_element_type=jnp.float32
        )
        hidden = jnp.maximum(hidden + up_bias, 0.0).astype(jnp.bfloat16)
        result = jnp.dot(hidden, down_ref[...], preferred_element_type=jnp.float32)
        result = (values + result + down_bias).astype(jnp.bfloat16)
        for flip in range(2):
            index = 2 * chunk + flip
            done_ref[index] = result[flip * cells : (flip + 1) * cells].reshape(
                run, run, pair_channels
            )
            copy = pltpu.make_async_copy(
                done_ref.at[index], out_ref.at[:, pl.ds(begins[flip], run), :], sems.at[index]
            )
            copy.start()
            copies.append(copy)
    for copy in copies:
        copy.wait()


def on_device(
    left_piece,
    right_piece,
    proj_weight,
    proj_bias,
    pair_rep,
    norm_gain,
    up_weight,
    up_bias,
    down_weight,
    down_bias,
):
    rows = lax.axis_size("row")
    cols = lax.axis_size("col")
    groups = lax.axis_size("seq")
    xs = rows // 2
    low = groups // 2
    row, col, seq = (lax.axis_index(name) for name in axes)
    core, z_low, z_high = row % 2, seq % low, seq // low
    run, columns, pair_channels = pair_rep.shape
    group_len, channels, _ = left_piece.shape
    e1 = right_piece.shape[1] // 2
    half = columns // 2
    bf16 = jnp.bfloat16

    def pick(value, index, axis=0):
        return lax.dynamic_index_in_dim(value, index, axis, False)

    def swap(value, name, size, flip):
        return lax.ppermute(value, name, [(i, i ^ flip) for i in range(size)])

    right = right_piece.reshape(group_len, e1, 2, 2, 2, half // 2).transpose(4, 1, 0, 2, 3, 5)
    source_rows = e1 * group_len
    right = right.reshape(2, source_rows, 2 * half)
    share_rows = 2 * run // cols * channels
    left = left_piece.transpose(2, 1, 0).reshape(2, low, run, channels, group_len)
    left = left.transpose(1, 0, 2, 3, 4).reshape(low, cols, share_rows, group_len)
    left = pick(left, col, 1)

    def after(value, *earlier):
        return lax.optimization_barrier((value, earlier))[0] if earlier else value

    mine, theirs = pick(right, z_high), pick(right, 1 - z_high)
    own, crossing = pick(left, z_low), pick(left, 1 - z_low)
    near = swap(crossing, "seq", groups, 1)
    blocks = {0: mine}
    blocks[low + 1] = swap(theirs, "seq", groups, low + 1)
    blocks[1] = swap(mine, "seq", groups, 1)
    blocks[low] = swap(blocks[low + 1], "seq", groups, 1)
    weight = proj_weight.reshape(channels, rows, e1, 2, pair_channels)
    weight = weight.transpose(1, 3, 4, 2, 0)
    weight = jnp.stack([pick(weight, row ^ m) for m in range(rows)], axis=2)
    weight = weight.reshape(2 * pair_channels, channels * channels // 2)
    bias = jnp.broadcast_to(proj_bias[:, None], (pair_channels, 2 * half))
    vectors = jnp.concatenate([norm_gain, down_bias, up_bias]).reshape(1, -1)
    cell = jnp.arange(run * run)
    mirror_cell = cell % run * run + cell // run
    swap_cells = (mirror_cell[:, None] == cell[None, :]).astype(bf16)
    lefts = [pack(own, near)]
    fars = [swap(own, "seq", groups, low), swap(near, "seq", groups, low)]
    shares = [[swap(lefts[0], "col", cols, dy)] for dy in range(1, cols)]
    near_shares = [pair[0] for pair in shares]
    for dy in range(1, cols):
        shares[dy - 1] += [swap(value, "col", cols, dy) for value in fars]
    far_shares = [pair[1] for pair in shares]
    far_tile = arrived(*fars, 10 * (share_rows * groups * group_len) * groups * group_len)
    share_tile = arrived(shares[0][1], shares[0][-1], 4 * (share_rows * groups * group_len) * groups * group_len)
    data = []
    right_places = {dz: [] for dz in range(groups)}
    order = (0, 1, low + 1, low)
    crosses = {dz: [blocks[dz]] for dz in order}
    last = ()
    for dz in order:
        for dx in range(1, xs):
            behind = last + ((near_shares,) if dz == low else ())
            crosses[dz].append(swap(after(blocks[dz], *behind), "row", rows, 2 * dx))
            last = (crosses[dz][-1],)
    for position in range(xs):
        values = [crosses[dz][position] for dz in order]
        count = len(order) if position == 0 else len(order) - 1
        packed = pack(*values[:count])
        for value in (packed, swap(packed, "row", rows, 1)):
            for index, dz in enumerate(order[:count]):
                right_places[dz].append((len(data), index * source_rows))
            data.append(value)
        if count < len(order):
            exchanged = swap(after(values[-1], far_tile, far_shares), "row", rows, 1)
            for value in (values[-1], exchanged):
                right_places[low].append((len(data), 0))
                data.append(value)
    right_places = [right_places[dz] for dz in range(groups)]
    last_lefts = [value for pair in shares for value in pair]

    place = jnp.stack([core, z_low, col, z_high]).astype(jnp.int32)
    vmem = pl.BlockSpec(memory_space=pltpu.VMEM)
    smem = pl.BlockSpec(memory_space=pltpu.SMEM)
    params = pltpu.CompilerParams(vmem_limit_bytes=16 * 1024 * 1024)
    scale = 1.0 / (group_len * groups)
    share = share_rows // channels

    def update_call(last, left_values, extra, out_shape, out_specs, scratch):
        blocks = len(left_values) // 3
        row_count = share * blocks
        outer_size = row_count * channels * channels * half
        places = (blocks, len(data), right_places, share_rows, source_rows, group_len, run)
        return pl.pallas_call(
            functools.partial(update_kernel, places, cols, low, last, scale),
            out_shape=out_shape,
            in_specs=[smem] + [vmem] * (len(left_values) + len(data) + 2 + len(extra)),
            out_specs=out_specs,
            scratch_shapes=[
                pltpu.VMEM((row_count * channels, groups * group_len), bf16),
                pltpu.VMEM((row_count, channels * channels // 2, 2 * half), bf16),
            ]
            + scratch,
            compiler_params=params,
            cost_estimate=pl.CostEstimate(
                flops=2 * outer_size * (groups * group_len + 2 * pair_channels),
                bytes_accessed=2 * outer_size,
                transcendentals=0,
            ),
            name="update_last" if last else "update_first",
        )(place, *left_values, *data, bias, weight, *extra)

    first = update_call(
        False, [lefts[0]] + fars, [far_tile], jax.ShapeDtypeStruct((share, half, pair_channels), bf16), vmem, []
    )
    outs = update_call(
        True,
        last_lefts,
        [first, share_tile],
        [jax.ShapeDtypeStruct((run, half, pair_channels), bf16)]
        + [jax.ShapeDtypeStruct((2 * run, run, pair_channels), bf16)] * (4 + low),
        [vmem] * (5 + low),
        [pltpu.VMEM((2 * run, half, pair_channels), bf16)],
    )

    def mirrored_place(r, c, q, dz, flip):
        return ((2 * c + (r % 2 ^ flip)) * cols + r // 2) * groups + (q ^ dz)

    def exchange(slot):
        pairs = []
        for r in range(rows):
            for c in range(cols):
                for q in range(groups):
                    source = (r * cols + c) * groups + q
                    if slot >= 4:
                        target = mirrored_place(r, c, q, slot - 4, 1)
                    elif r % 2 == slot % 2:
                        target = mirrored_place(r, c, q, slot // 2, 0)
                    else:
                        target = (r * cols + c) * groups + (q ^ low)
                    pairs.append((source, target))
        return lax.ppermute(outs[1 + slot], axes, pairs)

    operands = [place, pair_rep, outs[0]]
    operands += [exchange(slot) for slot in range(4 + low)]
    operands += [up_weight, down_weight, vectors, swap_cells]
    result = pl.pallas_call(
        functools.partial(finish_kernel, low),
        out_shape=jax.ShapeDtypeStruct(pair_rep.shape, bf16),
        in_specs=[smem] + [vmem] * (len(operands) - 1),
        out_specs=pl.BlockSpec(memory_space=pl.ANY),
        scratch_shapes=[
            pltpu.VMEM((4 * low, run, run, pair_channels), bf16),
            pltpu.SemaphoreType.DMA((4 * low,)),
        ],
        compiler_params=params,
        name="finish",
    )(*operands)
    return result


def solution(mesh):
    in_specs = (
        P("seq", None, "row"),
        P("seq", "row", "col"),
        P(),
        P(),
        P(("row", "seq"), "col", None),
        P(),
        P(),
        P(),
        P(),
        P(),
    )
    out_specs = P(("row", "seq"), "col", None)
    return jax.shard_map(
        on_device, mesh=mesh, in_specs=in_specs, out_specs=out_specs, check_vma=False
    )
```

```python
import functools

import jax
import jax.numpy as jnp
from jax import lax
from jax.experimental import pallas as pl
from jax.experimental.pallas import tpu as pltpu
from jax.sharding import PartitionSpec as P

epsilon = 1e-05
axes = ("row", "col", "seq")


def update_kernel(places, shares, low, last, scale, *refs):
    blocks, data_count, right_places, share_rows, source_rows, group_len, run = places
    groups = len(right_places)
    sources = len(right_places[0])
    refs = list(refs)
    place_ref = refs.pop(0)
    left_refs = [refs.pop(0) for _ in range(3 * blocks)]
    data_refs = [refs.pop(0) for _ in range(data_count)]
    bias_ref, weight_ref = refs.pop(0), refs.pop(0)
    first_ref = refs.pop(0)
    update_ref = refs.pop() if last else refs[0]
    outer_ref = refs.pop()
    lhs_ref = refs.pop()
    out_refs = refs
    row_count, _, lanes = outer_ref.shape
    low = groups // 2
    channels = share_rows * blocks // row_count
    share = share_rows // channels
    per = source_rows // group_len
    half = lanes // 2
    pair_channels = weight_ref.shape[0] // 2
    lane_low = lax.broadcasted_iota(jnp.int32, (pair_channels, lanes), 1) < half
    for block in range(blocks):
        for dz in range(groups):
            index = 3 * block + max(0, dz - low + 1)
            begin = dz * share_rows if dz < low else 0
            lhs_ref[
                block * share_rows : (block + 1) * share_rows,
                dz * group_len : (dz + 1) * group_len,
            ] = left_refs[index][begin : begin + share_rows]

    def right_tile(item):
        source, rest = divmod(item, per)
        tiles = []
        for dz in range(groups):
            operand, first = right_places[dz][source]
            first += rest * group_len
            tiles.append(data_refs[operand][first : first + group_len])
        return jnp.concatenate(tiles, axis=0)

    for pair in range(sources * per // 2):
        right = jnp.concatenate([right_tile(2 * pair), right_tile(2 * pair + 1)], axis=1)
        outer = jnp.dot(lhs_ref[...], right, preferred_element_type=jnp.float32)
        outer = outer.astype(jnp.bfloat16)
        for part in range(2):
            item = 2 * pair + part
            outer_ref[:, item * channels : (item + 1) * channels, :] = outer[
                :, part * lanes : (part + 1) * lanes
            ].reshape(row_count, channels, lanes)

    unroll = min(4, row_count // 2)

    @pl.loop(0, row_count // (2 * unroll))
    def _(step):
        for two in range(unroll):
            index = step * unroll + two
            both = jnp.concatenate([outer_ref[2 * index], outer_ref[2 * index + 1]], axis=1)
            proj = jnp.dot(weight_ref[...], both, preferred_element_type=jnp.float32)
            a0 = proj[:pair_channels, :lanes]
            a1 = proj[:pair_channels, lanes:]
            b0 = proj[pair_channels:, :lanes]
            b1 = proj[pair_channels:, lanes:]
            cell = jnp.where(lane_low, a0, b1) + pltpu.roll(
                jnp.where(lane_low, a1, b0), half, 1
            )
            cell = (cell * scale + bias_ref[...]).astype(jnp.bfloat16)
            begin = 2 * index
            if last:
                begin = (place_ref[2] ^ (1 + begin // share)) * share + begin % share
            update_ref[pl.ds(begin, 2)] = cell.T.reshape(2, half, pair_channels)

    if last:
        update_ref[pl.ds(place_ref[2] * share, share)] = first_ref[...]
        core, z_low, z_high = place_ref[0], place_ref[1], place_ref[3]
        out_refs[0][...] = update_ref[pl.ds(z_high * run, run)]
        quarter = half // 2

        def mirrored(slot, dz, flip):
            begin = (core ^ flip) * quarter + (z_low ^ dz) * run
            out_refs[1 + slot][...] = update_ref[:, pl.ds(pl.multiple_of(begin, run), run), :]

        def direct(slot, part):
            for index in range(low):
                begin = part * quarter + index * run
                out_refs[1 + slot][index * run : (index + 1) * run] = update_ref[
                    pl.ds((1 - z_high) * run, run), begin : begin + run, :
                ]

        for side in range(2):

            @pl.when(core == side)
            def _():
                for dz in range(2):
                    mirrored(2 * dz + side, dz, 0)
                    direct(2 * dz + 1 - side, dz)

        for dz in range(low):
            mirrored(4 + dz, dz, 1)


def pack_kernel(*refs):
    rows = refs[0].shape[0]
    for index, ref in enumerate(refs[:-1]):
        refs[-1][index * rows : (index + 1) * rows] = ref[...]


def pack(*values):
    rows, lanes = values[0].shape
    return pl.pallas_call(
        pack_kernel,
        out_shape=jax.ShapeDtypeStruct((len(values) * rows, lanes), values[0].dtype),
        in_specs=[pl.BlockSpec(memory_space=pltpu.VMEM)] * len(values),
        out_specs=pl.BlockSpec(memory_space=pltpu.VMEM),
        compiler_params=pltpu.CompilerParams(vmem_limit_bytes=4 * 1024 * 1024),
        name="pack",
    )(*values)


def arrived_kernel(first_ref, second_ref, out_ref):
    rows = out_ref.shape[0] // 2
    out_ref[:rows] = first_ref[:rows]
    out_ref[rows:] = second_ref[:rows]


def arrived(first, second, flops):
    return pl.pallas_call(
        arrived_kernel,
        out_shape=jax.ShapeDtypeStruct((32, first.shape[1]), first.dtype),
        in_specs=[pl.BlockSpec(memory_space=pltpu.VMEM)] * 2,
        out_specs=pl.BlockSpec(memory_space=pltpu.VMEM),
        compiler_params=pltpu.CompilerParams(vmem_limit_bytes=4 * 1024 * 1024),
        cost_estimate=pl.CostEstimate(
            flops=flops, bytes_accessed=4 * first.size, transcendentals=0
        ),
        name="arrived",
    )(first, second)


def finish_kernel(low, *refs):
    place_ref, pair_ref, own_ref = refs[:3]
    slot_refs, mirror_refs = refs[3:7], refs[7 : 7 + low]
    up_ref, down_ref, vector_ref, swap_ref = refs[7 + low : 11 + low]
    out_ref, done_ref, sems = refs[-3:]
    run, columns, pair_channels = pair_ref.shape
    half = columns // 2
    core, z_low, z_high = place_ref[0], place_ref[1], place_ref[3]
    cells = run * run
    gain = vector_ref[:, :pair_channels]
    down_bias = vector_ref[:, pair_channels : 2 * pair_channels]
    up_bias = vector_ref[:, 2 * pair_channels :]
    ones = jnp.full((2 * pair_channels, pair_channels), 1.0 / pair_channels, jnp.bfloat16)

    def chosen(first, second, rows):
        return jnp.where(core == 0, slot_refs[first][rows], slot_refs[second][rows])

    copies = []
    for chunk in range(2 * low):
        other, dz = divmod(chunk, low)
        part = z_high ^ other
        middles = []
        begins = []
        for flip in range(2):
            local = (core ^ flip) * (half // 2) + (z_low ^ dz) * run
            local = pl.multiple_of(local, run)
            begin = (core ^ flip) * half + (part * low + (z_low ^ dz)) * run
            begin = pl.multiple_of(begin, run)
            begins.append(begin)
            rows = pl.ds(part * run, run)
            if flip == 0:
                piece = chosen(2 * dz, 2 * dz + 1, rows)
            else:
                piece = mirror_refs[dz][rows]
            mirrored = jnp.dot(
                swap_ref[...],
                piece.reshape(cells, pair_channels),
                preferred_element_type=jnp.float32,
            )
            if other == 0:
                direct = own_ref[:, pl.ds(local, run), :]
            else:
                rows = pl.ds((z_low ^ dz) * run, run)
                direct = chosen(1, 2, rows) if flip == 0 else chosen(3, 0, rows)
            direct = direct.reshape(cells, pair_channels)
            residual = pair_ref[:, pl.ds(begin, run), :].reshape(cells, pair_channels)
            middles.append(
                (
                    residual.astype(jnp.float32) + 0.5 * (direct.astype(jnp.float32) + mirrored)
                ).astype(jnp.bfloat16)
            )
        middle = jnp.concatenate(middles, axis=0)
        values = middle.astype(jnp.float32)
        center = jnp.dot(middle, ones[:pair_channels], preferred_element_type=jnp.float32)
        moved = values - center
        square = jnp.square(moved)
        high = square.astype(jnp.bfloat16)
        rest = (square - high.astype(jnp.float32)).astype(jnp.bfloat16)
        spread = jnp.dot(
            jnp.concatenate([high, rest], axis=1), ones, preferred_element_type=jnp.float32
        )
        normed = moved * lax.rsqrt(spread + epsilon) * gain
        hidden = jnp.dot(
            normed.astype(jnp.bfloat16), up_ref[...], preferred_element_type=jnp.float32
        )
        hidden = jnp.maximum(hidden + up_bias, 0.0).astype(jnp.bfloat16)
        result = jnp.dot(hidden, down_ref[...], preferred_element_type=jnp.float32)
        result = (values + result + down_bias).astype(jnp.bfloat16)
        for flip in range(2):
            index = 2 * chunk + flip
            done_ref[index] = result[flip * cells : (flip + 1) * cells].reshape(
                run, run, pair_channels
            )
            copy = pltpu.make_async_copy(
                done_ref.at[index], out_ref.at[:, pl.ds(begins[flip], run), :], sems.at[index]
            )
            copy.start()
            copies.append(copy)
    for copy in copies:
        copy.wait()


def on_device(
    left_piece,
    right_piece,
    proj_weight,
    proj_bias,
    pair_rep,
    norm_gain,
    up_weight,
    up_bias,
    down_weight,
    down_bias,
):
    rows = lax.axis_size("row")
    cols = lax.axis_size("col")
    groups = lax.axis_size("seq")
    xs = rows // 2
    low = groups // 2
    row, col, seq = (lax.axis_index(name) for name in axes)
    core, z_low, z_high = row % 2, seq % low, seq // low
    run, columns, pair_channels = pair_rep.shape
    group_len, channels, _ = left_piece.shape
    e1 = right_piece.shape[1] // 2
    half = columns // 2
    bf16 = jnp.bfloat16

    def pick(value, index, axis=0):
        return lax.dynamic_index_in_dim(value, index, axis, False)

    def swap(value, name, size, flip):
        return lax.ppermute(value, name, [(i, i ^ flip) for i in range(size)])

    right = right_piece.reshape(group_len, e1, 2, 2, 2, half // 2).transpose(4, 1, 0, 2, 3, 5)
    source_rows = e1 * group_len
    right = right.reshape(2, source_rows, 2 * half)
    share_rows = 2 * run // cols * channels
    left = left_piece.transpose(2, 1, 0).reshape(2, low, run, channels, group_len)
    left = left.transpose(1, 0, 2, 3, 4).reshape(low, cols, share_rows, group_len)
    left = pick(left, col, 1)

    def after(value, *earlier):
        return lax.optimization_barrier((value, earlier))[0] if earlier else value

    mine, theirs = pick(right, z_high), pick(right, 1 - z_high)
    own, crossing = pick(left, z_low), pick(left, 1 - z_low)
    near = swap(crossing, "seq", groups, 1)
    blocks = {0: mine}
    blocks[low + 1] = swap(theirs, "seq", groups, low + 1)
    blocks[1] = swap(mine, "seq", groups, 1)
    blocks[low] = swap(blocks[low + 1], "seq", groups, 1)
    weight = proj_weight.reshape(channels, rows, e1, 2, pair_channels)
    weight = weight.transpose(1, 3, 4, 2, 0)
    weight = jnp.stack([pick(weight, row ^ m) for m in range(rows)], axis=2)
    weight = weight.reshape(2 * pair_channels, channels * channels // 2)
    bias = jnp.broadcast_to(proj_bias[:, None], (pair_channels, 2 * half))
    vectors = jnp.concatenate([norm_gain, down_bias, up_bias]).reshape(1, -1)
    cell = jnp.arange(run * run)
    mirror_cell = cell % run * run + cell // run
    swap_cells = (mirror_cell[:, None] == cell[None, :]).astype(bf16)
    lefts = [pack(own, near)]
    fars = [swap(own, "seq", groups, low), swap(near, "seq", groups, low)]
    shares = [[swap(lefts[0], "col", cols, dy)] for dy in range(1, cols)]
    near_shares = [pair[0] for pair in shares]
    for dy in range(1, cols):
        shares[dy - 1] += [swap(value, "col", cols, dy) for value in fars]
    far_shares = [pair[1] for pair in shares]
    far_tile = arrived(*fars, 32 * (share_rows * groups * group_len) * groups * group_len // 4)
    data = []
    right_places = {dz: [] for dz in range(groups)}
    order = (0, 1, low + 1, low)
    crosses = {dz: [blocks[dz]] for dz in order}
    last = ()
    for dz in order:
        for dx in range(1, xs):
            behind = last + ((near_shares, bias) if dz == low else ())
            crosses[dz].append(swap(after(blocks[dz], *behind), "row", rows, 2 * dx))
            last = (crosses[dz][-1],)
    for position in range(xs):
        values = [crosses[dz][position] for dz in order]
        count = len(order) if position == 0 else len(order) - 1
        packed = pack(*values[:count])
        for value in (packed, swap(packed, "row", rows, 1)):
            for index, dz in enumerate(order[:count]):
                right_places[dz].append((len(data), index * source_rows))
            data.append(value)
        if count < len(order):
            exchanged = swap(after(values[-1], far_tile, far_shares), "row", rows, 1)
            for value in (values[-1], exchanged):
                right_places[low].append((len(data), 0))
                data.append(value)
    right_places = [right_places[dz] for dz in range(groups)]
    last_lefts = [value for pair in shares for value in pair]

    place = jnp.stack([core, z_low, col, z_high]).astype(jnp.int32)
    vmem = pl.BlockSpec(memory_space=pltpu.VMEM)
    smem = pl.BlockSpec(memory_space=pltpu.SMEM)
    params = pltpu.CompilerParams(vmem_limit_bytes=16 * 1024 * 1024)
    scale = 1.0 / (group_len * groups)
    share = share_rows // channels

    def update_call(last, left_values, extra, out_shape, out_specs, scratch):
        blocks = len(left_values) // 3
        row_count = share * blocks
        outer_size = row_count * channels * channels * half
        places = (blocks, len(data), right_places, share_rows, source_rows, group_len, run)
        return pl.pallas_call(
            functools.partial(update_kernel, places, cols, low, last, scale),
            out_shape=out_shape,
            in_specs=[smem] + [vmem] * (len(left_values) + len(data) + 2 + len(extra)),
            out_specs=out_specs,
            scratch_shapes=[
                pltpu.VMEM((row_count * channels, groups * group_len), bf16),
                pltpu.VMEM((row_count, channels * channels // 2, 2 * half), bf16),
            ]
            + scratch,
            compiler_params=params,
            cost_estimate=pl.CostEstimate(
                flops=2 * outer_size * (groups * group_len + 2 * pair_channels),
                bytes_accessed=2 * outer_size,
                transcendentals=0,
            ),
            name="update_last" if last else "update_first",
        )(place, *left_values, *data, bias, weight, *extra)

    first = update_call(
        False, [lefts[0]] + fars, [far_tile], jax.ShapeDtypeStruct((share, half, pair_channels), bf16), vmem, []
    )
    outs = update_call(
        True,
        last_lefts,
        [first],
        [jax.ShapeDtypeStruct((run, half, pair_channels), bf16)]
        + [jax.ShapeDtypeStruct((2 * run, run, pair_channels), bf16)] * (4 + low),
        [vmem] * (5 + low),
        [pltpu.VMEM((2 * run, half, pair_channels), bf16)],
    )

    def mirrored_place(r, c, q, dz, flip):
        return ((2 * c + (r % 2 ^ flip)) * cols + r // 2) * groups + (q ^ dz)

    def exchange(slot):
        pairs = []
        for r in range(rows):
            for c in range(cols):
                for q in range(groups):
                    source = (r * cols + c) * groups + q
                    if slot >= 4:
                        target = mirrored_place(r, c, q, slot - 4, 1)
                    elif r % 2 == slot % 2:
                        target = mirrored_place(r, c, q, slot // 2, 0)
                    else:
                        target = (r * cols + c) * groups + (q ^ low)
                    pairs.append((source, target))
        return lax.ppermute(outs[1 + slot], axes, pairs)

    operands = [place, pair_rep, outs[0]]
    operands += [exchange(slot) for slot in range(4 + low)]
    operands += [up_weight, down_weight, vectors, swap_cells]
    result = pl.pallas_call(
        functools.partial(finish_kernel, low),
        out_shape=jax.ShapeDtypeStruct(pair_rep.shape, bf16),
        in_specs=[smem] + [vmem] * (len(operands) - 1),
        out_specs=pl.BlockSpec(memory_space=pl.ANY),
        scratch_shapes=[
            pltpu.VMEM((4 * low, run, run, pair_channels), bf16),
            pltpu.SemaphoreType.DMA((4 * low,)),
        ],
        compiler_params=params,
        name="finish",
    )(*operands)
    return result


def solution(mesh):
    in_specs = (
        P("seq", None, "row"),
        P("seq", "row", "col"),
        P(),
        P(),
        P(("row", "seq"), "col", None),
        P(),
        P(),
        P(),
        P(),
        P(),
    )
    out_specs = P(("row", "seq"), "col", None)
    return jax.shard_map(
        on_device, mesh=mesh, in_specs=in_specs, out_specs=out_specs, check_vma=False
    )
```
